512 devices in a mesh: gx: 16 (over z, x_lo), gy: 8 (over y), gz: 4 (over x_hi, core).
Axes of the slice: x: 4 (x_hi: 2, x_lo: 2; x = x_hi * 2 + x_lo), y: 8, z: 8, core: 2. Of those that a mesh axis runs over, the one named last changes fastest.
Arguments:
- blocks: float32 [3, 3, 3, 3, 3, 16, 64, 2048], P(None, None, None, None, None, 'gz', 'gy', 'gx'), may hold values from -0.02 to 3, as said below
- classes: int32 [16, 64, 2048], P('gz', 'gy', 'gx'), may hold values from 0 to 3
- residual: float32 [3, 16, 64, 2048], P(None, 'gz', 'gy', 'gx'), may hold values from -6 to 6
Outputs:
- coarse_operator: float32 [3, 3, 3, 3, 3, 8, 32, 1024], P(None, None, None, None, None, 'gz', 'gy', 'gx')
- coarse_solution: float32 [3, 8, 32, 1024], P(None, 'gz', 'gy', 'gx')
The draws below stay inside these ranges and needn't reach their ends.
Inputs may be any that keep to these rules, and one draw needn't show every extreme that they name: In each row of a node's 27 blocks the entry on the diagonal of the middle block is positive and larger than the sum of magnitudes of the row's other 80 entries.
All inputs are finite; a program needn't handle non-finite values.
Results may differ from the reference program's by a relative error of at most 0.0003.
Values sent between devices are 32-bit elements; how exact they have to be, the bound alone decides.
No kernel may reach another device: no remote copies, remote signals or barrier semaphores. Data moves between devices by JAX's collectives and lax.ppermute only.
A program may use at most 128 MiB of HBM per device.

```python
import jax
import jax.numpy as jnp
import numpy as np
from jax import lax

STEPS = 4
NCLASS = 4
NX = 2048
NY = 64
NZ = 16


def draw_blocks(key, part):
    key = jax.random.fold_in(key, 11)
    first_key, second_key = jax.random.split(key)
    full_shape = (3, 3, 3, 3, 3, NZ, NY, NX)
    others = jax.random.uniform(first_key, full_shape, jnp.float32, -0.02, 0.02)
    diagonal = jax.random.uniform(second_key, (3, NZ, NY, NX), jnp.float32, 2.0, 3.0)
    centre = np.zeros((3, 3, 3, 1, 1, 1, 1, 1), np.float32)
    centre[1, 1, 1] = 1.0
    select = centre * np.eye(3, dtype=np.float32).reshape(1, 1, 1, 3, 3, 1, 1, 1)
    select = jnp.asarray(select)
    return (others * (1.0 - select) + select * diagonal[None, None, None, :, None]).astype(jnp.float32)


def with_ends(values, own_key, least, high):
    longest = values.shape.index(max(values.shape))
    spots = []
    for shift in (0, 1):
        where = [jax.random.randint(jax.random.fold_in(own_key, axis), (), 0, length) for axis, length in enumerate(values.shape)]
        where[longest] = (where[longest] + shift) % values.shape[longest]
        spots.append(tuple(where))
    return values.at[spots[0]].set(least).at[spots[1]].set(high)


def levels(own_key, shape, pieces, least, high):
    def one(dim, blocks):
        draws = jax.random.uniform(jax.random.fold_in(jax.random.fold_in(own_key, 6), dim), (blocks,), jnp.float32, least / len(pieces), high / len(pieces))
        return jnp.repeat(jnp.exp(draws), shape[dim] // blocks).reshape((-1,) + (1,) * (len(shape) - dim - 1))

    level = one(*pieces[0])
    for cut in pieces[1:]:
        level = level * one(*cut)
    return level


def noise(rng, shape, scale, most, cuts=(), kind=jnp.bfloat16):
    result = scale * jax.random.normal(rng, shape, jnp.float32)
    if cuts:
        result = result * levels(rng, shape, cuts, -0.22, 0.18)
    return jnp.clip(result, -most, most).astype(kind)


def setup_inputs(seed: int = 0) -> dict:
    streams_of = jax.random.split(jax.random.key(seed), 4)
    return {
        "blocks": draw_blocks(jax.random.fold_in(streams_of[3], 71), 0),
        "classes": with_ends(jax.random.randint(streams_of[1], (NZ, NY, NX), 0, NCLASS), jax.random.fold_in(streams_of[1], 1), 0, NCLASS - 1).astype(jnp.int32),
        "residual": noise(streams_of[2], (3, NZ, NY, NX), 1.0, 6.0, ((1, 4), (2, 8), (3, 16)), jnp.float32),
    }


CHEB_LOW = 0.1
CHEB_HIGH = 1.0


def spread(distance):
    return 1.0 if distance == 0 else 0.5


def coarsen(stiffness, loads, odim, pdim, rdim, start, total):
    extent = stiffness.shape[pdim]
    halved = (extent - 1) // 2
    offsets = jnp.arange(3, dtype=jnp.int32) - 1
    fine_pos = start - 1 + jnp.arange(extent, dtype=jnp.int32)
    nearby = fine_pos[None, :] + offsets[:, None]
    inside = jnp.logical_and(nearby >= 0, nearby < total).astype(jnp.float32)
    shaped = [1] * stiffness.ndim
    shaped[odim] = 3
    shaped[pdim] = extent
    masked = stiffness * inside.reshape(shaped)
    stacked = []
    for coarse_step in (-1, 0, 1):
        running = None
        for fine_shift in (-1, 0, 1):
            picked = lax.slice_in_dim(masked, fine_shift + 1, fine_shift + 2 * halved, 2, pdim)
            for fine_step in (-1, 0, 1):
                remain = fine_shift + fine_step - 2 * coarse_step
                if abs(remain) <= 1:
                    product = (spread(fine_shift) * spread(remain)) * lax.slice_in_dim(picked, fine_step + 1, fine_step + 2, 1, odim)
                    running = product if running is None else running + product
        stacked.append(running)
    coarse = jnp.concatenate(stacked, axis=odim)
    coarse_pos = start // 2 + jnp.arange(halved, dtype=jnp.int32)
    reach = coarse_pos[None, :] + offsets[:, None]
    keeper = jnp.logical_and(reach >= 0, reach < total // 2).astype(jnp.float32)
    shaped[pdim] = halved
    coarse = coarse * keeper.reshape(shaped)
    restricted = None
    for fine_shift in (-1, 0, 1):
        sliced = spread(fine_shift) * lax.slice_in_dim(loads, fine_shift + 1, fine_shift + 2 * halved, 2, rdim)
        restricted = sliced if restricted is None else restricted + sliced
    return coarse, restricted


def apply_stencil(operator, padded):
    depth, height, width = operator.shape[5:]
    output = jnp.zeros((3, depth, height, width), jnp.float32)
    for along_z in range(3):
        for along_y in range(3):
            for along_x in range(3):
                nearby = padded[:, along_z:along_z + depth, along_y:along_y + height, along_x:along_x + width]
                output = output + jnp.sum(operator[along_z, along_y, along_x] * nearby[None], axis=1)
    return output


def chebyshev(operator, loads, apply_fn):
    row_total = jnp.sum(jnp.abs(operator), axis=(0, 1, 2, 4))
    inverse = 1.0 / (row_total + 1e-6)
    centre_value = (CHEB_HIGH + CHEB_LOW) / 2.0
    half_width = (CHEB_HIGH - CHEB_LOW) / 2.0
    ratio_sigma = centre_value / half_width
    rho_now = 1.0 / ratio_sigma
    solution = jnp.zeros_like(loads)
    remaining = loads
    direction = inverse * remaining / centre_value
    for iteration in range(STEPS):
        solution = solution + direction
        if iteration < STEPS - 1:
            remaining = remaining - apply_fn(direction)
            rho_next = 1.0 / (2.0 * ratio_sigma - rho_now)
            direction = (rho_next * rho_now) * direction + (2.0 * rho_next / half_width) * (inverse * remaining)
            rho_now = rho_next
    return solution


def reference(blocks, classes, residual):
    weight_k = classes.astype(jnp.float32)
    scaled = 0.05 + 0.95 * (weight_k * weight_k * weight_k) / 27.0
    stiffness = blocks * scaled[None, None, None, None, None]
    loads = residual
    stiffness = jnp.pad(stiffness, [(0, 0)] * 7 + [(1, 0)])
    loads = jnp.pad(loads, [(0, 0)] * 3 + [(1, 0)])
    stiffness, loads = coarsen(stiffness, loads, 2, 7, 3, 0, NX)
    stiffness = jnp.pad(stiffness, [(0, 0)] * 6 + [(1, 0), (0, 0)])
    loads = jnp.pad(loads, [(0, 0)] * 2 + [(1, 0), (0, 0)])
    stiffness, loads = coarsen(stiffness, loads, 1, 6, 2, 0, NY)
    stiffness = jnp.pad(stiffness, [(0, 0)] * 5 + [(1, 0), (0, 0), (0, 0)])
    loads = jnp.pad(loads, [(0, 0), (1, 0), (0, 0), (0, 0)])
    stiffness, loads = coarsen(stiffness, loads, 0, 5, 1, 0, NZ)

    def apply_fn(vector):
        return apply_stencil(stiffness, jnp.pad(vector, ((0, 0), (1, 1), (1, 1), (1, 1))))

    solution = chebyshev(stiffness, loads, apply_fn)
    return stiffness, solution
```

```python
import functools

import jax
import jax.numpy as jnp
from jax import lax
from jax.experimental import pallas as pl
from jax.experimental.pallas import tpu as pltpu
from jax.sharding import PartitionSpec as P

STEPS = 4
CHEB_LOW = 0.1
CHEB_HIGH = 1.0
CENTRE = (CHEB_HIGH + CHEB_LOW) / 2.0
HALF = (CHEB_HIGH - CHEB_LOW) / 2.0
SIGMA = CENTRE / HALF

ITEMS = 42
VMEM = pl.BlockSpec(memory_space=pltpu.VMEM)
LIMIT = pltpu.CompilerParams(vmem_limit_bytes=40 * 1024 * 1024)


def lanes_of():
    return lax.broadcasted_iota(jnp.int32, (8, 128), 1)


def rows_of():
    return lax.broadcasted_iota(jnp.int32, (8, 128), 0)


def lroll(v, s):
    s = s % 128
    return v if s == 0 else pltpu.roll(v, s, 1)


def sroll(v, s):
    s = s % 8
    return v if s == 0 else pltpu.roll(v, s, 0)


def slot_mask(lane, j):
    right = jnp.logical_and(lane >= 3 * j, lane < 3 * j + 3)
    left = jnp.logical_and(lane >= 3 * j + 61, lane < 3 * j + 64)
    return jnp.logical_or(right, left)


def packed_size(n):
    return (n + 1) // 2 + (n + 19) // 20


def pack(vs):
    lane = lanes_of()
    out = []
    for i in range(0, len(vs), 2):
        other = lroll(vs[i + 1], 64) if i + 1 < len(vs) else jnp.zeros_like(vs[i])
        out.append(jnp.where(lane < 64, vs[i], other))
    for base in range(0, len(vs), 20):
        held = jnp.zeros((8, 128), jnp.float32)
        for j, v in enumerate(vs[base : base + 20]):
            held = jnp.where(slot_mask(lane, j), lroll(v, 3 * j - 64), held)
        out.append(held)
    return out


def unpack(load, n):
    lane = lanes_of()
    edge = jnp.logical_or(jnp.logical_and(lane >= 64, lane < 67), lane >= 125)
    mains = (n + 1) // 2
    out = []
    for i in range(n):
        main = load(i // 2)
        if i % 2:
            main = lroll(main, 64)
        held = lroll(load(mains + i // 20), 64 - 3 * (i % 20))
        out.append(jnp.where(lane < 64, main, jnp.where(edge, held, 0.0)))
    return out


def to_right(v, j):
    return lroll(v, 4 * j - 61)


def to_left(v, j):
    return lroll(v, 4 * j)


def pack_sides(vs, store_right, store_left):
    lane = lanes_of()
    for base in range(0, len(vs), 32):
        right = jnp.zeros((8, 128), jnp.float32)
        left = jnp.zeros((8, 128), jnp.float32)
        for j, v in enumerate(vs[base : base + 32]):
            mask = lane // 4 == j
            right = jnp.where(mask, to_right(v, j), right)
            left = jnp.where(mask, to_left(v, j), left)
        store_right(base // 32, right)
        store_left(base // 32, left)


def add_sides(v, t, from_left, from_right):
    lane = lanes_of()
    j = t % 32
    low = jnp.logical_or(lane >= 125, lane == 0)
    high = jnp.logical_and(lane >= 64, lane < 67)
    left = lroll(from_left(t // 32), 125 - 4 * j)
    right = lroll(from_right(t // 32), 64 - 4 * j)
    return v + jnp.where(low, left, jnp.where(high, right, 0.0))


def halves(minus, zero, plus):
    h, g = 0.5 * minus, 0.5 * plus
    quarter = 0.25 * zero
    return h, g, h + quarter, g + quarter


def coarsen_kernel(blocks, classes, residual, w, wl, right, left, scale):
    step = pl.program_id(0)
    gx, gy, gz = (lax.axis_index(a) for a in ("gx", "gy", "gz"))
    lane, row = lanes_of(), rows_of()
    even = row % 2 == 0
    not_last_x = (gx < lax.axis_size("gx") - 1).astype(jnp.float32)
    not_last_y = (gy < lax.axis_size("gy") - 1).astype(jnp.float32)
    not_last_z = (gz < lax.axis_size("gz") - 1).astype(jnp.float32)
    pick = jnp.where(lane < 64, 2 * lane, 127) % 128

    def squeeze(v):
        g = jnp.take_along_axis(v, pick, axis=1, mode="promise_in_bounds")
        return jnp.where(lane <= 64, g, 0.0)

    @pl.when(step == 0)
    def _():
        low_x = jnp.where(jnp.logical_and(lane == 0, gx == 0), 0.0, 1.0)
        low_y = jnp.where(jnp.logical_and(row == 0, gy == 0), 0.0, 1.0)
        low_z = (gz > 0).astype(jnp.float32)
        for z in range(4):
            k = classes[z].astype(jnp.float32)
            s = 0.05 + 0.95 * (k * k * k) / 27.0
            for cy in range(2):
                for cx in range(2):
                    v = s
                    if cy:
                        v = v * low_y
                    if cx:
                        v = v * low_x
                    scale[cy * 2 + cx, z] = v
                    if z == 0:
                        scale[cy * 2 + cx, 4] = v * low_z

    @pl.when(step == 0)
    def _():
        items = []
        for c in range(3):
            f = [residual[c, z] for z in range(4)]
            planes = [f[0] + 0.5 * f[1], 0.5 * f[1] + f[2] + 0.5 * f[3], 0.5 * f[3]]
            full, beyond = [], []
            for v in planes:
                h = 0.5 * v
                before = sroll(h, 1)
                full.append(v + sroll(h, -1) + jnp.where(row == 0, 0.0, before))
                beyond.append(h * not_last_y)
            main = jnp.where(even, full[0], sroll(full[1], 1))
            ghost = jnp.where(even, full[2], 0.0)
            for z in range(3):
                ghost = jnp.where(row == 1 + 2 * z, sroll(beyond[z], 2 + 2 * z), ghost)
            items.append((main, ghost))
        vs = []
        for v in [m for m, _ in items] + [g for _, g in items]:
            h = 0.5 * v
            v = v + lroll(h, -1) + jnp.where(lane == 0, 0.0, lroll(h, 1))
            v = jnp.where(lane == 127, h * not_last_x, v)
            vs.append(squeeze(v))
        for i, v in enumerate(vs):
            wl[i] = v

        def put_right(i, v):
            right[9, i] = v

        def put_left(i, v):
            left[9, i] = v

        pack_sides(vs, put_right, put_left)
        right[9, 1] = jnp.zeros((8, 128), jnp.float32)
        left[9, 1] = jnp.zeros((8, 128), jnp.float32)

    ydone = {}
    for ox in range(3):
        slots = {}
        for oy in range(3):
            kind = (2 if oy == 0 else 0) + (1 if ox == 0 else 0)
            s = [[None] * 4 for _ in range(3)]
            for oz in range(3):
                for z in range(4):
                    factor = scale[kind, 4 if (z == 0 and oz == 0) else z]
                    s[oz][z] = blocks[oz, oy, ox, 0, 0, z] * factor
            _, _, a1, b1 = halves(s[0][1], s[1][1], s[2][1])
            _, _, a3, b3 = halves(s[0][3], s[1][3], s[2][3])
            h0, g0 = 0.5 * s[0][0], 0.5 * s[2][0]
            h2, g2 = 0.5 * s[0][2], 0.5 * s[2][2]
            slots[0, 0, oy] = h0
            slots[1, 0, oy] = h0 + g0 + s[1][0] + a1
            slots[2, 0, oy] = g0 + b1
            slots[0, 1, oy] = h2 + a1
            slots[1, 1, oy] = h2 + g2 + s[1][2] + b1 + a3
            slots[2, 1, oy] = (g2 + b3) * not_last_z
            slots[3, 0, oy] = a3
            slots[3, 1, oy] = b3
        beyond = [jnp.zeros((8, 128), jnp.float32) for _ in range(2)]
        for slot in range(4):
            parts = []
            for z in range(2):
                v = [slots[slot, z, oy] for oy in range(3)]
                h, g, a, b = halves(*v)
                first = row == 0
                lower = h + jnp.where(first, 0.0, sroll(a, 1))
                middle = h + g + v[1] + jnp.where(first, 0.0, sroll(b, 1)) + sroll(a, -1)
                upper = g + sroll(b, -1)
                upper = jnp.where(row == 6, upper * not_last_y, upper)
                parts.append((lower, middle, upper))
                for cy, ghost in enumerate((a, b)):
                    at = (slot % 2) * 4 + cy * 2 + z
                    beyond[slot // 2] = jnp.where(row == at, sroll(ghost, at + 1) * not_last_y, beyond[slot // 2])
            for cy in range(3):
                ydone[slot * 3 + cy, ox] = jnp.where(even, parts[0][cy], sroll(parts[1][cy], 1))
        ydone[12, ox], ydone[13, ox] = beyond
    vs = [None] * ITEMS
    for i in range(14):
        v = [ydone[i, ox] for ox in range(3)]
        h, g, a, b = halves(*v)
        first, end = lane == 0, lane == 127
        lower = h + jnp.where(first, 0.0, lroll(a, 1))
        lower = jnp.where(end, a * not_last_x, lower)
        middle = h + g + v[1] + jnp.where(first, 0.0, lroll(b, 1)) + lroll(a, -1)
        middle = jnp.where(end, b * not_last_x, middle)
        upper = g + lroll(b, -1)
        upper = jnp.where(end, 0.0, jnp.where(lane == 126, upper * not_last_x, upper))
        for cx, done in enumerate((lower, middle, upper)):
            at = i * 3 + cx if i < 12 else 36 + cx * 2 + i - 12
            vs[at] = squeeze(done)
            w[step, at] = vs[at]

    def keep_right(i, v):
        right[step, i] = v

    def keep_left(i, v):
        left[step, i] = v

    pack_sides(vs, keep_right, keep_left)


def sides_kernel(w, wl, from_left, from_right, w_out, wl_out, message):
    row = rows_of()

    def body(rc, carry):
        vs = []
        for t in range(ITEMS):
            v = add_sides(w[rc, t], t, lambda g: from_left[rc, g], lambda g: from_right[rc, g])
            w_out[rc, t] = v
            vs.append(v)
        ends = [vs[36 + cx * 2 + 1] for cx in range(3)]
        sent = vs[27:36] + [jnp.where(row < 4, sroll(ends[0], 4), ends[1]), ends[2]]
        for i, v in enumerate(pack(sent)):
            message[rc, i] = v
        return carry

    lax.fori_loop(0, 9, body, 0)
    vs = []
    for t in range(6):
        v = add_sides(wl[t], t, lambda g: from_left[9, g], lambda g: from_right[9, g])
        wl_out[t] = v
        vs.append(v)
    done = pack(vs[3:])
    for i in range(packed_size(11)):
        message[9, i] = done[i] if i < len(done) else jnp.zeros((8, 128), jnp.float32)


def planes_kernel(w, wl, received, w_out, wl_out, up, down, total):
    row = rows_of()
    even = row % 2 == 0
    total[...] = jnp.zeros_like(total)

    def body(rc, carry):
        got = unpack(lambda i: received[rc, i], 11)
        f = [None] * 27
        for k in range(27):
            v = w[rc, k]
            if k < 9:
                v = v + jnp.where(even, got[k], 0.0)
            elif k < 18:
                v = v + jnp.where(even, sroll(got[k - 9], -1), 0.0)
            f[k] = v
            w_out[rc, k] = v
        for k in range(27, 36):
            w_out[rc, k] = jnp.zeros((8, 128), jnp.float32)
        firsts, seconds = [], []
        for cx in range(3):
            end = (sroll(got[9], 4), got[9], got[10])[cx]
            v = w[rc, 36 + cx * 2]
            moved = jnp.where(row < 4, sroll(end, 4), sroll(end, -1))
            v = v + jnp.where(even, moved, 0.0)
            firsts.append(v)
            w_out[rc, 36 + cx * 2] = v
            v = w[rc, 36 + cx * 2 + 1]
            seconds.append(v)
            w_out[rc, 36 + cx * 2 + 1] = v
        magnitude = jnp.abs(f[0])
        for k in range(1, 27):
            magnitude = magnitude + jnp.abs(f[k])
        total[rc // 3] += magnitude
        ups, downs = [], []
        for k in range(0, 27, 2):
            one, two = f[k], f[k + 1] if k + 1 < 27 else jnp.zeros((8, 128), jnp.float32)
            ups.append(jnp.where(row < 4, sroll(one, 4), two))
            downs.append(jnp.where(row < 4, one, sroll(two, 4)))
        ups += firsts + [jnp.where(row < 4, seconds[0], sroll(seconds[1], 4)), seconds[2]]
        for i, v in enumerate(pack(ups)):
            up[rc, i] = v
        for i, v in enumerate(pack(downs)):
            down[rc, i] = v
        return carry

    lax.fori_loop(0, 9, body, 0)
    got = unpack(lambda i: received[9, i], 3)
    ups, downs = [], []
    for c in range(3):
        load = wl[c] + jnp.where(even, got[c], 0.0)
        ghost = wl[3 + c] + jnp.where(row == 1, sroll(got[c], -4), 0.0)
        wl_out[c] = load
        wl_out[3 + c] = ghost
        d = load * (1.0 / (total[c] + 1e-06)) / CENTRE
        v = jnp.where(row < 4, sroll(load, 4), 0.0)
        v = jnp.where(row == 4, sroll(ghost, 3), v)
        v = jnp.where(row == 5, sroll(ghost, 2), v)
        ups.append(jnp.where(row >= 6, sroll(d, 4), v))
        downs.append(jnp.where(row < 4, load, jnp.where(row >= 6, sroll(d, 2), 0.0)))
    for ref, vs, size in ((up, ups, packed_size(19)), (down, downs, packed_size(14))):
        done = pack(vs)
        for i in range(size):
            ref[9, i] = done[i] if i < len(done) else jnp.zeros((8, 128), jnp.float32)


def share_planes(d, piece):
    gz = lax.axis_index("gz")
    even = lax.broadcasted_iota(jnp.int32, (24, 128), 0) % 2 == 0

    def pair(one, two, z):
        if z == 0:
            return jnp.where(even, one, pltpu.roll(two, 1, 0))
        return jnp.where(even, pltpu.roll(one, 23, 0), two)

    for i, (one, two) in enumerate(((d[0], d[1]), (d[2], d[2]))):
        first, last = pair(one, two, 0), pair(one, two, 1)
        for to in range(piece.shape[0]):
            piece[to, i] = jnp.where(to < gz, first, last)


def rows_kernel(w, wl, from_low, from_high, operator, whole, q, d, inverse, piece, total, turned):
    row = rows_of()
    ghosts = jnp.logical_or(row == 4, row == 5)
    total[...] = jnp.zeros_like(total)

    def body(rc, carry):
        ups = unpack(lambda i: from_low[rc, i], 19)
        downs = unpack(lambda i: from_high[rc, i], 14)
        seconds = [ups[17], sroll(ups[17], 4), ups[18]]
        top_sum = jnp.zeros((8, 128), jnp.float32)
        bottom_sum = jnp.zeros((8, 128), jnp.float32)
        for cz in range(3):
            for cy in range(3):
                for cx in range(3):
                    k = cz * 9 + cy * 3 + cx
                    f = sroll(w[rc, k], 4)
                    above, below = ups[k // 2], downs[k // 2]
                    top = jnp.where(row < 4, sroll(above, 4) if k % 2 else above, f)
                    bottom = jnp.where(row < 4, f, below if k % 2 else sroll(below, 4))
                    if cy < 2:
                        at = (cz % 2) * 4 + cy * 2
                        got = ups[14 + cx] if cz < 2 else seconds[cx]
                        own = w[rc, 36 + cx * 2 + cz // 2]
                        top = top + jnp.where(ghosts, sroll(got, 4 - at), 0.0)
                        bottom = bottom + jnp.where(ghosts, sroll(own, 4 - at), 0.0)
                    whole[rc, k, 0:8] = top
                    whole[rc, k, 8:16] = bottom
                    top_sum = top_sum + jnp.abs(top)
                    bottom_sum = bottom_sum + jnp.abs(bottom)
        total[rc // 3, 0:8] += top_sum
        total[rc // 3, 8:16] += bottom_sum
        for cz in range(3):
            for cy in range(3):
                for cx in range(3):
                    for z in range(2):
                        v = whole[rc, cz * 9 + cy * 3 + cx, pl.ds(4 + z, 4, stride=2), :]
                        operator[cz, cy, cx, rc // 3, rc % 3, z] = v[:, 0:64]
        return carry

    lax.fori_loop(0, 9, body, 0)
    ups = unpack(lambda i: from_low[9, i], 3)
    downs = unpack(lambda i: from_high[9, i], 3)
    for c in range(3):
        load, ghost = sroll(wl[c], 4), wl[3 + c]
        q[c, 0:8] = jnp.where(row < 4, ups[c], load + jnp.where(ghosts, ups[c], 0.0))
        below = sroll(downs[c], 4)
        below = below + jnp.where(row == 4, sroll(ghost, 3), jnp.where(row == 5, sroll(ghost, 2), 0.0))
        q[c, 8:16] = jnp.where(row < 4, load, below)
        part = 1.0 / (total[c] + 1e-06)
        inverse[c] = part
        d[c, 16:24] = jnp.zeros((8, 128), jnp.float32)
        d[c, 2:18] = part * q[c] / CENTRE
        turned[...] = ups[c]
        d[c, 0:2] = turned[6:8]
        turned[...] = downs[c]
        d[c, 18:20] = turned[6:8]
    share_planes([d[c] for c in range(3)], piece)


def apply_to(whole, d, received, near, out):
    gz = lax.axis_index("gz")
    even = lax.broadcasted_iota(jnp.int32, (24, 128), 0) % 2 == 0
    below = jnp.maximum(gz - 1, 0)
    above = jnp.minimum(gz + 1, received.shape[0] - 1)
    for c in range(3):
        own = d[c]
        low, high = received[below, c // 2], received[above, c // 2]
        if c == 1:
            low = pltpu.roll(low, 23, 0)
        else:
            high = pltpu.roll(high, 1, 0)
        near[0, c] = jnp.where(even, low, pltpu.roll(own, 1, 0))
        near[1, c] = own
        near[2, c] = jnp.where(even, pltpu.roll(own, 23, 0), high)
    sums = [jnp.zeros((16, 128), jnp.float32) for _ in range(3)]
    for cz in range(3):
        for cy in range(3):
            for c in range(3):
                v = near[cz, c, pl.ds(2 * cy, 16), :]
                for cx, moved in enumerate((pltpu.roll(v, 1, 1), v, pltpu.roll(v, 127, 1))):
                    for r in range(3):
                        sums[r] = sums[r] + whole[r * 3 + c, cz * 9 + cy * 3 + cx] * moved
    for r in range(3):
        out(r, sums[r])


def step_kernel(first, rho_now, rho_next, last, *refs):
    whole, q, d, inverse, received = refs[:5]
    refs = refs[5:]
    if first:
        x = None
    else:
        x, refs = refs[0], refs[1:]
    if last:
        solution_out, near, turned = refs
    else:
        q_out, d_out, x_out, piece, near = refs

    def update(r, product):
        now = d[r, 2:18]
        x_now = now if x is None else x[r] + now
        q_now = q[r] - product
        d_new = rho_next * rho_now * now + 2.0 * rho_next / HALF * (inverse[r] * q_now)
        if last:
            turned[...] = x_now + d_new
            for z in range(2):
                solution_out[r, z] = turned[pl.ds(4 + z, 4, stride=2), :][:, 0:64]
        else:
            x_out[r] = x_now
            q_out[r] = q_now
            d_out[r, 0:8] = jnp.zeros((8, 128), jnp.float32)
            d_out[r, 16:24] = jnp.zeros((8, 128), jnp.float32)
            d_out[r, 2:18] = d_new

    apply_to(whole, d, received, near, update)
    if not last:
        share_planes([d_out[c] for c in range(3)], piece)


def shape(*dims):
    return jax.ShapeDtypeStruct(dims, jnp.float32)


def along(block, axis, distance):
    n = lax.axis_size(axis)
    route = [(i, i + distance) for i in range(n) if 0 <= i + distance < n]
    return lax.ppermute(block, axis, route)


def shards(blocks, classes, residual):
    nz = lax.axis_size("gz")
    w_shape, wl_shape = shape(9, ITEMS, 8, 128), shape(6, 8, 128)
    w, wl, right, left = pl.pallas_call(
        coarsen_kernel,
        grid=(9,),
        in_specs=[
            pl.BlockSpec((3, 3, 3, 1, 1, 4, 8, 128), lambda i: (0, 0, 0, i // 3, i % 3, 0, 0, 0)),
            pl.BlockSpec((4, 8, 128), lambda i: (0, 0, 0)),
            pl.BlockSpec((3, 4, 8, 128), lambda i: (0, 0, 0, 0)),
        ],
        out_specs=[VMEM] * 4,
        out_shape=[w_shape, wl_shape, shape(10, 2, 8, 128), shape(10, 2, 8, 128)],
        scratch_shapes=[pltpu.VMEM((4, 5, 8, 128), jnp.float32)],
        compiler_params=LIMIT,
    )(blocks, classes, residual)
    from_left, from_right = along(right, "gx", 1), along(left, "gx", -1)
    w, wl, message = pl.pallas_call(
        sides_kernel,
        in_specs=[VMEM] * 4,
        out_specs=[VMEM] * 3,
        out_shape=[w_shape, wl_shape, shape(10, packed_size(11), 8, 128)],
        compiler_params=LIMIT,
    )(w, wl, from_left, from_right)
    received = along(message, "gz", 1)
    w, wl, up, down = pl.pallas_call(
        planes_kernel,
        in_specs=[VMEM] * 3,
        out_specs=[VMEM] * 4,
        out_shape=[w_shape, wl_shape, shape(10, packed_size(19), 8, 128), shape(10, packed_size(14), 8, 128)],
        scratch_shapes=[pltpu.VMEM((3, 8, 128), jnp.float32)],
        compiler_params=LIMIT,
    )(w, wl, received)
    from_low, from_high = along(up, "gy", 1), along(down, "gy", -1)
    operator, whole, q, d, inverse, piece = pl.pallas_call(
        rows_kernel,
        in_specs=[VMEM] * 4,
        out_specs=[VMEM] * 6,
        out_shape=[
            shape(3, 3, 3, 3, 3, 2, 4, 64),
            shape(9, 27, 16, 128),
            shape(3, 16, 128),
            shape(3, 24, 128),
            shape(3, 16, 128),
            shape(nz, 2, 24, 128),
        ],
        scratch_shapes=[pltpu.VMEM((3, 16, 128), jnp.float32), pltpu.VMEM((8, 128), jnp.float32)],
        compiler_params=LIMIT,
    )(w, wl, from_low, from_high)
    x = []
    rho_now = 1.0 / SIGMA
    for step in range(STEPS - 1):
        rho_next = 1.0 / (2.0 * SIGMA - rho_now)
        last = step == STEPS - 2
        shared = lax.all_to_all(piece, "gz", 0, 0)
        if last:
            outs = shape(3, 2, 4, 64)
        else:
            outs = [shape(3, 16, 128), shape(3, 24, 128), shape(3, 16, 128), shape(nz, 2, 24, 128)]
        done = pl.pallas_call(
            functools.partial(step_kernel, step == 0, rho_now, rho_next, last),
            in_specs=[VMEM] * (5 + len(x)),
            out_specs=VMEM if last else [VMEM] * 4,
            out_shape=outs,
            scratch_shapes=[pltpu.VMEM((3, 3, 24, 128), jnp.float32)] + ([pltpu.VMEM((16, 128), jnp.float32)] if last else []),
            compiler_params=LIMIT,
        )(whole, q, d, inverse, shared, *x)
        if last:
            return operator, done
        q, d, x, piece = done
        x = [x]
        rho_now = rho_next


def solution(mesh):
    placed = (
        P(None, None, None, None, None, "gz", "gy", "gx"),
        P("gz", "gy", "gx"),
        P(None, "gz", "gy", "gx"),
    )
    return jax.shard_map(
        shards,
        mesh=mesh,
        in_specs=placed,
        out_specs=(P(None, None, None, None, None, "gz", "gy", "gx"), P(None, "gz", "gy", "gx")),
        check_vma=False,
    )
```

```python
import functools
import itertools

import jax
import jax.numpy as jnp
from jax import lax
from jax.experimental import pallas as pl
from jax.experimental.pallas import tpu as pltpu
from jax.sharding import PartitionSpec as P

STEPS = 4
CHEB_LOW = 0.1
CHEB_HIGH = 1.0
CENTRE = (CHEB_HIGH + CHEB_LOW) / 2.0
HALF = (CHEB_HIGH - CHEB_LOW) / 2.0
SIGMA = CENTRE / HALF

ITEMS = 32
PLANE = 11
UPS, DOWNS = 18, 14
VMEM = pl.BlockSpec(memory_space=pltpu.VMEM)
HBM = pl.BlockSpec(memory_space=pltpu.HBM)
LIMIT = pltpu.CompilerParams(vmem_limit_bytes=40 * 1024 * 1024)


def lanes_of():
    return lax.broadcasted_iota(jnp.int32, (8, 128), 1)


def rows_of():
    return lax.broadcasted_iota(jnp.int32, (8, 128), 0)


def lroll(v, s):
    s = s % 128
    return v if s == 0 else pltpu.roll(v, s, 1)


def sroll(v, s):
    s = s % 8
    return v if s == 0 else pltpu.roll(v, s, 0)


def slot_mask(lane, j):
    right = jnp.logical_and(lane >= 3 * j, lane < 3 * j + 3)
    left = jnp.logical_and(lane >= 3 * j + 61, lane < 3 * j + 64)
    return jnp.logical_or(right, left)


def packed_size(n):
    return (n + 1) // 2 + (n + 19) // 20


def pack(vs):
    lane = lanes_of()
    out = []
    for i in range(0, len(vs), 2):
        other = lroll(vs[i + 1], 64) if i + 1 < len(vs) else jnp.zeros_like(vs[i])
        out.append(jnp.where(lane < 64, vs[i], other))
    for base in range(0, len(vs), 20):
        held = jnp.zeros((8, 128), jnp.float32)
        for j, v in enumerate(vs[base : base + 20]):
            held = jnp.where(slot_mask(lane, j), lroll(v, 3 * j - 64), held)
        out.append(held)
    return out


def unpack(load, n):
    lane = lanes_of()
    edge = jnp.logical_or(jnp.logical_and(lane >= 64, lane < 67), lane >= 125)
    mains = (n + 1) // 2
    out = []
    for i in range(n):
        main = load(i // 2)
        if i % 2:
            main = lroll(main, 64)
        held = lroll(load(mains + i // 20), 64 - 3 * (i % 20))
        out.append(jnp.where(lane < 64, main, jnp.where(edge, held, 0.0)))
    return out


def right_slot(lane, j):
    return lane // 4 == j


def left_slot(lane, j):
    at = (lane - (4 * j + 67)) % 128
    return at < 3


def pack_sides(vs):
    lane = lanes_of()
    right = jnp.zeros((8, 128), jnp.float32)
    left = jnp.zeros((8, 128), jnp.float32)
    for j, v in enumerate(vs):
        moved = lroll(v, 4 * j - 61)
        right = jnp.where(right_slot(lane, j), moved, right)
        left = jnp.where(left_slot(lane, j), moved, left)
    return right, left


def sides(from_left, from_right, j):
    lane = lanes_of()
    both = lroll(jnp.where(right_slot(lane, j), from_left, from_right), -(4 * j + 3))
    ends = jnp.logical_or(jnp.logical_or(lane >= 125, lane == 0), jnp.logical_and(lane >= 64, lane < 67))
    return jnp.where(ends, both, 0.0)


def plane_size(n):
    return n // 2 + 1


def pack_plane(vs):
    lane = lanes_of()
    out = [jnp.where(lane < 64, vs[i], lroll(vs[i + 1], 64)) for i in range(0, len(vs) - 1, 2)]
    last = jnp.where(lane < 64, vs[-1], 0.0)
    for i, v in enumerate(vs):
        last = jnp.where(lane == 64 + i, lroll(v, i), last)
    return out + [last]


def unpack_plane(load, n, from_left, from_right):
    lane = lanes_of()
    last = load(n // 2)
    out = []
    for i in range(n):
        main = load(i // 2)
        if i % 2:
            main = lroll(main, 64)
        main = jnp.where(lane < 64, main, jnp.where(lane == 64, lroll(last, -i), 0.0))
        out.append(main + sides(from_left, from_right, i))
    return out


def halves(minus, zero, plus):
    h, g = 0.5 * minus, 0.5 * plus
    quarter = 0.25 * zero
    return h, g, h + quarter, g + quarter


def coarsen_kernel(blocks_in, classes_in, residual_in, w, wl, right, left, plane, plane_right, plane_left, blocks, classes, residual, scale, sems):
    def fetch(i):
        source = blocks_in.at[:, :, :, i // 3, i % 3]
        return pltpu.make_async_copy(source, blocks.at[i], sems.at[i])

    classes_copy = pltpu.make_async_copy(classes_in, classes, sems.at[9])
    residual_copy = pltpu.make_async_copy(residual_in, residual, sems.at[10])
    classes_copy.start()
    fetch(0).start()
    residual_copy.start()
    for i in range(1, 9):
        fetch(i).start()
    gx, gy, gz = (lax.axis_index(a) for a in ("gx", "gy", "gz"))
    lane, row = lanes_of(), rows_of()
    even = row % 2 == 0
    not_last_x = (gx < lax.axis_size("gx") - 1).astype(jnp.float32)
    not_last_y = (gy < lax.axis_size("gy") - 1).astype(jnp.float32)
    not_last_z = (gz < lax.axis_size("gz") - 1).astype(jnp.float32)
    pick = jnp.where(lane < 64, 2 * lane, 127) % 128

    def squeeze(v):
        g = jnp.take_along_axis(v, pick, axis=1, mode="promise_in_bounds")
        return jnp.where(lane <= 64, g, 0.0)

    def coarsen(step):
        ydone = {}
        for ox in range(3):
            slots = {}
            for oy in range(3):
                kind = (2 if oy == 0 else 0) + (1 if ox == 0 else 0)
                s = [[None] * 4 for _ in range(3)]
                for oz in range(3):
                    for z in range(4):
                        factor = scale[kind, 4 if (z == 0 and oz == 0) else z]
                        s[oz][z] = blocks[step, oz, oy, ox, z] * factor
                _, _, a1, b1 = halves(s[0][1], s[1][1], s[2][1])
                _, _, a3, b3 = halves(s[0][3], s[1][3], s[2][3])
                h0, g0 = 0.5 * s[0][0], 0.5 * s[2][0]
                h2, g2 = 0.5 * s[0][2], 0.5 * s[2][2]
                slots[0, 0, oy] = h0
                slots[1, 0, oy] = h0 + g0 + s[1][0] + a1
                slots[2, 0, oy] = g0 + b1
                slots[0, 1, oy] = h2 + a1
                slots[1, 1, oy] = h2 + g2 + s[1][2] + b1 + a3
                slots[2, 1, oy] = (g2 + b3) * not_last_z
                slots[3, 0, oy] = a3
                slots[3, 1, oy] = b3
            beyond = [jnp.zeros((8, 128), jnp.float32) for _ in range(2)]
            for slot in range(4):
                parts = []
                for z in range(2):
                    v = [slots[slot, z, oy] for oy in range(3)]
                    h, g, a, b = halves(*v)
                    first = row == 0
                    lower = h + jnp.where(first, 0.0, sroll(a, 1))
                    middle = h + g + v[1] + jnp.where(first, 0.0, sroll(b, 1)) + sroll(a, -1)
                    upper = g + sroll(b, -1)
                    upper = jnp.where(row == 6, upper * not_last_y, upper)
                    parts.append((lower, middle, upper))
                    for cy, ghost in enumerate((a, b)):
                        at = (slot % 2) * 4 + cy * 2 + z
                        beyond[slot // 2] = jnp.where(row == at, sroll(ghost, at + 1) * not_last_y, beyond[slot // 2])
                for cy in range(3):
                    ydone[slot * 3 + cy, ox] = jnp.where(even, parts[0][cy], sroll(parts[1][cy], 1))
            ydone[12, ox], ydone[13, ox] = beyond
        kept, sent, rows = [None] * ITEMS, [None] * PLANE, {}
        for i in range(14):
            v = [ydone[i, ox] for ox in range(3)]
            h, g, a, b = halves(*v)
            first, end = lane == 0, lane == 127
            lower = h + jnp.where(first, 0.0, lroll(a, 1))
            lower = jnp.where(end, a * not_last_x, lower)
            middle = h + g + v[1] + jnp.where(first, 0.0, lroll(b, 1)) + lroll(a, -1)
            middle = jnp.where(end, b * not_last_x, middle)
            upper = g + lroll(b, -1)
            upper = jnp.where(end, 0.0, jnp.where(lane == 126, upper * not_last_x, upper))
            for cx, done in enumerate((lower, middle, upper)):
                v = squeeze(done)
                if i < 9:
                    kept[i * 3 + cx] = v
                elif i < 12:
                    sent[(i - 9) * 3 + cx] = v
                elif i == 12:
                    kept[27 + cx] = v
                else:
                    rows[cx] = v
        kept[30] = jnp.where(row < 4, rows[0], sroll(rows[1], 4))
        sent[9] = jnp.where(row < 4, sroll(rows[0], 4), rows[1])
        kept[31] = sent[10] = rows[2]
        for i, v in enumerate(kept):
            w[step, i] = v
        right[step], left[step] = pack_sides(kept)
        plane_right[step], plane_left[step] = pack_sides(sent)
        for i, v in enumerate(pack_plane(sent)):
            plane[step * plane_size(PLANE) + i] = v

    def scales():
        low_x = jnp.where(jnp.logical_and(lane == 0, gx == 0), 0.0, 1.0)
        low_y = jnp.where(jnp.logical_and(row == 0, gy == 0), 0.0, 1.0)
        low_z = (gz > 0).astype(jnp.float32)
        for z in range(4):
            k = classes[z].astype(jnp.float32)
            s = 0.05 + 0.95 * (k * k * k) / 27.0
            for cy in range(2):
                for cx in range(2):
                    v = s
                    if cy:
                        v = v * low_y
                    if cx:
                        v = v * low_x
                    scale[cy * 2 + cx, z] = v
                    if z == 0:
                        scale[cy * 2 + cx, 4] = v * low_z

    def loads():
        items = []
        for c in range(3):
            f = [residual[c, z] for z in range(4)]
            planes = [f[0] + 0.5 * f[1], 0.5 * f[1] + f[2] + 0.5 * f[3], 0.5 * f[3]]
            full, beyond = [], []
            for v in planes:
                h = 0.5 * v
                before = sroll(h, 1)
                full.append(v + sroll(h, -1) + jnp.where(row == 0, 0.0, before))
                beyond.append(h * not_last_y)
            main = jnp.where(even, full[0], sroll(full[1], 1))
            ghost = jnp.where(even, full[2], 0.0)
            for z in range(3):
                ghost = jnp.where(row == 1 + 2 * z, sroll(beyond[z], 2 + 2 * z), ghost)
            items.append((main, ghost))
        vs = []
        for v in [m for m, _ in items] + [g for _, g in items]:
            h = 0.5 * v
            v = v + lroll(h, -1) + jnp.where(lane == 0, 0.0, lroll(h, 1))
            v = jnp.where(lane == 127, h * not_last_x, v)
            vs.append(squeeze(v))
        for i, v in enumerate(vs):
            wl[i] = v

        right[9], left[9] = pack_sides(vs)
        plane_right[9], plane_left[9] = pack_sides(vs[3:])
        for i, v in enumerate(pack_plane(vs[3:])):
            plane[9 * plane_size(PLANE) + i] = v

    classes_copy.wait()
    scales()
    residual_copy.wait()
    loads()

    def body(step, carry):
        fetch(step).wait()
        coarsen(step)
        return carry

    lax.fori_loop(0, 9, body, 0)


def planes_kernel(w, wl, from_left, from_right, plane, plane_left, plane_right, w_out, wl_out, up, down, total):
    row = rows_of()
    even = row % 2 == 0
    total[...] = jnp.zeros_like(total)

    def body(rc, carry):
        got = unpack_plane(lambda i: plane[rc * plane_size(PLANE) + i], PLANE, plane_left[rc], plane_right[rc])
        from_l, from_r = from_left[rc], from_right[rc]
        f = [None] * ITEMS
        for k in range(ITEMS):
            v = w[rc, k] + sides(from_l, from_r, k)
            if k < 9:
                v = v + jnp.where(even, got[k], 0.0)
            elif k < 18:
                v = v + jnp.where(even, sroll(got[k - 9], -1), 0.0)
            elif 27 <= k < 30:
                end = (sroll(got[9], 4), got[9], got[10])[k - 27]
                v = v + jnp.where(even, jnp.where(row < 4, sroll(end, 4), sroll(end, -1)), 0.0)
            f[k] = v
            w_out[rc, k] = v
        magnitude = jnp.abs(f[0])
        for k in range(1, 27):
            magnitude = magnitude + jnp.abs(f[k])
        total[rc // 3] += magnitude
        ups, downs = [], []
        for k in range(0, 27, 2):
            two = f[k + 1] if k + 1 < 27 else None
            ups.append(jnp.where(row < 4, sroll(f[k], 4), sroll(f[31], 4) if two is None else two))
            downs.append(jnp.where(row < 4, f[k], 0.0 if two is None else sroll(two, 4)))
        ups += f[27:31]
        for ref, vs in ((up, ups), (down, downs)):
            for i, v in enumerate(pack(vs)):
                ref[rc * packed_size(len(vs)) + i] = v
        return carry

    lax.fori_loop(0, 9, body, 0)
    got = unpack_plane(lambda i: plane[9 * plane_size(PLANE) + i], 3, plane_left[9], plane_right[9])
    ups, downs = [], []
    for c in range(3):
        load = wl[c] + sides(from_left[9], from_right[9], c) + jnp.where(even, got[c], 0.0)
        ghost = wl[3 + c] + jnp.where(row == 1, sroll(got[c], -4), 0.0)
        ghost = ghost + sides(from_left[9], from_right[9], 3 + c)
        wl_out[c] = load
        wl_out[3 + c] = ghost
        d = load * (1.0 / (total[c] + 1e-06)) / CENTRE
        v = jnp.where(row < 4, sroll(load, 4), 0.0)
        v = jnp.where(row == 4, sroll(ghost, 3), v)
        v = jnp.where(row == 5, sroll(ghost, 2), v)
        ups.append(jnp.where(row >= 6, sroll(d, 4), v))
        downs.append(jnp.where(row < 4, load, jnp.where(row >= 6, sroll(d, 2), 0.0)))
    for ref, vs, size in ((up, ups, packed_size(UPS)), (down, downs, packed_size(DOWNS))):
        for i, v in enumerate(pack(vs)):
            ref[9 * size + i] = v


def piece_rows(n):
    return n + 8 * ((n + 15) // 16)


def share_planes(load, n, piece):
    gz = lax.axis_index("gz")
    even = lax.broadcasted_iota(jnp.int32, (n, 128), 0) % 2 == 0
    d = [load(c) for c in range(3)]
    for z in range(2):
        if z == 0:
            both = jnp.where(even, d[0], pltpu.roll(d[1], 1, 0))
            third = d[2]
        else:
            both = jnp.where(even, pltpu.roll(d[0], n - 1, 0), d[1])
            third = pltpu.roll(d[2], n - 1, 0)
        folds = []
        for at in range(0, n, 16):
            fold = third[at : at + 8]
            if at + 8 < n:
                fold = jnp.where(even[0:8], fold, sroll(third[at + 8 : at + 16], 1))
            folds.append(fold)
        for to in range(piece.shape[0]):
            @pl.when((to >= gz) if z else (to < gz))
            def _():
                piece[to, 0:n] = both
                for i, fold in enumerate(folds):
                    piece[to, n + 8 * i : n + 8 * i + 8] = fold


def plane_of(received, at, n, c):
    if c < 2:
        return received[at, 0:n], c
    parts = []
    for i in range(0, n, 16):
        fold = received[at, n + i // 2 : n + i // 2 + 8]
        parts.append(fold)
        if i + 8 < n:
            parts.append(sroll(fold, -1))
    return jnp.concatenate(parts, axis=0), 0


def rows_kernel(w, wl, from_low, from_high, operator, whole, q, d, inverse, piece, total, turned):
    row = rows_of()
    ghosts = jnp.logical_or(row == 4, row == 5)
    total[...] = jnp.zeros_like(total)

    def body(rc, carry):
        ups = unpack(lambda i: from_low[rc * packed_size(UPS) + i], UPS)
        downs = unpack(lambda i: from_high[rc * packed_size(DOWNS) + i], DOWNS)
        got_ends = [ups[17], sroll(ups[17], 4), sroll(ups[13], 4)]
        own_ends = [w[rc, 30], sroll(w[rc, 30], 4), w[rc, 31]]
        top_sum = jnp.zeros((8, 128), jnp.float32)
        bottom_sum = jnp.zeros((8, 128), jnp.float32)
        for cz in range(3):
            for cy in range(3):
                for cx in range(3):
                    k = cz * 9 + cy * 3 + cx
                    f = sroll(w[rc, k], 4)
                    above, below = ups[k // 2], downs[k // 2]
                    top = jnp.where(row < 4, sroll(above, 4) if k % 2 else above, f)
                    bottom = jnp.where(row < 4, f, below if k % 2 else sroll(below, 4))
                    if cy < 2:
                        at = (cz % 2) * 4 + cy * 2
                        got = ups[14 + cx] if cz < 2 else got_ends[cx]
                        own = w[rc, 27 + cx] if cz < 2 else own_ends[cx]
                        top = top + jnp.where(ghosts, sroll(got, 4 - at), 0.0)
                        bottom = bottom + jnp.where(ghosts, sroll(own, 4 - at), 0.0)
                    whole[rc, k, 0:8] = top
                    whole[rc, k, 8:16] = bottom
                    top_sum = top_sum + jnp.abs(top)
                    bottom_sum = bottom_sum + jnp.abs(bottom)
        total[rc // 3, 0:8] += top_sum
        total[rc // 3, 8:16] += bottom_sum
        for cz in range(3):
            for cy in range(3):
                for cx in range(3):
                    for z in range(2):
                        v = whole[rc, cz * 9 + cy * 3 + cx, pl.ds(4 + z, 4, stride=2), :]
                        operator[cz, cy, cx, rc // 3, rc % 3, z] = v[:, 0:64]
        return carry

    lax.fori_loop(0, 9, body, 0)
    ups = unpack(lambda i: from_low[9 * packed_size(UPS) + i], 3)
    downs = unpack(lambda i: from_high[9 * packed_size(DOWNS) + i], 3)
    for c in range(3):
        load, ghost = sroll(wl[c], 4), wl[3 + c]
        q[c, 0:8] = jnp.where(row < 4, ups[c], load + jnp.where(ghosts, ups[c], 0.0))
        below = sroll(downs[c], 4)
        below = below + jnp.where(row == 4, sroll(ghost, 3), jnp.where(row == 5, sroll(ghost, 2), 0.0))
        q[c, 8:16] = jnp.where(row < 4, load, below)
        part = 1.0 / (total[c] + 1e-06)
        inverse[c] = part
        d[c, 16:24] = jnp.zeros((8, 128), jnp.float32)
        d[c, 2:18] = part * q[c] / CENTRE
        turned[...] = ups[c]
        d[c, 0:2] = turned[6:8]
        turned[...] = downs[c]
        d[c, 18:20] = turned[6:8]
    share_planes(lambda c: d[c], 24, piece)


def apply_to(whole, d, received, n, near, out):
    gz = lax.axis_index("gz")
    even = lax.broadcasted_iota(jnp.int32, (n, 128), 0) % 2 == 0
    below = jnp.maximum(gz - 1, 0)
    above = jnp.minimum(gz + 1, received.shape[0] - 1)
    base = (24 - n) // 4
    for c in range(3):
        own = d[c]
        low, odd = plane_of(received, below, n, c)
        high, _ = plane_of(received, above, n, c)
        if odd:
            low = pltpu.roll(low, n - 1, 0)
        else:
            high = pltpu.roll(high, 1, 0)
        for cz, v in enumerate((
            jnp.where(even, low, pltpu.roll(own, 1, 0)),
            own,
            jnp.where(even, pltpu.roll(own, n - 1, 0), high),
        )):
            if base:
                near[cz, c, 0:8] = jnp.zeros((8, 128), jnp.float32)
                near[cz, c, 16:24] = jnp.zeros((8, 128), jnp.float32)
            near[cz, c, base : base + n] = v
    sums = [jnp.zeros((16, 128), jnp.float32) for _ in range(3)]
    for cz in range(3):
        for cy in range(3):
            for c in range(3):
                v = near[cz, c, pl.ds(2 * cy, 16), :]
                for cx, moved in enumerate((pltpu.roll(v, 1, 1), v, pltpu.roll(v, 127, 1))):
                    for r in range(3):
                        sums[r] = sums[r] + whole[r * 3 + c, cz * 9 + cy * 3 + cx] * moved
    for r in range(3):
        out(r, sums[r])


def step_kernel(first, rho_now, rho_next, last, *refs):
    whole, q, d, inverse, received = refs[:5]
    refs = refs[5:]
    if first:
        x = None
    else:
        x, refs = refs[0], refs[1:]
    if last:
        solution_out, near, turned = refs
    else:
        q_out, d_out, x_out, piece, near = refs

    def update(r, product):
        now = d[r, 2:18] if first else d[r]
        x_now = now if x is None else x[r] + now
        q_now = q[r] - product
        d_new = rho_next * rho_now * now + 2.0 * rho_next / HALF * (inverse[r] * q_now)
        if last:
            turned[...] = x_now + d_new
            for z in range(2):
                solution_out[r, z] = turned[pl.ds(4 + z, 4, stride=2), :][:, 0:64]
        else:
            x_out[r] = x_now
            q_out[r] = q_now
            d_out[r] = d_new

    apply_to(whole, d, received, 24 if first else 16, near, update)
    if not last:
        share_planes(lambda c: d_out[c], 16, piece)


def shape(*dims):
    return jax.ShapeDtypeStruct(dims, jnp.float32)


def along(block, axes, distances):
    sizes = [lax.axis_size(a) for a in axes]
    route = []
    for source in itertools.product(*[range(n) for n in sizes]):
        target = [i + s for i, s in zip(source, distances)]
        if all(0 <= i < n for i, n in zip(target, sizes)):
            flat = [functools.reduce(lambda t, p: t * p[1] + p[0], zip(at, sizes), 0) for at in (source, target)]
            route.append(tuple(flat))
    return lax.ppermute(block, axes, route)


def shards(blocks, classes, residual):
    nz = lax.axis_size("gz")
    w_shape, wl_shape = shape(9, ITEMS, 8, 128), shape(6, 8, 128)
    side = shape(10, 8, 128)
    w, wl, right, left, plane, plane_right, plane_left_sent = pl.pallas_call(
        coarsen_kernel,
        in_specs=[HBM] * 3,
        out_specs=[VMEM] * 7,
        out_shape=[w_shape, wl_shape, side, side, shape(9 * plane_size(PLANE) + plane_size(3), 8, 128), side, side],
        scratch_shapes=[
            pltpu.VMEM((9, 3, 3, 3, 4, 8, 128), jnp.float32),
            pltpu.VMEM((4, 8, 128), jnp.int32),
            pltpu.VMEM((3, 4, 8, 128), jnp.float32),
            pltpu.VMEM((4, 5, 8, 128), jnp.float32),
            pltpu.SemaphoreType.DMA((11,)),
        ],
        compiler_params=LIMIT,
    )(*(pltpu.with_memory_space_constraint(v, pltpu.HBM) for v in (blocks, classes, residual)))
    plane = along(plane, ("gz",), (1,))
    from_left, from_right = along(right, ("gx",), (1,)), along(left, ("gx",), (-1,))
    plane_left = along(plane_right, ("gx", "gz"), (1, 1))
    plane_right = along(plane_left_sent, ("gx", "gz"), (-1, 1))
    w, wl, up, down = pl.pallas_call(
        planes_kernel,
        in_specs=[VMEM] * 7,
        out_specs=[VMEM] * 4,
        out_shape=[w_shape, wl_shape, shape(9 * packed_size(UPS) + packed_size(3), 8, 128), shape(9 * packed_size(DOWNS) + packed_size(3), 8, 128)],
        scratch_shapes=[pltpu.VMEM((3, 8, 128), jnp.float32)],
        compiler_params=LIMIT,
    )(w, wl, from_left, from_right, plane, plane_left, plane_right)
    from_low, from_high = along(up, ("gy",), (1,)), along(down, ("gy",), (-1,))
    operator, whole, q, d, inverse, piece = pl.pallas_call(
        rows_kernel,
        in_specs=[VMEM] * 4,
        out_specs=[VMEM] * 6,
        out_shape=[
            shape(3, 3, 3, 3, 3, 2, 4, 64),
            shape(9, 27, 16, 128),
            shape(3, 16, 128),
            shape(3, 24, 128),
            shape(3, 16, 128),
            shape(nz, piece_rows(24), 128),
        ],
        scratch_shapes=[pltpu.VMEM((3, 16, 128), jnp.float32), pltpu.VMEM((8, 128), jnp.float32)],
        compiler_params=LIMIT,
    )(w, wl, from_low, from_high)
    x = []
    rho_now = 1.0 / SIGMA
    for step in range(STEPS - 1):
        rho_next = 1.0 / (2.0 * SIGMA - rho_now)
        last = step == STEPS - 2
        shared = lax.all_to_all(piece, "gz", 0, 0)
        if last:
            outs = shape(3, 2, 4, 64)
        else:
            outs = [shape(3, 16, 128), shape(3, 16, 128), shape(3, 16, 128), shape(nz, piece_rows(16), 128)]
        done = pl.pallas_call(
            functools.partial(step_kernel, step == 0, rho_now, rho_next, last),
            in_specs=[VMEM] * (5 + len(x)),
            out_specs=VMEM if last else [VMEM] * 4,
            out_shape=outs,
            scratch_shapes=[pltpu.VMEM((3, 3, 24, 128), jnp.float32)] + ([pltpu.VMEM((16, 128), jnp.float32)] if last else []),
            compiler_params=LIMIT,
        )(whole, q, d, inverse, shared, *x)
        if last:
            return operator, done
        q, d, x, piece = done
        x = [x]
        rho_now = rho_next


def solution(mesh):
    placed = (
        P(None, None, None, None, None, "gz", "gy", "gx"),
        P("gz", "gy", "gx"),
        P(None, "gz", "gy", "gx"),
    )
    return jax.shard_map(
        shards,
        mesh=mesh,
        in_specs=placed,
        out_specs=(P(None, None, None, None, None, "gz", "gy", "gx"), P(None, "gz", "gy", "gx")),
        check_vma=False,
    )
```

```python
import functools
import itertools

import jax
import jax.numpy as jnp
from jax import lax
from jax.experimental import pallas as pl
from jax.experimental.pallas import tpu as pltpu
from jax.sharding import PartitionSpec as P

STEPS = 4
CHEB_LOW = 0.1
CHEB_HIGH = 1.0
CENTRE = (CHEB_HIGH + CHEB_LOW) / 2.0
HALF = (CHEB_HIGH - CHEB_LOW) / 2.0
SIGMA = CENTRE / HALF

ITEMS = 32
PLANE = 11
UPS, DOWNS = 18, 14
AHEAD = 3
VMEM = pl.BlockSpec(memory_space=pltpu.VMEM)
HBM = pl.BlockSpec(memory_space=pltpu.HBM)
LIMIT = pltpu.CompilerParams(vmem_limit_bytes=40 * 1024 * 1024)


def lanes_of():
    return lax.broadcasted_iota(jnp.int32, (8, 128), 1)


def rows_of():
    return lax.broadcasted_iota(jnp.int32, (8, 128), 0)


def lroll(v, s):
    s = s % 128
    return v if s == 0 else pltpu.roll(v, s, 1)


def sroll(v, s):
    s = s % 8
    return v if s == 0 else pltpu.roll(v, s, 0)


def slot_mask(lane, j):
    right = jnp.logical_and(lane >= 3 * j, lane < 3 * j + 3)
    left = jnp.logical_and(lane >= 3 * j + 61, lane < 3 * j + 64)
    return jnp.logical_or(right, left)


def packed_size(n):
    return (n + 1) // 2 + (n + 19) // 20


def pack(vs):
    lane = lanes_of()
    out = []
    for i in range(0, len(vs), 2):
        other = lroll(vs[i + 1], 64) if i + 1 < len(vs) else jnp.zeros_like(vs[i])
        out.append(jnp.where(lane < 64, vs[i], other))
    for base in range(0, len(vs), 20):
        held = jnp.zeros((8, 128), jnp.float32)
        for j, v in enumerate(vs[base : base + 20]):
            held = jnp.where(slot_mask(lane, j), lroll(v, 3 * j - 64), held)
        out.append(held)
    return out


def unpack(load, n):
    lane = lanes_of()
    edge = jnp.logical_or(jnp.logical_and(lane >= 64, lane < 67), lane >= 125)
    mains = (n + 1) // 2
    out = []
    for i in range(n):
        main = load(i // 2)
        if i % 2:
            main = lroll(main, 64)
        held = lroll(load(mains + i // 20), 64 - 3 * (i % 20))
        out.append(jnp.where(lane < 64, main, jnp.where(edge, held, 0.0)))
    return out


def right_slot(lane, j):
    return lane // 4 == j


def left_slot(lane, j):
    at = (lane - (4 * j + 67)) % 128
    return at < 3


def pack_sides(vs):
    lane = lanes_of()
    right = jnp.zeros((8, 128), jnp.float32)
    left = jnp.zeros((8, 128), jnp.float32)
    for j, v in enumerate(vs):
        moved = lroll(v, 4 * j - 61)
        right = jnp.where(right_slot(lane, j), moved, right)
        left = jnp.where(left_slot(lane, j), moved, left)
    return right, left


def sides(from_left, from_right, j):
    lane = lanes_of()
    both = lroll(jnp.where(right_slot(lane, j), from_left, from_right), -(4 * j + 3))
    ends = jnp.logical_or(jnp.logical_or(lane >= 125, lane == 0), jnp.logical_and(lane >= 64, lane < 67))
    return jnp.where(ends, both, 0.0)


def plane_size(n):
    return n // 2 + 1


def pack_plane(vs):
    lane = lanes_of()
    out = [jnp.where(lane < 64, vs[i], lroll(vs[i + 1], 64)) for i in range(0, len(vs) - 1, 2)]
    last = jnp.where(lane < 64, vs[-1], 0.0)
    for i, v in enumerate(vs):
        last = jnp.where(lane == 64 + i, lroll(v, i), last)
    return out + [last]


def unpack_plane(load, n, from_left, from_right):
    lane = lanes_of()
    last = load(n // 2)
    out = []
    for i in range(n):
        main = load(i // 2)
        if i % 2:
            main = lroll(main, 64)
        main = jnp.where(lane < 64, main, jnp.where(lane == 64, lroll(last, -i), 0.0))
        out.append(main + sides(from_left, from_right, i))
    return out


def coarsen_kernel(blocks_in, classes_in, residual_in, w, wl, right, left, plane, plane_right, plane_left, blocks, classes, residual, scale, sems):
    def fetch(i):
        source = blocks_in.at[:, :, :, i // 3, i % 3]
        return pltpu.make_async_copy(source, blocks.at[i], sems.at[i])

    classes_copy = pltpu.make_async_copy(classes_in, classes, sems.at[9])
    residual_copy = pltpu.make_async_copy(residual_in, residual, sems.at[10])
    classes_copy.start()
    fetch(0).start()
    residual_copy.start()
    for i in range(1, AHEAD):
        fetch(i).start()
    gx, gy, gz = (lax.axis_index(a) for a in ("gx", "gy", "gz"))
    lane, row = lanes_of(), rows_of()
    even = row % 2 == 0
    not_last_x = (gx < lax.axis_size("gx") - 1).astype(jnp.float32)
    last_x = gx == lax.axis_size("gx") - 1
    not_last_y = (gy < lax.axis_size("gy") - 1).astype(jnp.float32)
    keep_y = jnp.logical_or(row < 6, gy < lax.axis_size("gy") - 1)
    inner = lane < 64
    upper_x = jnp.logical_and(inner, jnp.logical_or(lane < 63, jnp.logical_not(last_x)))
    after_x = jnp.logical_and(lane > 0, jnp.logical_or(inner, jnp.logical_and(lane == 64, jnp.logical_not(last_x))))
    apart = jnp.where(inner, 2 * lane, 2 * lane - 127)
    not_last_z = (gz < lax.axis_size("gz") - 1).astype(jnp.float32)
    pick = jnp.where(lane < 64, 2 * lane, 127) % 128

    def squeeze(v):
        g = jnp.take_along_axis(v, pick, axis=1, mode="promise_in_bounds")
        return jnp.where(lane <= 64, g, 0.0)

    def coarsen(step):
        ydone = {}
        for ox in range(3):
            slots = {}
            for oy in range(3):
                kind = (2 if oy == 0 else 0) + (1 if ox == 0 else 0)
                s = [[None] * 4 for _ in range(3)]
                for oz in range(3):
                    for z in range(4):
                        factor = scale[kind, 5 + z if oz == 1 else 4 if (z == 0 and oz == 0) else z]
                        s[oz][z] = blocks[step, oz, oy, ox, z] * factor
                a1, b1 = s[0][1] + s[1][1], s[2][1] + s[1][1]
                a3, b3 = s[0][3] + s[1][3], s[2][3] + s[1][3]
                slots[0, 0, oy] = s[0][0]
                slots[1, 0, oy] = s[0][0] + s[2][0] + s[1][0] + a1
                slots[2, 0, oy] = s[2][0] + b1
                slots[0, 1, oy] = s[0][2] + a1
                slots[1, 1, oy] = s[0][2] + s[2][2] + s[1][2] + b1 + a3
                slots[2, 1, oy] = (s[2][2] + b3) * not_last_z
                slots[3, 0, oy] = a3
                slots[3, 1, oy] = b3
            beyond = [None, None]
            for slot in range(4):
                ev, od = [], []
                for oy in range(3):
                    z0, z1 = slots[slot, 0, oy], slots[slot, 1, oy]
                    ev.append(jnp.where(even, z0, sroll(z1, 1)))
                    od.append(jnp.where(even, sroll(z0, -1), z1))
                half = 0.5 * od[1]
                a, b = od[0] + half, od[2] + half
                a_before, b_before = sroll(a, 2), sroll(b, 2)
                ydone[slot * 3, ox] = ev[0] + jnp.where(row < 2, 0.0, a_before)
                ydone[slot * 3 + 1, ox] = ev[0] + ev[2] + (ev[1] + ev[1]) + a + jnp.where(row < 2, 0.0, b_before)
                ydone[slot * 3 + 2, ox] = jnp.where(keep_y, ev[2] + b, 0.0)
                if slot % 2 == 0:
                    beyond[slot // 2] = jnp.where(row < 2, a_before, sroll(b, 4))
                else:
                    ends = jnp.where(row < 6, sroll(a, 6), b)
                    beyond[slot // 2] = jnp.where(row < 4, beyond[slot // 2], ends) * not_last_y
            ydone[12, ox], ydone[13, ox] = beyond
        kept, sent, rows = [None] * ITEMS, [None] * PLANE, {}
        for i in range(14):
            v = [jnp.take_along_axis(ydone[i, ox], apart, axis=1, mode="promise_in_bounds") for ox in range(3)]
            half = 0.5 * v[1]
            a, b = v[0] + half, v[2] + half
            lower = jnp.where(inner, v[0], 0.0) + jnp.where(after_x, lroll(a, 65), 0.0)
            middle = jnp.where(inner, v[0] + v[2] + (v[1] + v[1]) + lroll(a, 64), 0.0) + jnp.where(after_x, lroll(b, 65), 0.0)
            upper = jnp.where(upper_x, v[2] + lroll(b, 64), 0.0)
            for cx, v in enumerate((lower, middle, upper)):
                if i < 9:
                    kept[i * 3 + cx] = v
                elif i < 12:
                    sent[(i - 9) * 3 + cx] = v
                elif i == 12:
                    kept[27 + cx] = v
                else:
                    rows[cx] = v
        kept[30] = jnp.where(row < 4, rows[0], sroll(rows[1], 4))
        sent[9] = jnp.where(row < 4, sroll(rows[0], 4), rows[1])
        kept[31] = sent[10] = rows[2]
        for i, v in enumerate(kept):
            w[step, i] = v
        right[step], left[step] = pack_sides(kept)
        plane_right[step], plane_left[step] = pack_sides(sent)
        for i, v in enumerate(pack_plane(sent)):
            plane[step * plane_size(PLANE) + i] = v

    def scales():
        low_x = jnp.where(jnp.logical_and(lane == 0, gx == 0), 0.0, 1.0)
        low_y = jnp.where(jnp.logical_and(row == 0, gy == 0), 0.0, 1.0)
        low_z = (gz > 0).astype(jnp.float32)
        for z in range(4):
            k = classes[z].astype(jnp.float32)
            s = 0.125 * (0.05 + 0.95 * (k * k * k) / 27.0)
            for cy in range(2):
                for cx in range(2):
                    v = s
                    if cy:
                        v = v * low_y
                    if cx:
                        v = v * low_x
                    scale[cy * 2 + cx, z] = v
                    scale[cy * 2 + cx, 5 + z] = (0.5 if z % 2 else 2.0) * v
                    if z == 0:
                        scale[cy * 2 + cx, 4] = v * low_z

    def loads():
        items = []
        for c in range(3):
            f = [residual[c, z] for z in range(4)]
            planes = [f[0] + 0.5 * f[1], 0.5 * f[1] + f[2] + 0.5 * f[3], 0.5 * f[3]]
            full, beyond = [], []
            for v in planes:
                h = 0.5 * v
                before = sroll(h, 1)
                full.append(v + sroll(h, -1) + jnp.where(row == 0, 0.0, before))
                beyond.append(h * not_last_y)
            main = jnp.where(even, full[0], sroll(full[1], 1))
            ghost = jnp.where(even, full[2], 0.0)
            for z in range(3):
                ghost = jnp.where(row == 1 + 2 * z, sroll(beyond[z], 2 + 2 * z), ghost)
            items.append((main, ghost))
        vs = []
        for v in [m for m, _ in items] + [g for _, g in items]:
            h = 0.5 * v
            v = v + lroll(h, -1) + jnp.where(lane == 0, 0.0, lroll(h, 1))
            v = jnp.where(lane == 127, h * not_last_x, v)
            vs.append(squeeze(v))
        for i, v in enumerate(vs):
            wl[i] = v

        right[9], left[9] = pack_sides(vs)
        plane_right[9], plane_left[9] = pack_sides(vs[3:])
        for i, v in enumerate(pack_plane(vs[3:])):
            plane[9 * plane_size(PLANE) + i] = v

    classes_copy.wait()
    scales()
    residual_copy.wait()
    loads()

    def body(step, carry):
        fetch(step).wait()

        @pl.when(step + AHEAD < 9)
        def _():
            fetch(step + AHEAD).start()

        coarsen(step)
        return carry

    lax.fori_loop(0, 9, body, 0, unroll=9)


def planes_kernel(plane_left, from_left, plane_right, from_right, plane, w, wl, w_out, wl_out, up, down, total):
    row = rows_of()
    even = row % 2 == 0
    total[...] = jnp.zeros_like(total)

    def body(rc, carry):
        got = unpack_plane(lambda i: plane[rc * plane_size(PLANE) + i], PLANE, plane_left[rc], plane_right[rc])
        from_l, from_r = from_left[rc], from_right[rc]
        f = [None] * ITEMS
        for k in range(ITEMS):
            v = w[rc, k] + sides(from_l, from_r, k)
            if k < 9:
                v = v + jnp.where(even, got[k], 0.0)
            elif k < 18:
                v = v + jnp.where(even, sroll(got[k - 9], -1), 0.0)
            elif 27 <= k < 30:
                end = (sroll(got[9], 4), got[9], got[10])[k - 27]
                v = v + jnp.where(even, jnp.where(row < 4, sroll(end, 4), sroll(end, -1)), 0.0)
            f[k] = v
            w_out[rc, k] = v
        magnitude = jnp.abs(f[0])
        for k in range(1, 27):
            magnitude = magnitude + jnp.abs(f[k])
        total[rc // 3] += magnitude
        ups, downs = [], []
        for k in range(0, 27, 2):
            two = f[k + 1] if k + 1 < 27 else None
            ups.append(jnp.where(row < 4, sroll(f[k], 4), sroll(f[31], 4) if two is None else two))
            downs.append(jnp.where(row < 4, f[k], 0.0 if two is None else sroll(two, 4)))
        ups += f[27:31]
        for ref, vs in ((up, ups), (down, downs)):
            for i, v in enumerate(pack(vs)):
                ref[rc * packed_size(len(vs)) + i] = v
        return carry

    lax.fori_loop(0, 9, body, 0, unroll=9)
    got = unpack_plane(lambda i: plane[9 * plane_size(PLANE) + i], 3, plane_left[9], plane_right[9])
    ups, downs = [], []
    for c in range(3):
        load = wl[c] + sides(from_left[9], from_right[9], c) + jnp.where(even, got[c], 0.0)
        ghost = wl[3 + c] + jnp.where(row == 1, sroll(got[c], -4), 0.0)
        ghost = ghost + sides(from_left[9], from_right[9], 3 + c)
        wl_out[c] = load
        wl_out[3 + c] = ghost
        d = load * (1.0 / (total[c] + 1e-06)) / CENTRE
        v = jnp.where(row < 4, sroll(load, 4), 0.0)
        v = jnp.where(row == 4, sroll(ghost, 3), v)
        v = jnp.where(row == 5, sroll(ghost, 2), v)
        ups.append(jnp.where(row >= 6, sroll(d, 4), v))
        downs.append(jnp.where(row < 4, load, jnp.where(row >= 6, sroll(d, 2), 0.0)))
    for ref, vs, size in ((up, ups, packed_size(UPS)), (down, downs, packed_size(DOWNS))):
        for i, v in enumerate(pack(vs)):
            ref[9 * size + i] = v


def piece_rows(n):
    return n + 8 * ((n + 15) // 16)


def share_planes(load, n, to_other, to_pair):
    low_of_pair = lax.axis_index("gz") % 2 == 0
    even = lax.broadcasted_iota(jnp.int32, (n, 128), 0) % 2 == 0
    d = [load(c) for c in range(3)]
    sent = []
    for z in range(2):
        if z == 0:
            both = jnp.where(even, d[0], pltpu.roll(d[1], 1, 0))
            third = d[2]
        else:
            both = jnp.where(even, pltpu.roll(d[0], n - 1, 0), d[1])
            third = pltpu.roll(d[2], n - 1, 0)
        folds = []
        for at in range(0, n, 16):
            fold = third[at : at + 8]
            if at + 8 < n:
                fold = jnp.where(even[0:8], fold, sroll(third[at + 8 : at + 16], 1))
            folds.append(fold)
        sent.append(jnp.concatenate([both] + folds, axis=0))
    to_pair[...] = jnp.where(low_of_pair, sent[1], sent[0])
    to_other[...] = jnp.where(low_of_pair, sent[0], sent[1])


def plane_of(piece, n, c):
    if c < 2:
        return piece[0:n], c
    parts = []
    for i in range(0, n, 16):
        fold = piece[n + i // 2 : n + i // 2 + 8]
        parts.append(fold)
        if i + 8 < n:
            parts.append(sroll(fold, -1))
    return jnp.concatenate(parts, axis=0), 0


def rows_kernel(w, wl, from_low, from_high, whole, q, d, inverse, to_other, to_pair, total, turned):
    row = rows_of()
    ghosts = jnp.logical_or(row == 4, row == 5)
    total[...] = jnp.zeros_like(total)

    def body(rc, carry):
        ups = unpack(lambda i: from_low[rc * packed_size(UPS) + i], UPS)
        downs = unpack(lambda i: from_high[rc * packed_size(DOWNS) + i], DOWNS)
        got_ends = [ups[17], sroll(ups[17], 4), sroll(ups[13], 4)]
        own_ends = [w[rc, 30], sroll(w[rc, 30], 4), w[rc, 31]]
        top_sum = jnp.zeros((8, 128), jnp.float32)
        bottom_sum = jnp.zeros((8, 128), jnp.float32)
        for cz in range(3):
            for cy in range(3):
                for cx in range(3):
                    k = cz * 9 + cy * 3 + cx
                    f = sroll(w[rc, k], 4)
                    above, below = ups[k // 2], downs[k // 2]
                    top = jnp.where(row < 4, sroll(above, 4) if k % 2 else above, f)
                    bottom = jnp.where(row < 4, f, below if k % 2 else sroll(below, 4))
                    if cy < 2:
                        at = (cz % 2) * 4 + cy * 2
                        got = ups[14 + cx] if cz < 2 else got_ends[cx]
                        own = w[rc, 27 + cx] if cz < 2 else own_ends[cx]
                        top = top + jnp.where(ghosts, sroll(got, 4 - at), 0.0)
                        bottom = bottom + jnp.where(ghosts, sroll(own, 4 - at), 0.0)
                    whole[rc, k, 0:8] = top
                    whole[rc, k, 8:16] = bottom
                    top_sum = top_sum + jnp.abs(top)
                    bottom_sum = bottom_sum + jnp.abs(bottom)
        total[rc // 3, 0:8] += top_sum
        total[rc // 3, 8:16] += bottom_sum
        return carry

    lax.fori_loop(0, 9, body, 0, unroll=9)
    ups = unpack(lambda i: from_low[9 * packed_size(UPS) + i], 3)
    downs = unpack(lambda i: from_high[9 * packed_size(DOWNS) + i], 3)
    for c in range(3):
        load, ghost = sroll(wl[c], 4), wl[3 + c]
        q[c, 0:8] = jnp.where(row < 4, ups[c], load + jnp.where(ghosts, ups[c], 0.0))
        below = sroll(downs[c], 4)
        below = below + jnp.where(row == 4, sroll(ghost, 3), jnp.where(row == 5, sroll(ghost, 2), 0.0))
        q[c, 8:16] = jnp.where(row < 4, load, below)
        part = 1.0 / (total[c] + 1e-06)
        inverse[c] = part
        d[c, 16:24] = jnp.zeros((8, 128), jnp.float32)
        d[c, 2:18] = part * q[c] / CENTRE
        turned[...] = ups[c]
        d[c, 0:2] = turned[6:8]
        turned[...] = downs[c]
        d[c, 18:20] = turned[6:8]
    share_planes(lambda c: d[c], 24, to_other, to_pair)


def operator_kernel(whole, operator):
    def body(rc, carry):
        for k in range(27):
            for z in range(2):
                v = whole[rc, k, pl.ds(4 + z, 4, stride=2), :]
                operator[k // 9, k // 3 % 3, k % 3, rc // 3, rc % 3, z] = v[:, 0:64]
        return carry

    lax.fori_loop(0, 9, body, 0, unroll=3)


def apply_to(whole, d, from_other, from_pair, n, near, out):
    low_of_pair = lax.axis_index("gz") % 2 == 0
    even = lax.broadcasted_iota(jnp.int32, (n, 128), 0) % 2 == 0
    other, pair = from_other[...], from_pair[...]
    below = jnp.where(low_of_pair, other, pair)
    above = jnp.where(low_of_pair, pair, other)
    base = (24 - n) // 4
    for c in range(3):
        own = d[c]
        low, odd = plane_of(below, n, c)
        high, _ = plane_of(above, n, c)
        if odd:
            low = pltpu.roll(low, n - 1, 0)
        else:
            high = pltpu.roll(high, 1, 0)
        for cz, v in enumerate((
            jnp.where(even, low, pltpu.roll(own, 1, 0)),
            own,
            jnp.where(even, pltpu.roll(own, n - 1, 0), high),
        )):
            if base:
                near[cz, c, 0:8] = jnp.zeros((8, 128), jnp.float32)
                near[cz, c, 16:24] = jnp.zeros((8, 128), jnp.float32)
            near[cz, c, base : base + n] = v
    sums = [jnp.zeros((16, 128), jnp.float32) for _ in range(3)]
    for cz in range(3):
        for cy in range(3):
            for c in range(3):
                v = near[cz, c, pl.ds(2 * cy, 16), :]
                for cx, moved in enumerate((pltpu.roll(v, 1, 1), v, pltpu.roll(v, 127, 1))):
                    for r in range(3):
                        sums[r] = sums[r] + whole[r * 3 + c, cz * 9 + cy * 3 + cx] * moved
    for r in range(3):
        out(r, sums[r])


def step_kernel(first, rho_now, rho_next, last, *refs):
    whole, q, d, inverse, from_other, from_pair = refs[:6]
    refs = refs[6:]
    if first:
        x = None
    else:
        x, refs = refs[0], refs[1:]
    if last:
        solution_out, near, turned = refs
    else:
        q_out, d_out, x_out, to_other, to_pair, near = refs

    def update(r, product):
        now = d[r, 2:18] if first else d[r]
        x_now = now if x is None else x[r] + now
        q_now = q[r] - product
        d_new = rho_next * rho_now * now + 2.0 * rho_next / HALF * (inverse[r] * q_now)
        if last:
            turned[...] = x_now + d_new
            for z in range(2):
                solution_out[r, z] = turned[pl.ds(4 + z, 4, stride=2), :][:, 0:64]
        else:
            x_out[r] = x_now
            q_out[r] = q_now
            d_out[r] = d_new

    apply_to(whole, d, from_other, from_pair, 24 if first else 16, near, update)
    if not last:
        share_planes(lambda c: d_out[c], 16, to_other, to_pair)


def shape(*dims):
    return jax.ShapeDtypeStruct(dims, jnp.float32)


def along(block, axes, distances):
    sizes = [lax.axis_size(a) for a in axes]
    route = []
    for source in itertools.product(*[range(n) for n in sizes]):
        target = [i + s for i, s in zip(source, distances)]
        if all(0 <= i < n for i, n in zip(target, sizes)):
            flat = [functools.reduce(lambda t, p: t * p[1] + p[0], zip(at, sizes), 0) for at in (source, target)]
            route.append(tuple(flat))
    return lax.ppermute(block, axes, route)


def exchanged(block, axis, first):
    n = lax.axis_size(axis)
    pairs = [(i, i + 1) for i in range(first, n - 1, 2)]
    return lax.ppermute(block, axis, pairs + [(j, i) for i, j in pairs])


def shards(blocks, classes, residual):
    w_shape, wl_shape = shape(9, ITEMS, 8, 128), shape(6, 8, 128)
    side = shape(10, 8, 128)
    w, wl, right, left, plane, plane_right, plane_left_sent = pl.pallas_call(
        coarsen_kernel,
        in_specs=[HBM] * 3,
        out_specs=[VMEM] * 7,
        out_shape=[w_shape, wl_shape, side, side, shape(9 * plane_size(PLANE) + plane_size(3), 8, 128), side, side],
        scratch_shapes=[
            pltpu.VMEM((9, 3, 3, 3, 4, 8, 128), jnp.float32),
            pltpu.VMEM((4, 8, 128), jnp.int32),
            pltpu.VMEM((3, 4, 8, 128), jnp.float32),
            pltpu.VMEM((4, 9, 8, 128), jnp.float32),
            pltpu.SemaphoreType.DMA((11,)),
        ],
        compiler_params=LIMIT,
    )(*(pltpu.with_memory_space_constraint(v, pltpu.HBM) for v in (blocks, classes, residual)))
    plane_left = along(plane_right, ("gx", "gz"), (1, 1))
    from_left = along(right, ("gx",), (1,))
    plane_right = along(plane_left_sent, ("gx", "gz"), (-1, 1))
    from_right = along(left, ("gx",), (-1,))
    plane = along(plane, ("gz",), (1,))
    w, wl, up, down = pl.pallas_call(
        planes_kernel,
        in_specs=[VMEM] * 7,
        out_specs=[VMEM] * 4,
        out_shape=[w_shape, wl_shape, shape(9 * packed_size(UPS) + packed_size(3), 8, 128), shape(9 * packed_size(DOWNS) + packed_size(3), 8, 128)],
        scratch_shapes=[pltpu.VMEM((3, 8, 128), jnp.float32)],
        compiler_params=LIMIT,
    )(plane_left, from_left, plane_right, from_right, plane, w, wl)
    from_high = along(down, ("gy",), (-1,))
    from_low = along(up, ("gy",), (1,))
    whole_shape, vector = shape(9, 27, 16, 128), shape(3, 16, 128)
    whole, q, d, inverse, to_other, to_pair = pl.pallas_call(
        rows_kernel,
        in_specs=[VMEM] * 4,
        out_specs=[VMEM] * 6,
        out_shape=[whole_shape, vector, shape(3, 24, 128), vector] + [shape(piece_rows(24), 128)] * 2,
        scratch_shapes=[pltpu.VMEM((3, 16, 128), jnp.float32), pltpu.VMEM((8, 128), jnp.float32)],
        compiler_params=LIMIT,
    )(w, wl, from_low, from_high)
    operator = pl.pallas_call(
        operator_kernel,
        in_specs=[VMEM],
        out_specs=VMEM,
        out_shape=shape(3, 3, 3, 3, 3, 2, 4, 64),
        compiler_params=LIMIT,
        cost_estimate=pl.CostEstimate(flops=500000, bytes_accessed=3000000, transcendentals=0),
    )(whole)
    x = []
    rho_now = 1.0 / SIGMA
    for step in range(STEPS - 1):
        rho_next = 1.0 / (2.0 * SIGMA - rho_now)
        last = step == STEPS - 2
        from_other, from_pair = exchanged(to_other, "gz", 1), exchanged(to_pair, "gz", 0)
        if last:
            outs = shape(3, 2, 4, 64)
        else:
            outs = [vector] * 3 + [shape(piece_rows(16), 128)] * 2
        done = pl.pallas_call(
            functools.partial(step_kernel, step == 0, rho_now, rho_next, last),
            in_specs=[VMEM] * (6 + len(x)),
            out_specs=VMEM if last else [VMEM] * 5,
            out_shape=outs,
            scratch_shapes=[pltpu.VMEM((3, 3, 24, 128), jnp.float32)] + ([pltpu.VMEM((16, 128), jnp.float32)] if last else []),
            compiler_params=LIMIT,
        )(whole, q, d, inverse, from_other, from_pair, *x)
        if last:
            return operator, done
        q, d, x, to_other, to_pair = done
        x = [x]
        rho_now = rho_next


def solution(mesh):
    placed = (
        P(None, None, None, None, None, "gz", "gy", "gx"),
        P("gz", "gy", "gx"),
        P(None, "gz", "gy", "gx"),
    )
    return jax.shard_map(
        shards,
        mesh=mesh,
        in_specs=placed,
        out_specs=(P(None, None, None, None, None, "gz", "gy", "gx"), P(None, "gz", "gy", "gx")),
        check_vma=False,
    )
```

```python
import functools
import itertools

import jax
import jax.numpy as jnp
from jax import lax
from jax.experimental import pallas as pl
from jax.experimental.pallas import tpu as pltpu
from jax.sharding import PartitionSpec as P

STEPS = 4
CHEB_LOW = 0.1
CHEB_HIGH = 1.0
CENTRE = (CHEB_HIGH + CHEB_LOW) / 2.0
HALF = (CHEB_HIGH - CHEB_LOW) / 2.0
SIGMA = CENTRE / HALF

ITEMS = 32
PLANE = 11
UPS, DOWNS = 18, 14
AHEAD = 3
EDGES = 8 * 48
VMEM = pl.BlockSpec(memory_space=pltpu.VMEM)
HBM = pl.BlockSpec(memory_space=pltpu.HBM)
LIMIT = pltpu.CompilerParams(vmem_limit_bytes=40 * 1024 * 1024)


def lanes_of():
    return lax.broadcasted_iota(jnp.int32, (8, 128), 1)


def rows_of():
    return lax.broadcasted_iota(jnp.int32, (8, 128), 0)


def lroll(v, s):
    s = s % 128
    return v if s == 0 else pltpu.roll(v, s, 1)


def sroll(v, s):
    s = s % 8
    return v if s == 0 else pltpu.roll(v, s, 0)


def slot_mask(lane, j):
    right = jnp.logical_and(lane >= 3 * j, lane < 3 * j + 3)
    left = jnp.logical_and(lane >= 3 * j + 61, lane < 3 * j + 64)
    return jnp.logical_or(right, left)


def packed_size(n):
    return (n + 1) // 2 + (n + 19) // 20


def pack(vs):
    lane = lanes_of()
    out = []
    for i in range(0, len(vs), 2):
        other = lroll(vs[i + 1], 64) if i + 1 < len(vs) else jnp.zeros_like(vs[i])
        out.append(jnp.where(lane < 64, vs[i], other))
    for base in range(0, len(vs), 20):
        held = jnp.zeros((8, 128), jnp.float32)
        for j, v in enumerate(vs[base : base + 20]):
            held = jnp.where(slot_mask(lane, j), lroll(v, 3 * j - 64), held)
        out.append(held)
    return out


def unpack(load, n):
    lane = lanes_of()
    edge = jnp.logical_or(jnp.logical_and(lane >= 64, lane < 67), lane >= 125)
    mains = (n + 1) // 2
    out = []
    for i in range(n):
        main = load(i // 2)
        if i % 2:
            main = lroll(main, 64)
        held = lroll(load(mains + i // 20), 64 - 3 * (i % 20))
        out.append(jnp.where(lane < 64, main, jnp.where(edge, held, 0.0)))
    return out


def right_slot(lane, j):
    return lane // 4 == j


def left_slot(lane, j):
    at = (lane - (4 * j + 67)) % 128
    return at < 3


def pack_sides(vs):
    lane = lanes_of()
    right = jnp.zeros((8, 128), jnp.float32)
    left = jnp.zeros((8, 128), jnp.float32)
    for j, v in enumerate(vs):
        moved = lroll(v, 4 * j - 61)
        right = jnp.where(right_slot(lane, j), moved, right)
        left = jnp.where(left_slot(lane, j), moved, left)
    return right, left


def sides(from_left, from_right, j):
    lane = lanes_of()
    both = lroll(jnp.where(right_slot(lane, j), from_left, from_right), -(4 * j + 3))
    ends = jnp.logical_or(jnp.logical_or(lane >= 125, lane == 0), jnp.logical_and(lane >= 64, lane < 67))
    return jnp.where(ends, both, 0.0)


def plane_size(n):
    return n // 2 + 1


def pack_plane(vs):
    lane = lanes_of()
    out = [jnp.where(lane < 64, vs[i], lroll(vs[i + 1], 64)) for i in range(0, len(vs) - 1, 2)]
    last = jnp.where(lane < 64, vs[-1], 0.0)
    for i, v in enumerate(vs):
        last = jnp.where(lane == 64 + i, lroll(v, i), last)
    return out + [last]


def unpack_plane(load, n, from_left, from_right):
    lane = lanes_of()
    last = load(n // 2)
    out = []
    for i in range(n):
        main = load(i // 2)
        if i % 2:
            main = lroll(main, 64)
        main = jnp.where(lane < 64, main, jnp.where(lane == 64, lroll(last, -i), 0.0))
        out.append(main + sides(from_left, from_right, i))
    return out


def coarsen_kernel(blocks_in, classes_in, residual_in, w, wl, right, left, plane, plane_right, plane_left, blocks, classes, residual, scale, sems):
    def fetch(i):
        source = blocks_in.at[:, :, :, i // 3, i % 3]
        return pltpu.make_async_copy(source, blocks.at[i], sems.at[i])

    classes_copy = pltpu.make_async_copy(classes_in, classes, sems.at[9])
    residual_copy = pltpu.make_async_copy(residual_in, residual, sems.at[10])
    classes_copy.start()
    fetch(0).start()
    residual_copy.start()
    for i in range(1, AHEAD):
        fetch(i).start()
    gx, gy, gz = (lax.axis_index(a) for a in ("gx", "gy", "gz"))
    lane, row = lanes_of(), rows_of()
    even = row % 2 == 0
    not_last_x = (gx < lax.axis_size("gx") - 1).astype(jnp.float32)
    last_x = gx == lax.axis_size("gx") - 1
    not_last_y = (gy < lax.axis_size("gy") - 1).astype(jnp.float32)
    keep_y = jnp.logical_or(row < 6, gy < lax.axis_size("gy") - 1)
    inner = lane < 64
    upper_x = jnp.logical_and(inner, jnp.logical_or(lane < 63, jnp.logical_not(last_x)))
    after_x = jnp.logical_and(lane > 0, jnp.logical_or(inner, jnp.logical_and(lane == 64, jnp.logical_not(last_x))))
    apart = jnp.where(inner, 2 * lane, 2 * lane - 127)
    not_last_z = (gz < lax.axis_size("gz") - 1).astype(jnp.float32)
    pick = jnp.where(lane < 64, 2 * lane, 127) % 128

    def squeeze(v):
        g = jnp.take_along_axis(v, pick, axis=1, mode="promise_in_bounds")
        return jnp.where(lane <= 64, g, 0.0)

    def coarsen(step):
        ydone = {}
        for ox in range(3):
            slots = {}
            for oy in range(3):
                kind = (2 if oy == 0 else 0) + (1 if ox == 0 else 0)
                s = [[None] * 4 for _ in range(3)]
                for oz in range(3):
                    for z in range(4):
                        factor = scale[kind, 5 + z if oz == 1 else 4 if (z == 0 and oz == 0) else z]
                        s[oz][z] = blocks[step, oz, oy, ox, z] * factor
                a1, b1 = s[0][1] + s[1][1], s[2][1] + s[1][1]
                a3, b3 = s[0][3] + s[1][3], s[2][3] + s[1][3]
                slots[0, 0, oy] = s[0][0]
                slots[1, 0, oy] = s[0][0] + s[2][0] + s[1][0] + a1
                slots[2, 0, oy] = s[2][0] + b1
                slots[0, 1, oy] = s[0][2] + a1
                slots[1, 1, oy] = s[0][2] + s[2][2] + s[1][2] + b1 + a3
                slots[2, 1, oy] = (s[2][2] + b3) * not_last_z
                slots[3, 0, oy] = a3
                slots[3, 1, oy] = b3
            beyond = [None, None]
            for slot in range(4):
                ev, od = [], []
                for oy in range(3):
                    z0, z1 = slots[slot, 0, oy], slots[slot, 1, oy]
                    ev.append(jnp.where(even, z0, sroll(z1, 1)))
                    od.append(jnp.where(even, sroll(z0, -1), z1))
                half = 0.5 * od[1]
                a, b = od[0] + half, od[2] + half
                a_before, b_before = sroll(a, 2), sroll(b, 2)
                ydone[slot * 3, ox] = ev[0] + jnp.where(row < 2, 0.0, a_before)
                ydone[slot * 3 + 1, ox] = ev[0] + ev[2] + (ev[1] + ev[1]) + a + jnp.where(row < 2, 0.0, b_before)
                ydone[slot * 3 + 2, ox] = jnp.where(keep_y, ev[2] + b, 0.0)
                if slot % 2 == 0:
                    beyond[slot // 2] = jnp.where(row < 2, a_before, sroll(b, 4))
                else:
                    ends = jnp.where(row < 6, sroll(a, 6), b)
                    beyond[slot // 2] = jnp.where(row < 4, beyond[slot // 2], ends) * not_last_y
            ydone[12, ox], ydone[13, ox] = beyond
        kept, sent, rows = [None] * ITEMS, [None] * PLANE, {}
        for i in range(14):
            v = [jnp.take_along_axis(ydone[i, ox], apart, axis=1, mode="promise_in_bounds") for ox in range(3)]
            half = 0.5 * v[1]
            a, b = v[0] + half, v[2] + half
            lower = jnp.where(inner, v[0], 0.0) + jnp.where(after_x, lroll(a, 65), 0.0)
            middle = jnp.where(inner, v[0] + v[2] + (v[1] + v[1]) + lroll(a, 64), 0.0) + jnp.where(after_x, lroll(b, 65), 0.0)
            upper = jnp.where(upper_x, v[2] + lroll(b, 64), 0.0)
            for cx, v in enumerate((lower, middle, upper)):
                if i < 9:
                    kept[i * 3 + cx] = v
                elif i < 12:
                    sent[(i - 9) * 3 + cx] = v
                elif i == 12:
                    kept[27 + cx] = v
                else:
                    rows[cx] = v
        kept[30] = jnp.where(row < 4, rows[0], sroll(rows[1], 4))
        sent[9] = jnp.where(row < 4, sroll(rows[0], 4), rows[1])
        kept[31] = sent[10] = rows[2]
        for i, v in enumerate(kept):
            w[step, i] = v
        right[step], left[step] = pack_sides(kept)
        plane_right[step], plane_left[step] = pack_sides(sent)
        for i, v in enumerate(pack_plane(sent)):
            plane[step * plane_size(PLANE) + i] = v

    def scales():
        low_x = jnp.where(jnp.logical_and(lane == 0, gx == 0), 0.0, 1.0)
        low_y = jnp.where(jnp.logical_and(row == 0, gy == 0), 0.0, 1.0)
        low_z = (gz > 0).astype(jnp.float32)
        for z in range(4):
            k = classes[z].astype(jnp.float32)
            s = 0.125 * (0.05 + 0.95 * (k * k * k) / 27.0)
            for cy in range(2):
                for cx in range(2):
                    v = s
                    if cy:
                        v = v * low_y
                    if cx:
                        v = v * low_x
                    scale[cy * 2 + cx, z] = v
                    scale[cy * 2 + cx, 5 + z] = (0.5 if z % 2 else 2.0) * v
                    if z == 0:
                        scale[cy * 2 + cx, 4] = v * low_z

    def loads():
        items = []
        for c in range(3):
            f = [residual[c, z] for z in range(4)]
            planes = [f[0] + 0.5 * f[1], 0.5 * f[1] + f[2] + 0.5 * f[3], 0.5 * f[3]]
            full, beyond = [], []
            for v in planes:
                h = 0.5 * v
                before = sroll(h, 1)
                full.append(v + sroll(h, -1) + jnp.where(row == 0, 0.0, before))
                beyond.append(h * not_last_y)
            main = jnp.where(even, full[0], sroll(full[1], 1))
            ghost = jnp.where(even, full[2], 0.0)
            for z in range(3):
                ghost = jnp.where(row == 1 + 2 * z, sroll(beyond[z], 2 + 2 * z), ghost)
            items.append((main, ghost))
        vs = []
        for v in [m for m, _ in items] + [g for _, g in items]:
            h = 0.5 * v
            v = v + lroll(h, -1) + jnp.where(lane == 0, 0.0, lroll(h, 1))
            v = jnp.where(lane == 127, h * not_last_x, v)
            vs.append(squeeze(v))
        for i, v in enumerate(vs):
            wl[i] = v

        right[9], left[9] = pack_sides(vs)
        plane_right[9], plane_left[9] = pack_sides(vs[3:])
        for i, v in enumerate(pack_plane(vs[3:])):
            plane[9 * plane_size(PLANE) + i] = v

    classes_copy.wait()
    scales()
    residual_copy.wait()
    loads()

    def body(step, carry):
        fetch(step).wait()

        @pl.when(step + AHEAD < 9)
        def _():
            fetch(step + AHEAD).start()

        coarsen(step)
        return carry

    lax.fori_loop(0, 9, body, 0, unroll=9)


def planes_kernel(plane_left, from_left, plane_right, from_right, plane, w, wl, w_out, wl_out, up, down, total):
    row = rows_of()
    even = row % 2 == 0
    total[...] = jnp.zeros_like(total)

    def body(rc, carry):
        got = unpack_plane(lambda i: plane[rc * plane_size(PLANE) + i], PLANE, plane_left[rc], plane_right[rc])
        from_l, from_r = from_left[rc], from_right[rc]
        f = [None] * ITEMS
        for k in range(ITEMS):
            v = w[rc, k] + sides(from_l, from_r, k)
            if k < 9:
                v = v + jnp.where(even, got[k], 0.0)
            elif k < 18:
                v = v + jnp.where(even, sroll(got[k - 9], -1), 0.0)
            elif 27 <= k < 30:
                end = (sroll(got[9], 4), got[9], got[10])[k - 27]
                v = v + jnp.where(even, jnp.where(row < 4, sroll(end, 4), sroll(end, -1)), 0.0)
            f[k] = v
            w_out[rc, k] = v
        magnitude = jnp.abs(f[0])
        for k in range(1, 27):
            magnitude = magnitude + jnp.abs(f[k])
        total[rc // 3] += magnitude
        ups, downs = [], []
        for k in range(0, 27, 2):
            two = f[k + 1] if k + 1 < 27 else None
            ups.append(jnp.where(row < 4, sroll(f[k], 4), sroll(f[31], 4) if two is None else two))
            downs.append(jnp.where(row < 4, f[k], 0.0 if two is None else sroll(two, 4)))
        ups += f[27:31]
        for ref, vs in ((up, ups), (down, downs)):
            for i, v in enumerate(pack(vs)):
                ref[rc * packed_size(len(vs)) + i] = v
        return carry

    lax.fori_loop(0, 9, body, 0, unroll=9)
    got = unpack_plane(lambda i: plane[9 * plane_size(PLANE) + i], 3, plane_left[9], plane_right[9])
    ups, downs = [], []
    for c in range(3):
        load = wl[c] + sides(from_left[9], from_right[9], c) + jnp.where(even, got[c], 0.0)
        ghost = wl[3 + c] + jnp.where(row == 1, sroll(got[c], -4), 0.0)
        ghost = ghost + sides(from_left[9], from_right[9], 3 + c)
        wl_out[c] = load
        wl_out[3 + c] = ghost
        d = load * (1.0 / (total[c] + 1e-06)) / CENTRE
        v = jnp.where(row < 4, sroll(load, 4), 0.0)
        v = jnp.where(row == 4, sroll(ghost, 3), v)
        v = jnp.where(row == 5, sroll(ghost, 2), v)
        ups.append(jnp.where(row >= 6, sroll(d, 4), v))
        downs.append(jnp.where(row < 4, load, jnp.where(row >= 6, sroll(d, 2), 0.0)))
    for ref, vs, size in ((up, ups, packed_size(UPS)), (down, downs, packed_size(DOWNS))):
        for i, v in enumerate(pack(vs)):
            ref[9 * size + i] = v


def piece_rows(n):
    return n + 8 * ((n + 15) // 16)


def split_planes(one, two):
    n = one.shape[0]
    even = lax.broadcasted_iota(jnp.int32, one.shape, 0) % 2 == 0
    first = jnp.where(even, one, pltpu.roll(two, 1, 0))
    second = jnp.where(even, pltpu.roll(one, n - 1, 0), two)
    return first, second


def join_planes(below, above):
    n = below.shape[0]
    even = lax.broadcasted_iota(jnp.int32, below.shape, 0) % 2 == 0
    one = jnp.where(even, below, pltpu.roll(above, 1, 0))
    two = jnp.where(even, pltpu.roll(below, n - 1, 0), above)
    return one, two


def share(at, planes, to_other, to_pair):
    low_of_pair = lax.axis_index("gz") % 2 == 0
    first, second = planes
    n = first.shape[0]
    to_pair[at : at + n] = jnp.where(low_of_pair, second, first)
    to_other[at : at + n] = jnp.where(low_of_pair, first, second)


def shared(at, n, from_other, from_pair):
    low_of_pair = lax.axis_index("gz") % 2 == 0
    other, pair = from_other[at : at + n], from_pair[at : at + n]
    return jnp.where(low_of_pair, other, pair), jnp.where(low_of_pair, pair, other)


def share_vector(load, n, at, to_other, to_pair):
    share(at, split_planes(load(0), load(1)), to_other, to_pair)
    third = load(2)
    at += n
    for i in range(0, n, 16):
        one = third[i : i + 8]
        two = third[i + 8 : i + 16] if i + 8 < n else jnp.zeros_like(one)
        share(at, split_planes(one, two), to_other, to_pair)
        at += 8


def shared_vector(n, at, from_other, from_pair):
    one, two = join_planes(*shared(at, n, from_other, from_pair))
    at += n
    parts = []
    for i in range(0, n, 16):
        parts += join_planes(*shared(at, 8, from_other, from_pair))
        at += 8
    return one, two, jnp.concatenate(parts[: n // 8], axis=0)


def rows_kernel(w, wl, from_low, from_high, whole, q, d, inverse, to_other, to_pair, total, turned, near):
    row = rows_of()
    ghosts = jnp.logical_or(row == 4, row == 5)
    total[...] = jnp.zeros_like(total)

    def body(rc, carry):
        ups = unpack(lambda i: from_low[rc * packed_size(UPS) + i], UPS)
        downs = unpack(lambda i: from_high[rc * packed_size(DOWNS) + i], DOWNS)
        got_ends = [ups[17], sroll(ups[17], 4), sroll(ups[13], 4)]
        own_ends = [w[rc, 30], sroll(w[rc, 30], 4), w[rc, 31]]
        top_sum = jnp.zeros((8, 128), jnp.float32)
        bottom_sum = jnp.zeros((8, 128), jnp.float32)
        for cz in range(3):
            for cy in range(3):
                for cx in range(3):
                    k = cz * 9 + cy * 3 + cx
                    f = sroll(w[rc, k], 4)
                    above, below = ups[k // 2], downs[k // 2]
                    top = jnp.where(row < 4, sroll(above, 4) if k % 2 else above, f)
                    bottom = jnp.where(row < 4, f, below if k % 2 else sroll(below, 4))
                    if cy < 2:
                        at = (cz % 2) * 4 + cy * 2
                        got = ups[14 + cx] if cz < 2 else got_ends[cx]
                        own = w[rc, 27 + cx] if cz < 2 else own_ends[cx]
                        top = top + jnp.where(ghosts, sroll(got, 4 - at), 0.0)
                        bottom = bottom + jnp.where(ghosts, sroll(own, 4 - at), 0.0)
                    whole[rc, k, 0:8] = top
                    whole[rc, k, 8:16] = bottom
                    top_sum = top_sum + jnp.abs(top)
                    bottom_sum = bottom_sum + jnp.abs(bottom)
        total[rc // 3, 0:8] += top_sum
        total[rc // 3, 8:16] += bottom_sum
        return carry

    lax.fori_loop(0, 9, body, 0, unroll=9)
    ups = unpack(lambda i: from_low[9 * packed_size(UPS) + i], 3)
    downs = unpack(lambda i: from_high[9 * packed_size(DOWNS) + i], 3)
    for c in range(3):
        load, ghost = sroll(wl[c], 4), wl[3 + c]
        q[c, 0:8] = jnp.where(row < 4, ups[c], load + jnp.where(ghosts, ups[c], 0.0))
        below = sroll(downs[c], 4)
        below = below + jnp.where(row == 4, sroll(ghost, 3), jnp.where(row == 5, sroll(ghost, 2), 0.0))
        q[c, 8:16] = jnp.where(row < 4, load, below)
        part = 1.0 / (total[c] + 1e-06)
        inverse[c] = part
        d[c, 16:24] = jnp.zeros((8, 128), jnp.float32)
        d[c, 2:18] = part * q[c] / CENTRE
        turned[...] = ups[c]
        d[c, 0:2] = turned[6:8]
        turned[...] = downs[c]
        d[c, 18:20] = turned[6:8]
    for c in range(3):
        fill_near(near, c, d[c], None)
    for r, product in enumerate(apply_to(whole, near)):
        q[r] = q[r] - product
    items = [edge_of(whole, i // 9, i % 9) for i in range(81)] + [q[r] for r in range(3)] + [inverse[r] for r in range(3)]
    packed = pack([v[h : h + 8] for v in items for h in (0, 8)])
    for i in range(0, len(packed), 2):
        share(4 * i, split_planes(packed[i], packed[i + 1]), to_other, to_pair)
    share_vector(lambda c: d[c], 24, EDGES, to_other, to_pair)


def operator_kernel(whole, operator):
    def body(rc, carry):
        for k in range(27):
            for z in range(2):
                v = whole[rc, k, pl.ds(4 + z, 4, stride=2), :]
                operator[k // 9, k // 3 % 3, k % 3, rc // 3, rc % 3, z] = v[:, 0:64]
        return carry

    lax.fori_loop(0, 9, body, 0, unroll=3)


def edge_of(whole, rc, at):
    even = lax.broadcasted_iota(jnp.int32, (16, 128), 0) % 2 == 0
    return jnp.where(even, whole[rc, at], whole[rc, 18 + at])


def fill_near(near, c, own, beyond):
    n = own.shape[0]
    even = lax.broadcasted_iota(jnp.int32, (n, 128), 0) % 2 == 0
    base = (24 - n) // 4
    if beyond is None:
        beyond = jnp.zeros_like(own)
    for cz, v in enumerate((
        jnp.where(even, beyond, pltpu.roll(own, 1, 0)),
        own,
        jnp.where(even, pltpu.roll(own, n - 1, 0), beyond),
    )):
        if base:
            near[cz, c, 0:8] = jnp.zeros((8, 128), jnp.float32)
            near[cz, c, 16:24] = jnp.zeros((8, 128), jnp.float32)
        near[cz, c, base : base + n] = v


def shifted(v):
    return pltpu.roll(v, 1, 1), v, pltpu.roll(v, 127, 1)


def apply_to(whole, near):
    sums = [jnp.zeros((16, 128), jnp.float32) for _ in range(3)]
    for cz in range(3):
        for cy in range(3):
            for c in range(3):
                for cx, moved in enumerate(shifted(near[cz, c, pl.ds(2 * cy, 16), :])):
                    for r in range(3):
                        sums[r] = sums[r] + whole[r * 3 + c, cz * 9 + cy * 3 + cx] * moved
    return sums


def two_steps_kernel(rhos, whole, q, d, inverse, from_other, from_pair, q_out, d_out, x_out, to_other, to_pair, near, packed, edges):
    even = rows_of() % 2 == 0
    for i in range(0, packed.shape[0], 2):
        packed[i], packed[i + 1] = join_planes(*shared(4 * i, 8, from_other, from_pair))
    for i, v in enumerate(unpack(lambda i: packed[i], 174)):
        edges[i // 2, 8 * (i % 2) : 8 * (i % 2) + 8] = v
    for c, v in enumerate(shared_vector(24, EDGES, from_other, from_pair)):
        near[0, c] = v
        near[1, c] = d[c]
    own = [jnp.zeros((16, 128), jnp.float32) for _ in range(3)]
    beyond = [jnp.zeros((16, 128), jnp.float32) for _ in range(3)]
    for cy in range(3):
        for c in range(3):
            outer = shifted(near[0, c, pl.ds(2 * cy, 16), :])
            inner = shifted(near[1, c, pl.ds(2 * cy, 16), :])
            for cx in range(3):
                for r in range(3):
                    rc, at = r * 3 + c, cy * 3 + cx
                    own[r] = own[r] + edge_of(whole, rc, at) * outer[cx]
                    beyond[r] = beyond[r] + edges[rc * 9 + at] * inner[cx]
    (same, slope), (same_next, slope_next) = rhos
    q_now, d_now, d_beyond = [], [], []
    for r in range(3):
        q_now.append(q[r] - own[r])
        d_now.append(same * d[r, 2:18] + slope * (inverse[r] * q_now[r]))
        d_beyond.append(same * near[0, r, 2:18] + slope * (edges[84 + r] * (edges[81 + r] - beyond[r])))
        x_out[r] = d[r, 2:18] + d_now[r]
    for r in range(3):
        fill_near(near, r, d_now[r], d_beyond[r])
    for r, product in enumerate(apply_to(whole, near)):
        q_next = q_now[r] - product
        q_out[r] = q_next
        d_out[r] = same_next * d_now[r] + slope_next * (inverse[r] * q_next)
    share_vector(lambda c: d_out[c], 16, 0, to_other, to_pair)


def last_step_kernel(rho, whole, q, d, inverse, x, from_other, from_pair, solution_out, near, turned):
    same, slope = rho
    for c, v in enumerate(shared_vector(16, 0, from_other, from_pair)):
        fill_near(near, c, d[c], v)
    for r, product in enumerate(apply_to(whole, near)):
        d_new = same * d[r] + slope * (inverse[r] * (q[r] - product))
        turned[...] = x[r] + d[r] + d_new
        for z in range(2):
            solution_out[r, z] = turned[pl.ds(4 + z, 4, stride=2), :][:, 0:64]


def shape(*dims):
    return jax.ShapeDtypeStruct(dims, jnp.float32)


def along(block, axes, distances):
    sizes = [lax.axis_size(a) for a in axes]
    route = []
    for source in itertools.product(*[range(n) for n in sizes]):
        target = [i + s for i, s in zip(source, distances)]
        if all(0 <= i < n for i, n in zip(target, sizes)):
            flat = [functools.reduce(lambda t, p: t * p[1] + p[0], zip(at, sizes), 0) for at in (source, target)]
            route.append(tuple(flat))
    return lax.ppermute(block, axes, route)


def exchanged(block, axis, first):
    n = lax.axis_size(axis)
    pairs = [(i, i + 1) for i in range(first, n - 1, 2)]
    return lax.ppermute(block, axis, pairs + [(j, i) for i, j in pairs])


def shards(blocks, classes, residual):
    w_shape, wl_shape = shape(9, ITEMS, 8, 128), shape(6, 8, 128)
    side = shape(10, 8, 128)
    w, wl, right, left, plane, plane_right, plane_left_sent = pl.pallas_call(
        coarsen_kernel,
        in_specs=[HBM] * 3,
        out_specs=[VMEM] * 7,
        out_shape=[w_shape, wl_shape, side, side, shape(9 * plane_size(PLANE) + plane_size(3), 8, 128), side, side],
        scratch_shapes=[
            pltpu.VMEM((9, 3, 3, 3, 4, 8, 128), jnp.float32),
            pltpu.VMEM((4, 8, 128), jnp.int32),
            pltpu.VMEM((3, 4, 8, 128), jnp.float32),
            pltpu.VMEM((4, 9, 8, 128), jnp.float32),
            pltpu.SemaphoreType.DMA((11,)),
        ],
        compiler_params=LIMIT,
    )(*(pltpu.with_memory_space_constraint(v, pltpu.HBM) for v in (blocks, classes, residual)))
    plane_left = along(plane_right, ("gx", "gz"), (1, 1))
    from_left = along(right, ("gx",), (1,))
    plane_right = along(plane_left_sent, ("gx", "gz"), (-1, 1))
    from_right = along(left, ("gx",), (-1,))
    plane = along(plane, ("gz",), (1,))
    w, wl, up, down = pl.pallas_call(
        planes_kernel,
        in_specs=[VMEM] * 7,
        out_specs=[VMEM] * 4,
        out_shape=[w_shape, wl_shape, shape(9 * packed_size(UPS) + packed_size(3), 8, 128), shape(9 * packed_size(DOWNS) + packed_size(3), 8, 128)],
        scratch_shapes=[pltpu.VMEM((3, 8, 128), jnp.float32)],
        compiler_params=LIMIT,
    )(plane_left, from_left, plane_right, from_right, plane, w, wl)
    from_high = along(down, ("gy",), (-1,))
    from_low = along(up, ("gy",), (1,))
    whole_shape, vector = shape(9, 27, 16, 128), shape(3, 16, 128)
    near = pltpu.VMEM((3, 3, 24, 128), jnp.float32)
    whole, q, d, inverse, to_other, to_pair = pl.pallas_call(
        rows_kernel,
        in_specs=[VMEM] * 4,
        out_specs=[VMEM] * 6,
        out_shape=[whole_shape, vector, shape(3, 24, 128), vector] + [shape(EDGES + piece_rows(24), 128)] * 2,
        scratch_shapes=[pltpu.VMEM((3, 16, 128), jnp.float32), pltpu.VMEM((8, 128), jnp.float32), near],
        compiler_params=LIMIT,
    )(w, wl, from_low, from_high)
    operator = pl.pallas_call(
        operator_kernel,
        in_specs=[VMEM],
        out_specs=VMEM,
        out_shape=shape(3, 3, 3, 3, 3, 2, 4, 64),
        compiler_params=LIMIT,
        cost_estimate=pl.CostEstimate(flops=500000, bytes_accessed=3000000, transcendentals=0),
    )(whole)
    rhos, rho_now = [], 1.0 / SIGMA
    for _ in range(STEPS - 1):
        rho_next = 1.0 / (2.0 * SIGMA - rho_now)
        rhos.append((rho_next * rho_now, 2.0 * rho_next / HALF))
        rho_now = rho_next
    from_other, from_pair = exchanged(to_other, "gz", 1), exchanged(to_pair, "gz", 0)
    q, d, x, to_other, to_pair = pl.pallas_call(
        functools.partial(two_steps_kernel, rhos[:2]),
        in_specs=[VMEM] * 6,
        out_specs=[VMEM] * 5,
        out_shape=[vector] * 3 + [shape(piece_rows(16), 128)] * 2,
        scratch_shapes=[near, pltpu.VMEM((96, 8, 128), jnp.float32), pltpu.VMEM((87, 16, 128), jnp.float32)],
        compiler_params=LIMIT,
    )(whole, q, d, inverse, from_other, from_pair)
    from_other, from_pair = exchanged(to_other, "gz", 1), exchanged(to_pair, "gz", 0)
    coarse_solution = pl.pallas_call(
        functools.partial(last_step_kernel, rhos[2]),
        in_specs=[VMEM] * 7,
        out_specs=VMEM,
        out_shape=shape(3, 2, 4, 64),
        scratch_shapes=[near, pltpu.VMEM((16, 128), jnp.float32)],
        compiler_params=LIMIT,
    )(whole, q, d, inverse, x, from_other, from_pair)
    return operator, coarse_solution


def solution(mesh):
    placed = (
        P(None, None, None, None, None, "gz", "gy", "gx"),
        P("gz", "gy", "gx"),
        P(None, "gz", "gy", "gx"),
    )
    return jax.shard_map(
        shards,
        mesh=mesh,
        in_specs=placed,
        out_specs=(P(None, None, None, None, None, "gz", "gy", "gx"), P(None, "gz", "gy", "gx")),
        check_vma=False,
    )
```

```python
import functools
import itertools

import jax
import jax.numpy as jnp
from jax import lax
from jax.experimental import pallas as pl
from jax.experimental.pallas import tpu as pltpu
from jax.sharding import PartitionSpec as P

STEPS = 4
CHEB_LOW = 0.1
CHEB_HIGH = 1.0
CENTRE = (CHEB_HIGH + CHEB_LOW) / 2.0
HALF = (CHEB_HIGH - CHEB_LOW) / 2.0
SIGMA = CENTRE / HALF

ITEMS = 32
PLANE = 11
UPS, DOWNS = 18, 14
AHEAD = 3
EDGES = 8 * 48
VMEM = pl.BlockSpec(memory_space=pltpu.VMEM)
HBM = pl.BlockSpec(memory_space=pltpu.HBM)
LIMIT = pltpu.CompilerParams(vmem_limit_bytes=40 * 1024 * 1024)


def lanes_of():
    return lax.broadcasted_iota(jnp.int32, (8, 128), 1)


def rows_of():
    return lax.broadcasted_iota(jnp.int32, (8, 128), 0)


def lroll(v, s):
    s = s % 128
    return v if s == 0 else pltpu.roll(v, s, 1)


def sroll(v, s):
    s = s % 8
    return v if s == 0 else pltpu.roll(v, s, 0)


def halo_slots():
    lane = lanes_of()
    left = jnp.where(jnp.logical_and(lane >= 61, lane < 121), lax.div(lane - 61, 3), -1)
    return jnp.where(lane < 60, lax.div(lane, 3), left)


def packed_size(n):
    return (n + 1) // 2 + (n + 19) // 20


def pack(vs):
    lane = lanes_of()
    slots = halo_slots()
    out = []
    for i in range(0, len(vs), 2):
        other = lroll(vs[i + 1], 64) if i + 1 < len(vs) else jnp.zeros_like(vs[i])
        out.append(jnp.where(lane < 64, vs[i], other))
    for base in range(0, len(vs), 20):
        held = jnp.zeros((8, 128), jnp.float32)
        for j, v in enumerate(vs[base : base + 20]):
            held = jnp.where(slots == j, lroll(v, 3 * j - 64), held)
        out.append(held)
    return out


def unpack(load, n):
    lane = lanes_of()
    edge = jnp.logical_or(jnp.logical_and(lane >= 64, lane < 67), lane >= 125)
    mains = (n + 1) // 2
    out = []
    for i in range(n):
        main = load(i // 2)
        if i % 2:
            main = lroll(main, 64)
        held = lroll(load(mains + i // 20), 64 - 3 * (i % 20))
        out.append(jnp.where(lane < 64, main, jnp.where(edge, held, 0.0)))
    return out


def right_slots():
    return lax.div(lanes_of(), 4)


def left_slots():
    lane = lanes_of()
    return lax.div(jnp.where(lane < 67, lane + 61, lane - 67), 4)


def pack_sides(vs):
    rights, lefts = right_slots(), left_slots()
    right = jnp.zeros((8, 128), jnp.float32)
    left = jnp.zeros((8, 128), jnp.float32)
    for j, v in enumerate(vs):
        moved = lroll(v, 4 * j - 61)
        right = jnp.where(rights == j, moved, right)
        left = jnp.where(lefts == j, moved, left)
    return right, left


def sides(from_left, from_right, j):
    lane = lanes_of()
    both = lroll(jnp.where(right_slots() == j, from_left, from_right), -(4 * j + 3))
    ends = jnp.logical_or(jnp.logical_or(lane >= 125, lane == 0), jnp.logical_and(lane >= 64, lane < 67))
    return jnp.where(ends, both, 0.0)


def plane_size(n):
    return n // 2 + 1


def pack_plane(vs, right):
    lane = lanes_of()
    out = [jnp.where(lane < 64, vs[i], lroll(vs[i + 1], 64)) for i in range(0, len(vs) - 1, 2)]
    return out + [jnp.where(lane < 64, vs[-1], lroll(right, 64))]


def unpack_plane(load, n, from_left, from_right):
    lane = lanes_of()
    beyond = jnp.logical_and(jnp.logical_and(lane >= 67, lane < 64 + 4 * n), lax.rem(lane, 4) == 3)
    from_right = from_right + jnp.where(beyond, load(n // 2), 0.0)
    out = []
    for i in range(n):
        main = load(i // 2)
        if i % 2:
            main = lroll(main, 64)
        out.append(jnp.where(lane < 64, main, 0.0) + sides(from_left, from_right, i))
    return out


def coarsen_kernel(blocks_in, classes_in, residual_in, w, wl, right, left, plane, plane_right, plane_left, blocks, classes, residual, scale, sems):
    def fetch(i):
        source = blocks_in.at[:, :, :, i // 3, i % 3]
        return pltpu.make_async_copy(source, blocks.at[i], sems.at[i])

    classes_copy = pltpu.make_async_copy(classes_in, classes, sems.at[9])
    residual_copy = pltpu.make_async_copy(residual_in, residual, sems.at[10])
    classes_copy.start()
    fetch(0).start()
    residual_copy.start()
    for i in range(1, AHEAD):
        fetch(i).start()
    gx, gy, gz = (lax.axis_index(a) for a in ("gx", "gy", "gz"))
    lane, row = lanes_of(), rows_of()
    even = row % 2 == 0
    not_last_x = (gx < lax.axis_size("gx") - 1).astype(jnp.float32)
    last_x = gx == lax.axis_size("gx") - 1
    not_last_y = (gy < lax.axis_size("gy") - 1).astype(jnp.float32)
    keep_y = jnp.logical_or(row < 6, gy < lax.axis_size("gy") - 1)
    inner = lane < 64
    upper_x = jnp.logical_and(inner, jnp.logical_or(lane < 63, jnp.logical_not(last_x)))
    after_x = jnp.logical_and(lane > 0, jnp.logical_or(inner, jnp.logical_and(lane == 64, jnp.logical_not(last_x))))
    apart = jnp.where(inner, 2 * lane, 2 * lane - 127)
    not_last_z = (gz < lax.axis_size("gz") - 1).astype(jnp.float32)
    pick = jnp.where(lane < 64, 2 * lane, 127) % 128

    def squeeze(v):
        g = jnp.take_along_axis(v, pick, axis=1, mode="promise_in_bounds")
        return jnp.where(lane <= 64, g, 0.0)

    def coarsen(step):
        ydone = {}
        for ox in range(3):
            slots = {}
            for oy in range(3):
                kind = (2 if oy == 0 else 0) + (1 if ox == 0 else 0)
                s = [[None] * 4 for _ in range(3)]
                for oz in range(3):
                    for z in range(4):
                        factor = scale[kind, 5 + z if oz == 1 else 4 if (z == 0 and oz == 0) else z]
                        s[oz][z] = blocks[step, oz, oy, ox, z] * factor
                a1, b1 = s[0][1] + s[1][1], s[2][1] + s[1][1]
                a3, b3 = s[0][3] + s[1][3], s[2][3] + s[1][3]
                slots[0, 0, oy] = s[0][0]
                slots[1, 0, oy] = s[0][0] + s[2][0] + s[1][0] + a1
                slots[2, 0, oy] = s[2][0] + b1
                slots[0, 1, oy] = s[0][2] + a1
                slots[1, 1, oy] = s[0][2] + s[2][2] + s[1][2] + b1 + a3
                slots[2, 1, oy] = (s[2][2] + b3) * not_last_z
                slots[3, 0, oy] = a3
                slots[3, 1, oy] = b3
            beyond = [None, None]
            for slot in range(4):
                ev, od = [], []
                for oy in range(3):
                    z0, z1 = slots[slot, 0, oy], slots[slot, 1, oy]
                    ev.append(jnp.where(even, z0, sroll(z1, 1)))
                    od.append(jnp.where(even, sroll(z0, -1), z1))
                half = 0.5 * od[1]
                a, b = od[0] + half, od[2] + half
                a_before, b_before = sroll(a, 2), sroll(b, 2)
                ydone[slot * 3, ox] = ev[0] + jnp.where(row < 2, 0.0, a_before)
                ydone[slot * 3 + 1, ox] = ev[0] + ev[2] + (ev[1] + ev[1]) + a + jnp.where(row < 2, 0.0, b_before)
                ydone[slot * 3 + 2, ox] = jnp.where(keep_y, ev[2] + b, 0.0)
                if slot % 2 == 0:
                    beyond[slot // 2] = jnp.where(row < 2, a_before, sroll(b, 4))
                else:
                    ends = jnp.where(row < 6, sroll(a, 6), b)
                    beyond[slot // 2] = jnp.where(row < 4, beyond[slot // 2], ends) * not_last_y
            ydone[12, ox], ydone[13, ox] = beyond
        kept, sent, rows = [None] * ITEMS, [None] * PLANE, {}
        for i in range(14):
            v = [jnp.take_along_axis(ydone[i, ox], apart, axis=1, mode="promise_in_bounds") for ox in range(3)]
            half = 0.5 * v[1]
            a, b = v[0] + half, v[2] + half
            lower = jnp.where(inner, v[0], 0.0) + jnp.where(after_x, lroll(a, 65), 0.0)
            middle = jnp.where(inner, v[0] + v[2] + (v[1] + v[1]) + lroll(a, 64), 0.0) + jnp.where(after_x, lroll(b, 65), 0.0)
            upper = jnp.where(upper_x, v[2] + lroll(b, 64), 0.0)
            for cx, v in enumerate((lower, middle, upper)):
                if i < 9:
                    kept[i * 3 + cx] = v
                elif i < 12:
                    sent[(i - 9) * 3 + cx] = v
                elif i == 12:
                    kept[27 + cx] = v
                else:
                    rows[cx] = v
        kept[30] = jnp.where(row < 4, rows[0], sroll(rows[1], 4))
        sent[9] = jnp.where(row < 4, sroll(rows[0], 4), rows[1])
        kept[31] = sent[10] = rows[2]
        for i, v in enumerate(kept):
            w[step, i] = v
        right[step], left[step] = pack_sides(kept)
        sent_right, plane_left[step] = pack_sides(sent)
        plane_right[step] = sent_right
        for i, v in enumerate(pack_plane(sent, sent_right)):
            plane[step * plane_size(PLANE) + i] = v

    def scales():
        low_x = jnp.where(jnp.logical_and(lane == 0, gx == 0), 0.0, 1.0)
        low_y = jnp.where(jnp.logical_and(row == 0, gy == 0), 0.0, 1.0)
        low_z = (gz > 0).astype(jnp.float32)
        for z in range(4):
            k = classes[z].astype(jnp.float32)
            s = 0.125 * (0.05 + 0.95 * (k * k * k) / 27.0)
            for cy in range(2):
                for cx in range(2):
                    v = s
                    if cy:
                        v = v * low_y
                    if cx:
                        v = v * low_x
                    scale[cy * 2 + cx, z] = v
                    scale[cy * 2 + cx, 5 + z] = (0.5 if z % 2 else 2.0) * v
                    if z == 0:
                        scale[cy * 2 + cx, 4] = v * low_z

    def loads():
        items = []
        for c in range(3):
            f = [residual[c, z] for z in range(4)]
            planes = [f[0] + 0.5 * f[1], 0.5 * f[1] + f[2] + 0.5 * f[3], 0.5 * f[3]]
            full, beyond = [], []
            for v in planes:
                h = 0.5 * v
                before = sroll(h, 1)
                full.append(v + sroll(h, -1) + jnp.where(row == 0, 0.0, before))
                beyond.append(h * not_last_y)
            main = jnp.where(even, full[0], sroll(full[1], 1))
            ghost = jnp.where(even, full[2], 0.0)
            for z in range(3):
                ghost = jnp.where(row == 1 + 2 * z, sroll(beyond[z], 2 + 2 * z), ghost)
            items.append((main, ghost))
        vs = []
        for v in [m for m, _ in items] + [g for _, g in items]:
            h = 0.5 * v
            v = v + lroll(h, -1) + jnp.where(lane == 0, 0.0, lroll(h, 1))
            v = jnp.where(lane == 127, h * not_last_x, v)
            vs.append(squeeze(v))
        for i, v in enumerate(vs):
            wl[i] = v

        right[9], left[9] = pack_sides(vs)
        sent_right, plane_left[9] = pack_sides(vs[3:])
        plane_right[9] = sent_right
        for i, v in enumerate(pack_plane(vs[3:], sent_right)):
            plane[9 * plane_size(PLANE) + i] = v

    classes_copy.wait()
    scales()
    residual_copy.wait()
    loads()

    def body(step, carry):
        fetch(step).wait()

        @pl.when(step + AHEAD < 9)
        def _():
            fetch(step + AHEAD).start()

        coarsen(step)
        return carry

    lax.fori_loop(0, 9, body, 0, unroll=9)


def planes_kernel(plane_right, from_right, plane_left, from_left, plane, w, wl, w_out, wl_out, up, down, total):
    row = rows_of()
    even = row % 2 == 0
    total[...] = jnp.zeros_like(total)

    def body(rc, carry):
        got = unpack_plane(lambda i: plane[rc * plane_size(PLANE) + i], PLANE, plane_left[rc], plane_right[rc])
        from_l, from_r = from_left[rc], from_right[rc]
        f = [None] * ITEMS
        for k in range(ITEMS):
            v = w[rc, k] + sides(from_l, from_r, k)
            if k < 9:
                v = v + jnp.where(even, got[k], 0.0)
            elif k < 18:
                v = v + jnp.where(even, sroll(got[k - 9], -1), 0.0)
            elif 27 <= k < 30:
                end = (sroll(got[9], 4), got[9], got[10])[k - 27]
                v = v + jnp.where(even, jnp.where(row < 4, sroll(end, 4), sroll(end, -1)), 0.0)
            f[k] = v
            w_out[rc, k] = v
        magnitude = jnp.abs(f[0])
        for k in range(1, 27):
            magnitude = magnitude + jnp.abs(f[k])
        total[rc // 3] += magnitude
        ups, downs = [], []
        for k in range(0, 27, 2):
            two = f[k + 1] if k + 1 < 27 else None
            ups.append(jnp.where(row < 4, sroll(f[k], 4), sroll(f[31], 4) if two is None else two))
            downs.append(jnp.where(row < 4, f[k], 0.0 if two is None else sroll(two, 4)))
        ups += f[27:31]
        for ref, vs in ((up, ups), (down, downs)):
            for i, v in enumerate(pack(vs)):
                ref[rc * packed_size(len(vs)) + i] = v
        return carry

    lax.fori_loop(0, 9, body, 0, unroll=9)
    got = unpack_plane(lambda i: plane[9 * plane_size(PLANE) + i], 3, plane_left[9], plane_right[9])
    ups, downs = [], []
    for c in range(3):
        load = wl[c] + sides(from_left[9], from_right[9], c) + jnp.where(even, got[c], 0.0)
        ghost = wl[3 + c] + jnp.where(row == 1, sroll(got[c], -4), 0.0)
        ghost = ghost + sides(from_left[9], from_right[9], 3 + c)
        wl_out[c] = load
        wl_out[3 + c] = ghost
        d = load * (1.0 / (total[c] + 1e-06)) / CENTRE
        v = jnp.where(row < 4, sroll(load, 4), 0.0)
        v = jnp.where(row == 4, sroll(ghost, 3), v)
        v = jnp.where(row == 5, sroll(ghost, 2), v)
        ups.append(jnp.where(row >= 6, sroll(d, 4), v))
        downs.append(jnp.where(row < 4, load, jnp.where(row >= 6, sroll(d, 2), 0.0)))
    for ref, vs, size in ((up, ups, packed_size(UPS)), (down, downs, packed_size(DOWNS))):
        for i, v in enumerate(pack(vs)):
            ref[9 * size + i] = v


def piece_rows(n):
    return n + 8 * ((n + 15) // 16)


def split_planes(one, two):
    n = one.shape[0]
    even = lax.broadcasted_iota(jnp.int32, one.shape, 0) % 2 == 0
    first = jnp.where(even, one, pltpu.roll(two, 1, 0))
    second = jnp.where(even, pltpu.roll(one, n - 1, 0), two)
    return first, second


def join_planes(below, above):
    n = below.shape[0]
    even = lax.broadcasted_iota(jnp.int32, below.shape, 0) % 2 == 0
    one = jnp.where(even, below, pltpu.roll(above, 1, 0))
    two = jnp.where(even, pltpu.roll(below, n - 1, 0), above)
    return one, two


def share(at, planes, to_other, to_pair):
    low_of_pair = lax.axis_index("gz") % 2 == 0
    first, second = planes
    n = first.shape[0]
    to_pair[at : at + n] = jnp.where(low_of_pair, second, first)
    to_other[at : at + n] = jnp.where(low_of_pair, first, second)


def shared(at, n, from_other, from_pair):
    low_of_pair = lax.axis_index("gz") % 2 == 0
    other, pair = from_other[at : at + n], from_pair[at : at + n]
    return jnp.where(low_of_pair, other, pair), jnp.where(low_of_pair, pair, other)


def share_vector(load, n, at, to_other, to_pair):
    share(at, split_planes(load(0), load(1)), to_other, to_pair)
    third = load(2)
    at += n
    for i in range(0, n, 16):
        one = third[i : i + 8]
        two = third[i + 8 : i + 16] if i + 8 < n else jnp.zeros_like(one)
        share(at, split_planes(one, two), to_other, to_pair)
        at += 8


def shared_vector(n, at, from_other, from_pair):
    one, two = join_planes(*shared(at, n, from_other, from_pair))
    at += n
    parts = []
    for i in range(0, n, 16):
        parts += join_planes(*shared(at, 8, from_other, from_pair))
        at += 8
    return one, two, jnp.concatenate(parts[: n // 8], axis=0)


def rows_kernel(w, wl, from_low, from_high, whole, q, d, inverse, to_other, to_pair, total, turned, near):
    row = rows_of()
    ghosts = jnp.logical_or(row == 4, row == 5)
    total[...] = jnp.zeros_like(total)

    def body(rc, carry):
        ups = unpack(lambda i: from_low[rc * packed_size(UPS) + i], UPS)
        downs = unpack(lambda i: from_high[rc * packed_size(DOWNS) + i], DOWNS)
        got_ends = [ups[17], sroll(ups[17], 4), sroll(ups[13], 4)]
        own_ends = [w[rc, 30], sroll(w[rc, 30], 4), w[rc, 31]]
        top_sum = jnp.zeros((8, 128), jnp.float32)
        bottom_sum = jnp.zeros((8, 128), jnp.float32)
        for cz in range(3):
            for cy in range(3):
                for cx in range(3):
                    k = cz * 9 + cy * 3 + cx
                    f = sroll(w[rc, k], 4)
                    above, below = ups[k // 2], downs[k // 2]
                    top = jnp.where(row < 4, sroll(above, 4) if k % 2 else above, f)
                    bottom = jnp.where(row < 4, f, below if k % 2 else sroll(below, 4))
                    if cy < 2:
                        at = (cz % 2) * 4 + cy * 2
                        got = ups[14 + cx] if cz < 2 else got_ends[cx]
                        own = w[rc, 27 + cx] if cz < 2 else own_ends[cx]
                        top = top + jnp.where(ghosts, sroll(got, 4 - at), 0.0)
                        bottom = bottom + jnp.where(ghosts, sroll(own, 4 - at), 0.0)
                    whole[rc, k, 0:8] = top
                    whole[rc, k, 8:16] = bottom
                    top_sum = top_sum + jnp.abs(top)
                    bottom_sum = bottom_sum + jnp.abs(bottom)
        total[rc // 3, 0:8] += top_sum
        total[rc // 3, 8:16] += bottom_sum
        return carry

    lax.fori_loop(0, 9, body, 0, unroll=9)
    ups = unpack(lambda i: from_low[9 * packed_size(UPS) + i], 3)
    downs = unpack(lambda i: from_high[9 * packed_size(DOWNS) + i], 3)
    for c in range(3):
        load, ghost = sroll(wl[c], 4), wl[3 + c]
        q[c, 0:8] = jnp.where(row < 4, ups[c], load + jnp.where(ghosts, ups[c], 0.0))
        below = sroll(downs[c], 4)
        below = below + jnp.where(row == 4, sroll(ghost, 3), jnp.where(row == 5, sroll(ghost, 2), 0.0))
        q[c, 8:16] = jnp.where(row < 4, load, below)
        part = 1.0 / (total[c] + 1e-06)
        inverse[c] = part
        d[c, 16:24] = jnp.zeros((8, 128), jnp.float32)
        d[c, 2:18] = part * q[c] / CENTRE
        turned[...] = ups[c]
        d[c, 0:2] = turned[6:8]
        turned[...] = downs[c]
        d[c, 18:20] = turned[6:8]
    for c in range(3):
        fill_near(near, c, d[c], None)
    for r, product in enumerate(apply_to(whole, near)):
        q[r] = q[r] - product
    items = [edge_of(whole, i // 9, i % 9) for i in range(81)] + [q[r] for r in range(3)] + [inverse[r] for r in range(3)]
    packed = pack([v[h : h + 8] for v in items for h in (0, 8)])
    for i in range(0, len(packed), 2):
        share(4 * i, split_planes(packed[i], packed[i + 1]), to_other, to_pair)
    share_vector(lambda c: d[c], 24, EDGES, to_other, to_pair)


def operator_kernel(whole, operator):
    def body(rc, carry):
        for k in range(27):
            for z in range(2):
                v = whole[rc, k, pl.ds(4 + z, 4, stride=2), :]
                operator[k // 9, k // 3 % 3, k % 3, rc // 3, rc % 3, z] = v[:, 0:64]
        return carry

    lax.fori_loop(0, 9, body, 0, unroll=3)


def edge_of(whole, rc, at):
    even = lax.broadcasted_iota(jnp.int32, (16, 128), 0) % 2 == 0
    return jnp.where(even, whole[rc, at], whole[rc, 18 + at])


def fill_near(near, c, own, beyond):
    n = own.shape[0]
    even = lax.broadcasted_iota(jnp.int32, (n, 128), 0) % 2 == 0
    base = (24 - n) // 4
    if beyond is None:
        beyond = jnp.zeros_like(own)
    for cz, v in enumerate((
        jnp.where(even, beyond, pltpu.roll(own, 1, 0)),
        own,
        jnp.where(even, pltpu.roll(own, n - 1, 0), beyond),
    )):
        if base:
            near[cz, c, 0:8] = jnp.zeros((8, 128), jnp.float32)
            near[cz, c, 16:24] = jnp.zeros((8, 128), jnp.float32)
        near[cz, c, base : base + n] = v


def shifted(v):
    return pltpu.roll(v, 1, 1), v, pltpu.roll(v, 127, 1)


def apply_to(whole, near):
    sums = [jnp.zeros((16, 128), jnp.float32) for _ in range(3)]
    for cz in range(3):
        for cy in range(3):
            for c in range(3):
                for cx, moved in enumerate(shifted(near[cz, c, pl.ds(2 * cy, 16), :])):
                    for r in range(3):
                        sums[r] = sums[r] + whole[r * 3 + c, cz * 9 + cy * 3 + cx] * moved
    return sums


def two_steps_kernel(rhos, whole, q, d, inverse, from_other, from_pair, q_out, d_out, x_out, to_other, to_pair, near, packed, edges):
    even = rows_of() % 2 == 0
    for i in range(0, packed.shape[0], 2):
        packed[i], packed[i + 1] = join_planes(*shared(4 * i, 8, from_other, from_pair))
    for i, v in enumerate(unpack(lambda i: packed[i], 174)):
        edges[i // 2, 8 * (i % 2) : 8 * (i % 2) + 8] = v
    for c, v in enumerate(shared_vector(24, EDGES, from_other, from_pair)):
        near[0, c] = v
        near[1, c] = d[c]
    own = [jnp.zeros((16, 128), jnp.float32) for _ in range(3)]
    beyond = [jnp.zeros((16, 128), jnp.float32) for _ in range(3)]
    for cy in range(3):
        for c in range(3):
            outer = shifted(near[0, c, pl.ds(2 * cy, 16), :])
            inner = shifted(near[1, c, pl.ds(2 * cy, 16), :])
            for cx in range(3):
                for r in range(3):
                    rc, at = r * 3 + c, cy * 3 + cx
                    own[r] = own[r] + edge_of(whole, rc, at) * outer[cx]
                    beyond[r] = beyond[r] + edges[rc * 9 + at] * inner[cx]
    (same, slope), (same_next, slope_next) = rhos
    q_now, d_now, d_beyond = [], [], []
    for r in range(3):
        q_now.append(q[r] - own[r])
        d_now.append(same * d[r, 2:18] + slope * (inverse[r] * q_now[r]))
        d_beyond.append(same * near[0, r, 2:18] + slope * (edges[84 + r] * (edges[81 + r] - beyond[r])))
        x_out[r] = d[r, 2:18] + d_now[r]
    for r in range(3):
        fill_near(near, r, d_now[r], d_beyond[r])
    for r, product in enumerate(apply_to(whole, near)):
        q_next = q_now[r] - product
        q_out[r] = q_next
        d_out[r] = same_next * d_now[r] + slope_next * (inverse[r] * q_next)
    share_vector(lambda c: d_out[c], 16, 0, to_other, to_pair)


def last_step_kernel(rho, whole, q, d, inverse, x, from_other, from_pair, solution_out, near, turned):
    same, slope = rho
    for c, v in enumerate(shared_vector(16, 0, from_other, from_pair)):
        fill_near(near, c, d[c], v)
    for r, product in enumerate(apply_to(whole, near)):
        d_new = same * d[r] + slope * (inverse[r] * (q[r] - product))
        turned[...] = x[r] + d[r] + d_new
        for z in range(2):
            solution_out[r, z] = turned[pl.ds(4 + z, 4, stride=2), :][:, 0:64]


def shape(*dims):
    return jax.ShapeDtypeStruct(dims, jnp.float32)


def along(block, axes, distances):
    sizes = [lax.axis_size(a) for a in axes]
    route = []
    for source in itertools.product(*[range(n) for n in sizes]):
        target = [i + s for i, s in zip(source, distances)]
        if all(0 <= i < n for i, n in zip(target, sizes)):
            flat = [functools.reduce(lambda t, p: t * p[1] + p[0], zip(at, sizes), 0) for at in (source, target)]
            route.append(tuple(flat))
    return lax.ppermute(block, axes, route)


def exchanged(block, axis, first):
    n = lax.axis_size(axis)
    pairs = [(i, i + 1) for i in range(first, n - 1, 2)]
    return lax.ppermute(block, axis, pairs + [(j, i) for i, j in pairs])


def shards(blocks, classes, residual):
    w_shape, wl_shape = shape(9, ITEMS, 8, 128), shape(6, 8, 128)
    side = shape(10, 8, 128)
    w, wl, right, left, plane, plane_right, plane_left_sent = pl.pallas_call(
        coarsen_kernel,
        in_specs=[HBM] * 3,
        out_specs=[VMEM] * 7,
        out_shape=[w_shape, wl_shape, side, side, shape(9 * plane_size(PLANE) + plane_size(3), 8, 128), side, side],
        scratch_shapes=[
            pltpu.VMEM((9, 3, 3, 3, 4, 8, 128), jnp.float32),
            pltpu.VMEM((4, 8, 128), jnp.int32),
            pltpu.VMEM((3, 4, 8, 128), jnp.float32),
            pltpu.VMEM((4, 9, 8, 128), jnp.float32),
            pltpu.SemaphoreType.DMA((11,)),
        ],
        compiler_params=LIMIT,
    )(*(pltpu.with_memory_space_constraint(v, pltpu.HBM) for v in (blocks, classes, residual)))
    plane_left = along(plane_right, ("gx", "gz"), (1, 1))
    from_left = along(right, ("gx",), (1,))
    plane_right = along(plane_left_sent, ("gx", "gz"), (-1, 1))
    from_right = along(left, ("gx",), (-1,))
    plane = along(plane, ("gz",), (1,))
    w, wl, up, down = pl.pallas_call(
        planes_kernel,
        in_specs=[VMEM] * 7,
        out_specs=[VMEM] * 4,
        out_shape=[w_shape, wl_shape, shape(9 * packed_size(UPS) + packed_size(3), 8, 128), shape(9 * packed_size(DOWNS) + packed_size(3), 8, 128)],
        scratch_shapes=[pltpu.VMEM((3, 8, 128), jnp.float32)],
        compiler_params=LIMIT,
    )(plane_right, from_right, plane_left, from_left, plane, w, wl)
    from_high = along(down, ("gy",), (-1,))
    from_low = along(up, ("gy",), (1,))
    whole_shape, vector = shape(9, 27, 16, 128), shape(3, 16, 128)
    near = pltpu.VMEM((3, 3, 24, 128), jnp.float32)
    whole, q, d, inverse, to_other, to_pair = pl.pallas_call(
        rows_kernel,
        in_specs=[VMEM] * 4,
        out_specs=[VMEM] * 6,
        out_shape=[whole_shape, vector, shape(3, 24, 128), vector] + [shape(EDGES + piece_rows(24), 128)] * 2,
        scratch_shapes=[pltpu.VMEM((3, 16, 128), jnp.float32), pltpu.VMEM((8, 128), jnp.float32), near],
        compiler_params=LIMIT,
    )(w, wl, from_low, from_high)
    operator = pl.pallas_call(
        operator_kernel,
        in_specs=[VMEM],
        out_specs=VMEM,
        out_shape=shape(3, 3, 3, 3, 3, 2, 4, 64),
        compiler_params=LIMIT,
        cost_estimate=pl.CostEstimate(flops=500000, bytes_accessed=3000000, transcendentals=0),
    )(whole)
    rhos, rho_now = [], 1.0 / SIGMA
    for _ in range(STEPS - 1):
        rho_next = 1.0 / (2.0 * SIGMA - rho_now)
        rhos.append((rho_next * rho_now, 2.0 * rho_next / HALF))
        rho_now = rho_next
    from_other, from_pair = exchanged(to_other, "gz", 1), exchanged(to_pair, "gz", 0)
    q, d, x, to_other, to_pair = pl.pallas_call(
        functools.partial(two_steps_kernel, rhos[:2]),
        in_specs=[VMEM] * 6,
        out_specs=[VMEM] * 5,
        out_shape=[vector] * 3 + [shape(piece_rows(16), 128)] * 2,
        scratch_shapes=[near, pltpu.VMEM((96, 8, 128), jnp.float32), pltpu.VMEM((87, 16, 128), jnp.float32)],
        compiler_params=LIMIT,
    )(whole, q, d, inverse, from_other, from_pair)
    from_other, from_pair = exchanged(to_other, "gz", 1), exchanged(to_pair, "gz", 0)
    coarse_solution = pl.pallas_call(
        functools.partial(last_step_kernel, rhos[2]),
        in_specs=[VMEM] * 7,
        out_specs=VMEM,
        out_shape=shape(3, 2, 4, 64),
        scratch_shapes=[near, pltpu.VMEM((16, 128), jnp.float32)],
        compiler_params=LIMIT,
    )(whole, q, d, inverse, x, from_other, from_pair)
    return operator, coarse_solution


def solution(mesh):
    placed = (
        P(None, None, None, None, None, "gz", "gy", "gx"),
        P("gz", "gy", "gx"),
        P(None, "gz", "gy", "gx"),
    )
    return jax.shard_map(
        shards,
        mesh=mesh,
        in_specs=placed,
        out_specs=(P(None, None, None, None, None, "gz", "gy", "gx"), P(None, "gz", "gy", "gx")),
        check_vma=False,
    )
```

```python
import functools
import itertools

import jax
import jax.numpy as jnp
from jax import lax
from jax.experimental import pallas as pl
from jax.experimental.pallas import tpu as pltpu
from jax.sharding import PartitionSpec as P

STEPS = 4
CHEB_LOW = 0.1
CHEB_HIGH = 1.0
CENTRE = (CHEB_HIGH + CHEB_LOW) / 2.0
HALF = (CHEB_HIGH - CHEB_LOW) / 2.0
SIGMA = CENTRE / HALF

ITEMS = 32
PLANE = 11
UPS, DOWNS = 18, 14
AHEAD = 3
EDGES = 8 * 48
VMEM = pl.BlockSpec(memory_space=pltpu.VMEM)
HBM = pl.BlockSpec(memory_space=pltpu.HBM)
LIMIT = pltpu.CompilerParams(vmem_limit_bytes=40 * 1024 * 1024)


def lanes_of():
    return lax.broadcasted_iota(jnp.int32, (8, 128), 1)


def rows_of():
    return lax.broadcasted_iota(jnp.int32, (8, 128), 0)


def lroll(v, s):
    s = s % 128
    return v if s == 0 else pltpu.roll(v, s, 1)


def sroll(v, s):
    s = s % 8
    return v if s == 0 else pltpu.roll(v, s, 0)


def halo_slots():
    lane = lanes_of()
    left = jnp.where(jnp.logical_and(lane >= 61, lane < 121), lax.div(lane - 61, 3), -1)
    return jnp.where(lane < 60, lax.div(lane, 3), left)


def packed_size(n):
    return (n + 1) // 2 + (n + 19) // 20


def pack(vs):
    lane = lanes_of()
    slots = halo_slots()
    out = []
    for i in range(0, len(vs), 2):
        other = lroll(vs[i + 1], 64) if i + 1 < len(vs) else jnp.zeros_like(vs[i])
        out.append(jnp.where(lane < 64, vs[i], other))
    for base in range(0, len(vs), 20):
        held = jnp.zeros((8, 128), jnp.float32)
        for j, v in enumerate(vs[base : base + 20]):
            held = jnp.where(slots == j, lroll(v, 3 * j - 64), held)
        out.append(held)
    return out


def unpack(load, n):
    lane = lanes_of()
    edge = jnp.logical_or(jnp.logical_and(lane >= 64, lane < 67), lane >= 125)
    mains = (n + 1) // 2
    out = []
    for i in range(n):
        main = load(i // 2)
        if i % 2:
            main = lroll(main, 64)
        held = lroll(load(mains + i // 20), 64 - 3 * (i % 20))
        out.append(jnp.where(lane < 64, main, jnp.where(edge, held, 0.0)))
    return out


def right_slots():
    return lax.div(lanes_of(), 4)


def left_slots():
    lane = lanes_of()
    return lax.div(jnp.where(lane < 67, lane + 61, lane - 67), 4)


def pack_sides(vs):
    rights, lefts = right_slots(), left_slots()
    right = jnp.zeros((8, 128), jnp.float32)
    left = jnp.zeros((8, 128), jnp.float32)
    for j, v in enumerate(vs):
        moved = lroll(v, 4 * j - 61)
        right = jnp.where(rights == j, moved, right)
        left = jnp.where(lefts == j, moved, left)
    return right, left


def sides(from_left, from_right, j):
    lane = lanes_of()
    both = lroll(jnp.where(right_slots() == j, from_left, from_right), -(4 * j + 3))
    ends = jnp.logical_or(jnp.logical_or(lane >= 125, lane == 0), jnp.logical_and(lane >= 64, lane < 67))
    return jnp.where(ends, both, 0.0)


def plane_size(n):
    return n // 2 + 1


def pack_plane(vs, right):
    lane = lanes_of()
    out = [jnp.where(lane < 64, vs[i], lroll(vs[i + 1], 64)) for i in range(0, len(vs) - 1, 2)]
    return out + [jnp.where(lane < 64, vs[-1], lroll(right, 64))]


def unpack_plane(load, n, from_left, from_right):
    lane = lanes_of()
    beyond = jnp.logical_and(jnp.logical_and(lane >= 67, lane < 64 + 4 * n), lax.rem(lane, 4) == 3)
    from_right = from_right + jnp.where(beyond, load(n // 2), 0.0)
    out = []
    for i in range(n):
        main = load(i // 2)
        if i % 2:
            main = lroll(main, 64)
        out.append(jnp.where(lane < 64, main, 0.0) + sides(from_left, from_right, i))
    return out


def coarsen_kernel(blocks_in, classes_in, residual_in, w, wl, right, left, plane, plane_right, plane_left, blocks, classes, residual, scale, sems):
    def fetch(i):
        source = blocks_in.at[:, :, :, i // 3, i % 3]
        return pltpu.make_async_copy(source, blocks.at[i], sems.at[i])

    classes_copy = pltpu.make_async_copy(classes_in, classes, sems.at[9])
    residual_copy = pltpu.make_async_copy(residual_in, residual, sems.at[10])
    classes_copy.start()
    fetch(0).start()
    residual_copy.start()
    for i in range(1, AHEAD):
        fetch(i).start()
    gx, gy, gz = (lax.axis_index(a) for a in ("gx", "gy", "gz"))
    lane, row = lanes_of(), rows_of()
    even = row % 2 == 0
    not_last_x = (gx < lax.axis_size("gx") - 1).astype(jnp.float32)
    last_x = gx == lax.axis_size("gx") - 1
    not_last_y = (gy < lax.axis_size("gy") - 1).astype(jnp.float32)
    keep_y = jnp.logical_or(row < 6, gy < lax.axis_size("gy") - 1)
    inner = lane < 64
    upper_x = jnp.logical_and(inner, jnp.logical_or(lane < 63, jnp.logical_not(last_x)))
    after_x = jnp.logical_and(lane > 0, jnp.logical_or(inner, jnp.logical_and(lane == 64, jnp.logical_not(last_x))))
    apart = jnp.where(inner, 2 * lane, 2 * lane - 127)
    not_last_z = (gz < lax.axis_size("gz") - 1).astype(jnp.float32)
    pick = jnp.where(lane < 64, 2 * lane, 127) % 128

    def squeeze(v):
        g = jnp.take_along_axis(v, pick, axis=1, mode="promise_in_bounds")
        return jnp.where(lane <= 64, g, 0.0)

    def coarsen(step):
        ydone = {}
        for ox in range(3):
            slots = {}
            for oy in range(3):
                kind = (2 if oy == 0 else 0) + (1 if ox == 0 else 0)
                s = [[None] * 4 for _ in range(3)]
                for oz in range(3):
                    for z in range(4):
                        factor = scale[kind, 5 + z if oz == 1 else 4 if (z == 0 and oz == 0) else z]
                        s[oz][z] = blocks[step, oz, oy, ox, z] * factor
                a1, b1 = s[0][1] + s[1][1], s[2][1] + s[1][1]
                a3, b3 = s[0][3] + s[1][3], s[2][3] + s[1][3]
                slots[0, 0, oy] = s[0][0]
                slots[1, 0, oy] = s[0][0] + s[2][0] + s[1][0] + a1
                slots[2, 0, oy] = s[2][0] + b1
                slots[0, 1, oy] = s[0][2] + a1
                slots[1, 1, oy] = s[0][2] + s[2][2] + s[1][2] + b1 + a3
                slots[2, 1, oy] = (s[2][2] + b3) * not_last_z
                slots[3, 0, oy] = a3
                slots[3, 1, oy] = b3
            beyond = [None, None]
            for slot in range(4):
                ev, od = [], []
                for oy in range(3):
                    z0, z1 = slots[slot, 0, oy], slots[slot, 1, oy]
                    ev.append(jnp.where(even, z0, sroll(z1, 1)))
                    od.append(jnp.where(even, sroll(z0, -1), z1))
                half = 0.5 * od[1]
                a, b = od[0] + half, od[2] + half
                a_before, b_before = sroll(a, 2), sroll(b, 2)
                ydone[slot * 3, ox] = ev[0] + jnp.where(row < 2, 0.0, a_before)
                ydone[slot * 3 + 1, ox] = ev[0] + ev[2] + (ev[1] + ev[1]) + a + jnp.where(row < 2, 0.0, b_before)
                ydone[slot * 3 + 2, ox] = jnp.where(keep_y, ev[2] + b, 0.0)
                if slot % 2 == 0:
                    beyond[slot // 2] = jnp.where(row < 2, a_before, sroll(b, 4))
                else:
                    ends = jnp.where(row < 6, sroll(a, 6), b)
                    beyond[slot // 2] = jnp.where(row < 4, beyond[slot // 2], ends) * not_last_y
            ydone[12, ox], ydone[13, ox] = beyond
        kept, sent, rows = [None] * ITEMS, [None] * PLANE, {}
        for i in range(14):
            v = [jnp.take_along_axis(ydone[i, ox], apart, axis=1, mode="promise_in_bounds") for ox in range(3)]
            half = 0.5 * v[1]
            a, b = v[0] + half, v[2] + half
            lower = jnp.where(inner, v[0], 0.0) + jnp.where(after_x, lroll(a, 65), 0.0)
            middle = jnp.where(inner, v[0] + v[2] + (v[1] + v[1]) + lroll(a, 64), 0.0) + jnp.where(after_x, lroll(b, 65), 0.0)
            upper = jnp.where(upper_x, v[2] + lroll(b, 64), 0.0)
            for cx, v in enumerate((lower, middle, upper)):
                if i < 9:
                    kept[i * 3 + cx] = v
                elif i < 12:
                    sent[(i - 9) * 3 + cx] = v
                elif i == 12:
                    kept[27 + cx] = v
                else:
                    rows[cx] = v
        kept[30] = jnp.where(row < 4, rows[0], sroll(rows[1], 4))
        sent[9] = jnp.where(row < 4, sroll(rows[0], 4), rows[1])
        kept[31] = sent[10] = rows[2]
        for i, v in enumerate(kept):
            w[step, i] = v
        right[step], left[step] = pack_sides(kept)
        sent_right, plane_left[step] = pack_sides(sent)
        plane_right[step] = sent_right
        for i, v in enumerate(pack_plane(sent, sent_right)):
            plane[step * plane_size(PLANE) + i] = v

    def scales():
        low_x = jnp.where(jnp.logical_and(lane == 0, gx == 0), 0.0, 1.0)
        low_y = jnp.where(jnp.logical_and(row == 0, gy == 0), 0.0, 1.0)
        low_z = (gz > 0).astype(jnp.float32)
        for z in range(4):
            k = classes[z].astype(jnp.float32)
            s = 0.125 * (0.05 + 0.95 * (k * k * k) / 27.0)
            for cy in range(2):
                for cx in range(2):
                    v = s
                    if cy:
                        v = v * low_y
                    if cx:
                        v = v * low_x
                    scale[cy * 2 + cx, z] = v
                    scale[cy * 2 + cx, 5 + z] = (0.5 if z % 2 else 2.0) * v
                    if z == 0:
                        scale[cy * 2 + cx, 4] = v * low_z

    def loads():
        items = []
        for c in range(3):
            f = [residual[c, z] for z in range(4)]
            planes = [f[0] + 0.5 * f[1], 0.5 * f[1] + f[2] + 0.5 * f[3], 0.5 * f[3]]
            full, beyond = [], []
            for v in planes:
                h = 0.5 * v
                before = sroll(h, 1)
                full.append(v + sroll(h, -1) + jnp.where(row == 0, 0.0, before))
                beyond.append(h * not_last_y)
            main = jnp.where(even, full[0], sroll(full[1], 1))
            ghost = jnp.where(even, full[2], 0.0)
            for z in range(3):
                ghost = jnp.where(row == 1 + 2 * z, sroll(beyond[z], 2 + 2 * z), ghost)
            items.append((main, ghost))
        vs = []
        for v in [m for m, _ in items] + [g for _, g in items]:
            h = 0.5 * v
            v = v + lroll(h, -1) + jnp.where(lane == 0, 0.0, lroll(h, 1))
            v = jnp.where(lane == 127, h * not_last_x, v)
            vs.append(squeeze(v))
        for i, v in enumerate(vs):
            wl[i] = v

        right[9], left[9] = pack_sides(vs)
        sent_right, plane_left[9] = pack_sides(vs[3:])
        plane_right[9] = sent_right
        for i, v in enumerate(pack_plane(vs[3:], sent_right)):
            plane[9 * plane_size(PLANE) + i] = v

    classes_copy.wait()
    scales()
    residual_copy.wait()
    loads()

    def body(step, carry):
        fetch(step).wait()

        @pl.when(step + AHEAD < 9)
        def _():
            fetch(step + AHEAD).start()

        coarsen(step)
        return carry

    lax.fori_loop(0, 9, body, 0, unroll=9)


def planes_kernel(from_right, plane_right, plane_left, from_left, plane, w, wl, w_out, wl_out, up, down, total):
    row = rows_of()
    even = row % 2 == 0
    total[...] = jnp.zeros_like(total)

    def body(rc, carry):
        got = unpack_plane(lambda i: plane[rc * plane_size(PLANE) + i], PLANE, plane_left[rc], plane_right[rc])
        from_l, from_r = from_left[rc], from_right[rc]
        f = [None] * ITEMS
        for k in range(ITEMS):
            v = w[rc, k] + sides(from_l, from_r, k)
            if k < 9:
                v = v + jnp.where(even, got[k], 0.0)
            elif k < 18:
                v = v + jnp.where(even, sroll(got[k - 9], -1), 0.0)
            elif 27 <= k < 30:
                end = (sroll(got[9], 4), got[9], got[10])[k - 27]
                v = v + jnp.where(even, jnp.where(row < 4, sroll(end, 4), sroll(end, -1)), 0.0)
            f[k] = v
            w_out[rc, k] = v
        magnitude = jnp.abs(f[0])
        for k in range(1, 27):
            magnitude = magnitude + jnp.abs(f[k])
        total[rc // 3] += magnitude
        ups, downs = [], []
        for k in range(0, 27, 2):
            two = f[k + 1] if k + 1 < 27 else None
            ups.append(jnp.where(row < 4, sroll(f[k], 4), sroll(f[31], 4) if two is None else two))
            downs.append(jnp.where(row < 4, f[k], 0.0 if two is None else sroll(two, 4)))
        ups += f[27:31]
        for ref, vs in ((up, ups), (down, downs)):
            for i, v in enumerate(pack(vs)):
                ref[rc * packed_size(len(vs)) + i] = v
        return carry

    lax.fori_loop(0, 9, body, 0, unroll=9)
    got = unpack_plane(lambda i: plane[9 * plane_size(PLANE) + i], 3, plane_left[9], plane_right[9])
    ups, downs = [], []
    for c in range(3):
        load = wl[c] + sides(from_left[9], from_right[9], c) + jnp.where(even, got[c], 0.0)
        ghost = wl[3 + c] + jnp.where(row == 1, sroll(got[c], -4), 0.0)
        ghost = ghost + sides(from_left[9], from_right[9], 3 + c)
        wl_out[c] = load
        wl_out[3 + c] = ghost
        d = load * (1.0 / (total[c] + 1e-06)) / CENTRE
        v = jnp.where(row < 4, sroll(load, 4), 0.0)
        v = jnp.where(row == 4, sroll(ghost, 3), v)
        v = jnp.where(row == 5, sroll(ghost, 2), v)
        ups.append(jnp.where(row >= 6, sroll(d, 4), v))
        downs.append(jnp.where(row < 4, load, jnp.where(row >= 6, sroll(d, 2), 0.0)))
    for ref, vs, size in ((up, ups, packed_size(UPS)), (down, downs, packed_size(DOWNS))):
        for i, v in enumerate(pack(vs)):
            ref[9 * size + i] = v


def piece_rows(n):
    return n + 8 * ((n + 15) // 16)


def split_planes(one, two):
    n = one.shape[0]
    even = lax.broadcasted_iota(jnp.int32, one.shape, 0) % 2 == 0
    first = jnp.where(even, one, pltpu.roll(two, 1, 0))
    second = jnp.where(even, pltpu.roll(one, n - 1, 0), two)
    return first, second


def join_planes(below, above):
    n = below.shape[0]
    even = lax.broadcasted_iota(jnp.int32, below.shape, 0) % 2 == 0
    one = jnp.where(even, below, pltpu.roll(above, 1, 0))
    two = jnp.where(even, pltpu.roll(below, n - 1, 0), above)
    return one, two


def share(at, planes, to_other, to_pair):
    low_of_pair = lax.axis_index("gz") % 2 == 0
    first, second = planes
    n = first.shape[0]
    to_pair[at : at + n] = jnp.where(low_of_pair, second, first)
    to_other[at : at + n] = jnp.where(low_of_pair, first, second)


def shared(at, n, from_other, from_pair):
    low_of_pair = lax.axis_index("gz") % 2 == 0
    other, pair = from_other[at : at + n], from_pair[at : at + n]
    return jnp.where(low_of_pair, other, pair), jnp.where(low_of_pair, pair, other)


def share_vector(load, n, at, to_other, to_pair):
    share(at, split_planes(load(0), load(1)), to_other, to_pair)
    third = load(2)
    at += n
    for i in range(0, n, 16):
        one = third[i : i + 8]
        two = third[i + 8 : i + 16] if i + 8 < n else jnp.zeros_like(one)
        share(at, split_planes(one, two), to_other, to_pair)
        at += 8


def shared_vector(n, at, from_other, from_pair):
    one, two = join_planes(*shared(at, n, from_other, from_pair))
    at += n
    parts = []
    for i in range(0, n, 16):
        parts += join_planes(*shared(at, 8, from_other, from_pair))
        at += 8
    return one, two, jnp.concatenate(parts[: n // 8], axis=0)


def rows_kernel(w, wl, from_low, from_high, whole, q, d, inverse, to_other, to_pair, total, turned, near):
    row = rows_of()
    ghosts = jnp.logical_or(row == 4, row == 5)
    total[...] = jnp.zeros_like(total)

    def body(rc, carry):
        ups = unpack(lambda i: from_low[rc * packed_size(UPS) + i], UPS)
        downs = unpack(lambda i: from_high[rc * packed_size(DOWNS) + i], DOWNS)
        got_ends = [ups[17], sroll(ups[17], 4), sroll(ups[13], 4)]
        own_ends = [w[rc, 30], sroll(w[rc, 30], 4), w[rc, 31]]
        top_sum = jnp.zeros((8, 128), jnp.float32)
        bottom_sum = jnp.zeros((8, 128), jnp.float32)
        for cz in range(3):
            for cy in range(3):
                for cx in range(3):
                    k = cz * 9 + cy * 3 + cx
                    f = sroll(w[rc, k], 4)
                    above, below = ups[k // 2], downs[k // 2]
                    top = jnp.where(row < 4, sroll(above, 4) if k % 2 else above, f)
                    bottom = jnp.where(row < 4, f, below if k % 2 else sroll(below, 4))
                    if cy < 2:
                        at = (cz % 2) * 4 + cy * 2
                        got = ups[14 + cx] if cz < 2 else got_ends[cx]
                        own = w[rc, 27 + cx] if cz < 2 else own_ends[cx]
                        top = top + jnp.where(ghosts, sroll(got, 4 - at), 0.0)
                        bottom = bottom + jnp.where(ghosts, sroll(own, 4 - at), 0.0)
                    whole[rc, k, 0:8] = top
                    whole[rc, k, 8:16] = bottom
                    top_sum = top_sum + jnp.abs(top)
                    bottom_sum = bottom_sum + jnp.abs(bottom)
        total[rc // 3, 0:8] += top_sum
        total[rc // 3, 8:16] += bottom_sum
        return carry

    lax.fori_loop(0, 9, body, 0, unroll=9)
    ups = unpack(lambda i: from_low[9 * packed_size(UPS) + i], 3)
    downs = unpack(lambda i: from_high[9 * packed_size(DOWNS) + i], 3)
    for c in range(3):
        load, ghost = sroll(wl[c], 4), wl[3 + c]
        q[c, 0:8] = jnp.where(row < 4, ups[c], load + jnp.where(ghosts, ups[c], 0.0))
        below = sroll(downs[c], 4)
        below = below + jnp.where(row == 4, sroll(ghost, 3), jnp.where(row == 5, sroll(ghost, 2), 0.0))
        q[c, 8:16] = jnp.where(row < 4, load, below)
        part = 1.0 / (total[c] + 1e-06)
        inverse[c] = part
        d[c, 16:24] = jnp.zeros((8, 128), jnp.float32)
        d[c, 2:18] = part * q[c] / CENTRE
        turned[...] = ups[c]
        d[c, 0:2] = turned[6:8]
        turned[...] = downs[c]
        d[c, 18:20] = turned[6:8]
    for c in range(3):
        fill_near(near, c, d[c], None)
    for r, product in enumerate(apply_to(whole, near)):
        q[r] = q[r] - product
    items = [edge_of(whole, i // 9, i % 9) for i in range(81)] + [q[r] for r in range(3)] + [inverse[r] for r in range(3)]
    packed = pack([v[h : h + 8] for v in items for h in (0, 8)])
    for i in range(0, len(packed), 2):
        share(4 * i, split_planes(packed[i], packed[i + 1]), to_other, to_pair)
    share_vector(lambda c: d[c], 24, EDGES, to_other, to_pair)


def operator_kernel(whole, operator, written):
    written[...] = jnp.zeros_like(written)

    def body(rc, carry):
        for k in range(27):
            for z in range(2):
                v = whole[rc, k, pl.ds(4 + z, 4, stride=2), :]
                operator[k // 9, k // 3 % 3, k % 3, rc // 3, rc % 3, z] = v[:, 0:64]
        return carry

    lax.fori_loop(0, 9, body, 0, unroll=3)


def edge_of(whole, rc, at):
    even = lax.broadcasted_iota(jnp.int32, (16, 128), 0) % 2 == 0
    return jnp.where(even, whole[rc, at], whole[rc, 18 + at])


def fill_near(near, c, own, beyond):
    n = own.shape[0]
    even = lax.broadcasted_iota(jnp.int32, (n, 128), 0) % 2 == 0
    base = (24 - n) // 4
    if beyond is None:
        beyond = jnp.zeros_like(own)
    for cz, v in enumerate((
        jnp.where(even, beyond, pltpu.roll(own, 1, 0)),
        own,
        jnp.where(even, pltpu.roll(own, n - 1, 0), beyond),
    )):
        if base:
            near[cz, c, 0:8] = jnp.zeros((8, 128), jnp.float32)
            near[cz, c, 16:24] = jnp.zeros((8, 128), jnp.float32)
        near[cz, c, base : base + n] = v


def shifted(v):
    return pltpu.roll(v, 1, 1), v, pltpu.roll(v, 127, 1)


def apply_to(whole, near):
    sums = [jnp.zeros((16, 128), jnp.float32) for _ in range(3)]
    for cz in range(3):
        for cy in range(3):
            for c in range(3):
                for cx, moved in enumerate(shifted(near[cz, c, pl.ds(2 * cy, 16), :])):
                    for r in range(3):
                        sums[r] = sums[r] + whole[r * 3 + c, cz * 9 + cy * 3 + cx] * moved
    return sums


def two_steps_kernel(rhos, whole, q, d, inverse, from_other, from_pair, after, q_out, d_out, x_out, to_other, to_pair, near, packed, edges):
    even = rows_of() % 2 == 0
    for i in range(0, packed.shape[0], 2):
        packed[i], packed[i + 1] = join_planes(*shared(4 * i, 8, from_other, from_pair))
    for i, v in enumerate(unpack(lambda i: packed[i], 174)):
        edges[i // 2, 8 * (i % 2) : 8 * (i % 2) + 8] = v
    for c, v in enumerate(shared_vector(24, EDGES, from_other, from_pair)):
        near[0, c] = v
        near[1, c] = d[c]
    own = [jnp.zeros((16, 128), jnp.float32) for _ in range(3)]
    beyond = [jnp.zeros((16, 128), jnp.float32) for _ in range(3)]
    for cy in range(3):
        for c in range(3):
            outer = shifted(near[0, c, pl.ds(2 * cy, 16), :])
            inner = shifted(near[1, c, pl.ds(2 * cy, 16), :])
            for cx in range(3):
                for r in range(3):
                    rc, at = r * 3 + c, cy * 3 + cx
                    own[r] = own[r] + edge_of(whole, rc, at) * outer[cx]
                    beyond[r] = beyond[r] + edges[rc * 9 + at] * inner[cx]
    (same, slope), (same_next, slope_next) = rhos
    q_now, d_now, d_beyond = [], [], []
    for r in range(3):
        q_now.append(q[r] - own[r])
        d_now.append(same * d[r, 2:18] + slope * (inverse[r] * q_now[r]))
        d_beyond.append(same * near[0, r, 2:18] + slope * (edges[84 + r] * (edges[81 + r] - beyond[r])))
        x_out[r] = d[r, 2:18] + d_now[r]
    for r in range(3):
        fill_near(near, r, d_now[r], d_beyond[r])
    for r, product in enumerate(apply_to(whole, near)):
        q_next = q_now[r] - product
        q_out[r] = q_next
        d_out[r] = same_next * d_now[r] + slope_next * (inverse[r] * q_next)
    share_vector(lambda c: d_out[c], 16, 0, to_other, to_pair)


def last_step_kernel(rho, whole, q, d, inverse, x, from_other, from_pair, solution_out, near, turned):
    same, slope = rho
    for c, v in enumerate(shared_vector(16, 0, from_other, from_pair)):
        fill_near(near, c, d[c], v)
    for r, product in enumerate(apply_to(whole, near)):
        d_new = same * d[r] + slope * (inverse[r] * (q[r] - product))
        turned[...] = x[r] + d[r] + d_new
        for z in range(2):
            solution_out[r, z] = turned[pl.ds(4 + z, 4, stride=2), :][:, 0:64]


def shape(*dims):
    return jax.ShapeDtypeStruct(dims, jnp.float32)


def along(block, axes, distances):
    sizes = [lax.axis_size(a) for a in axes]
    route = []
    for source in itertools.product(*[range(n) for n in sizes]):
        target = [i + s for i, s in zip(source, distances)]
        if all(0 <= i < n for i, n in zip(target, sizes)):
            flat = [functools.reduce(lambda t, p: t * p[1] + p[0], zip(at, sizes), 0) for at in (source, target)]
            route.append(tuple(flat))
    return lax.ppermute(block, axes, route)


def exchanged(block, axis, first):
    n = lax.axis_size(axis)
    pairs = [(i, i + 1) for i in range(first, n - 1, 2)]
    return lax.ppermute(block, axis, pairs + [(j, i) for i, j in pairs])


def shards(blocks, classes, residual):
    w_shape, wl_shape = shape(9, ITEMS, 8, 128), shape(6, 8, 128)
    side = shape(10, 8, 128)
    w, wl, right, left, plane, plane_right, plane_left_sent = pl.pallas_call(
        coarsen_kernel,
        in_specs=[HBM] * 3,
        out_specs=[VMEM] * 7,
        out_shape=[w_shape, wl_shape, side, side, shape(9 * plane_size(PLANE) + plane_size(3), 8, 128), side, side],
        scratch_shapes=[
            pltpu.VMEM((9, 3, 3, 3, 4, 8, 128), jnp.float32),
            pltpu.VMEM((4, 8, 128), jnp.int32),
            pltpu.VMEM((3, 4, 8, 128), jnp.float32),
            pltpu.VMEM((4, 9, 8, 128), jnp.float32),
            pltpu.SemaphoreType.DMA((11,)),
        ],
        compiler_params=LIMIT,
    )(*(pltpu.with_memory_space_constraint(v, pltpu.HBM) for v in (blocks, classes, residual)))
    plane_left = along(plane_right, ("gx", "gz"), (1, 1))
    from_left = along(right, ("gx",), (1,))
    plane_right = along(plane_left_sent, ("gx", "gz"), (-1, 1))
    from_right = along(left, ("gx",), (-1,))
    plane = along(plane, ("gz",), (1,))
    w, wl, up, down = pl.pallas_call(
        planes_kernel,
        in_specs=[VMEM] * 7,
        out_specs=[VMEM] * 4,
        out_shape=[w_shape, wl_shape, shape(9 * packed_size(UPS) + packed_size(3), 8, 128), shape(9 * packed_size(DOWNS) + packed_size(3), 8, 128)],
        scratch_shapes=[pltpu.VMEM((3, 8, 128), jnp.float32)],
        compiler_params=LIMIT,
    )(from_right, plane_right, plane_left, from_left, plane, w, wl)
    from_high = along(down, ("gy",), (-1,))
    from_low = along(up, ("gy",), (1,))
    whole_shape, vector = shape(9, 27, 16, 128), shape(3, 16, 128)
    near = pltpu.VMEM((3, 3, 24, 128), jnp.float32)
    whole, q, d, inverse, to_other, to_pair = pl.pallas_call(
        rows_kernel,
        in_specs=[VMEM] * 4,
        out_specs=[VMEM] * 6,
        out_shape=[whole_shape, vector, shape(3, 24, 128), vector] + [shape(EDGES + piece_rows(24), 128)] * 2,
        scratch_shapes=[pltpu.VMEM((3, 16, 128), jnp.float32), pltpu.VMEM((8, 128), jnp.float32), near],
        compiler_params=LIMIT,
    )(w, wl, from_low, from_high)
    operator, written = pl.pallas_call(
        operator_kernel,
        in_specs=[VMEM],
        out_specs=[VMEM] * 2,
        out_shape=[shape(3, 3, 3, 3, 3, 2, 4, 64), shape(8, 128)],
        compiler_params=LIMIT,
        cost_estimate=pl.CostEstimate(flops=500000, bytes_accessed=3000000, transcendentals=0),
    )(whole)
    rhos, rho_now = [], 1.0 / SIGMA
    for _ in range(STEPS - 1):
        rho_next = 1.0 / (2.0 * SIGMA - rho_now)
        rhos.append((rho_next * rho_now, 2.0 * rho_next / HALF))
        rho_now = rho_next
    from_other, from_pair = exchanged(to_other, "gz", 1), exchanged(to_pair, "gz", 0)
    q, d, x, to_other, to_pair = pl.pallas_call(
        functools.partial(two_steps_kernel, rhos[:2]),
        in_specs=[VMEM] * 7,
        out_specs=[VMEM] * 5,
        out_shape=[vector] * 3 + [shape(piece_rows(16), 128)] * 2,
        scratch_shapes=[near, pltpu.VMEM((96, 8, 128), jnp.float32), pltpu.VMEM((87, 16, 128), jnp.float32)],
        compiler_params=LIMIT,
    )(whole, q, d, inverse, from_other, from_pair, written)
    from_other, from_pair = exchanged(to_other, "gz", 1), exchanged(to_pair, "gz", 0)
    coarse_solution = pl.pallas_call(
        functools.partial(last_step_kernel, rhos[2]),
        in_specs=[VMEM] * 7,
        out_specs=VMEM,
        out_shape=shape(3, 2, 4, 64),
        scratch_shapes=[near, pltpu.VMEM((16, 128), jnp.float32)],
        compiler_params=LIMIT,
    )(whole, q, d, inverse, x, from_other, from_pair)
    return operator, coarse_solution


def solution(mesh):
    placed = (
        P(None, None, None, None, None, "gz", "gy", "gx"),
        P("gz", "gy", "gx"),
        P(None, "gz", "gy", "gx"),
    )
    return jax.shard_map(
        shards,
        mesh=mesh,
        in_specs=placed,
        out_specs=(P(None, None, None, None, None, "gz", "gy", "gx"), P(None, "gz", "gy", "gx")),
        check_vma=False,
    )
```

```python
import functools
import itertools

import jax
import jax.numpy as jnp
from jax import lax
from jax.experimental import pallas as pl
from jax.experimental.pallas import tpu as pltpu
from jax.sharding import PartitionSpec as P

STEPS = 4
CHEB_LOW = 0.1
CHEB_HIGH = 1.0
CENTRE = (CHEB_HIGH + CHEB_LOW) / 2.0
HALF = (CHEB_HIGH - CHEB_LOW) / 2.0
SIGMA = CENTRE / HALF

ITEMS = 32
PLANE = 11
UPS, DOWNS = 18, 14
AHEAD = 3
EDGES = 8 * 48
VMEM = pl.BlockSpec(memory_space=pltpu.VMEM)
HBM = pl.BlockSpec(memory_space=pltpu.HBM)
LIMIT = pltpu.CompilerParams(vmem_limit_bytes=40 * 1024 * 1024)


def lanes_of():
    return lax.broadcasted_iota(jnp.int32, (8, 128), 1)


def rows_of():
    return lax.broadcasted_iota(jnp.int32, (8, 128), 0)


def lroll(v, s):
    s = s % 128
    return v if s == 0 else pltpu.roll(v, s, 1)


def sroll(v, s):
    s = s % 8
    return v if s == 0 else pltpu.roll(v, s, 0)


def halo_slots():
    lane = lanes_of()
    left = jnp.where(jnp.logical_and(lane >= 61, lane < 121), lax.div(lane - 61, 3), -1)
    return jnp.where(lane < 60, lax.div(lane, 3), left)


def packed_size(n):
    return (n + 1) // 2 + (n + 19) // 20


def pack(vs):
    lane = lanes_of()
    slots = halo_slots()
    out = []
    for i in range(0, len(vs), 2):
        other = lroll(vs[i + 1], 64) if i + 1 < len(vs) else jnp.zeros_like(vs[i])
        out.append(jnp.where(lane < 64, vs[i], other))
    for base in range(0, len(vs), 20):
        held = jnp.zeros((8, 128), jnp.float32)
        for j, v in enumerate(vs[base : base + 20]):
            held = jnp.where(slots == j, lroll(v, 3 * j - 64), held)
        out.append(held)
    return out


def unpack(load, n):
    lane = lanes_of()
    edge = jnp.logical_or(jnp.logical_and(lane >= 64, lane < 67), lane >= 125)
    mains = (n + 1) // 2
    out = []
    for i in range(n):
        main = load(i // 2)
        if i % 2:
            main = lroll(main, 64)
        held = lroll(load(mains + i // 20), 64 - 3 * (i % 20))
        out.append(jnp.where(lane < 64, main, jnp.where(edge, held, 0.0)))
    return out


def right_slots():
    return lax.div(lanes_of(), 4)


def left_slots():
    lane = lanes_of()
    return lax.div(jnp.where(lane < 67, lane + 61, lane - 67), 4)


def pack_sides(vs):
    rights, lefts = right_slots(), left_slots()
    right = jnp.zeros((8, 128), jnp.float32)
    left = jnp.zeros((8, 128), jnp.float32)
    for j, v in enumerate(vs):
        moved = lroll(v, 4 * j - 61)
        right = jnp.where(rights == j, moved, right)
        left = jnp.where(lefts == j, moved, left)
    return right, left


def sides(from_left, from_right, j):
    lane = lanes_of()
    both = lroll(jnp.where(right_slots() == j, from_left, from_right), -(4 * j + 3))
    ends = jnp.logical_or(jnp.logical_or(lane >= 125, lane == 0), jnp.logical_and(lane >= 64, lane < 67))
    return jnp.where(ends, both, 0.0)


def plane_size(n):
    return n // 2 + 1


def pack_plane(vs, right):
    lane = lanes_of()
    out = [jnp.where(lane < 64, vs[i], lroll(vs[i + 1], 64)) for i in range(0, len(vs) - 1, 2)]
    return out + [jnp.where(lane < 64, vs[-1], lroll(right, 64))]


def unpack_plane(load, n, from_left, from_right):
    lane = lanes_of()
    beyond = jnp.logical_and(jnp.logical_and(lane >= 67, lane < 64 + 4 * n), lax.rem(lane, 4) == 3)
    from_right = from_right + jnp.where(beyond, load(n // 2), 0.0)
    out = []
    for i in range(n):
        main = load(i // 2)
        if i % 2:
            main = lroll(main, 64)
        out.append(jnp.where(lane < 64, main, 0.0) + sides(from_left, from_right, i))
    return out


def coarsen_kernel(blocks_in, classes_in, residual_in, w, wl, right, left, plane, plane_right, plane_left, blocks, classes, residual, scale, sems):
    def fetch(i):
        source = blocks_in.at[:, :, :, i // 3, i % 3]
        return pltpu.make_async_copy(source, blocks.at[i], sems.at[i])

    classes_copy = pltpu.make_async_copy(classes_in, classes, sems.at[9])
    residual_copy = pltpu.make_async_copy(residual_in, residual, sems.at[10])
    classes_copy.start()
    fetch(0).start()
    residual_copy.start()
    for i in range(1, AHEAD):
        fetch(i).start()
    gx, gy, gz = (lax.axis_index(a) for a in ("gx", "gy", "gz"))
    lane, row = lanes_of(), rows_of()
    even = row % 2 == 0
    not_last_x = (gx < lax.axis_size("gx") - 1).astype(jnp.float32)
    last_x = gx == lax.axis_size("gx") - 1
    not_last_y = (gy < lax.axis_size("gy") - 1).astype(jnp.float32)
    keep_y = jnp.logical_or(row < 6, gy < lax.axis_size("gy") - 1)
    inner = lane < 64
    upper_x = jnp.logical_and(inner, jnp.logical_or(lane < 63, jnp.logical_not(last_x)))
    after_x = jnp.logical_and(lane > 0, jnp.logical_or(inner, jnp.logical_and(lane == 64, jnp.logical_not(last_x))))
    apart = jnp.where(inner, 2 * lane, 2 * lane - 127)
    not_last_z = (gz < lax.axis_size("gz") - 1).astype(jnp.float32)
    pick = jnp.where(lane < 64, 2 * lane, 127) % 128

    def squeeze(v):
        g = jnp.take_along_axis(v, pick, axis=1, mode="promise_in_bounds")
        return jnp.where(lane <= 64, g, 0.0)

    def coarsen(step):
        ydone = {}
        for ox in range(3):
            slots = {}
            for oy in range(3):
                kind = (2 if oy == 0 else 0) + (1 if ox == 0 else 0)
                s = [[None] * 4 for _ in range(3)]
                for oz in range(3):
                    for z in range(4):
                        factor = scale[kind, 5 + z if oz == 1 else 4 if (z == 0 and oz == 0) else z]
                        s[oz][z] = blocks[step, oz, oy, ox, z] * factor
                a1, b1 = s[0][1] + s[1][1], s[2][1] + s[1][1]
                a3, b3 = s[0][3] + s[1][3], s[2][3] + s[1][3]
                slots[0, 0, oy] = s[0][0]
                slots[1, 0, oy] = s[0][0] + s[2][0] + s[1][0] + a1
                slots[2, 0, oy] = s[2][0] + b1
                slots[0, 1, oy] = s[0][2] + a1
                slots[1, 1, oy] = s[0][2] + s[2][2] + s[1][2] + b1 + a3
                slots[2, 1, oy] = (s[2][2] + b3) * not_last_z
                slots[3, 0, oy] = a3
                slots[3, 1, oy] = b3
            beyond = [None, None]
            for slot in range(4):
                ev, od = [], []
                for oy in range(3):
                    z0, z1 = slots[slot, 0, oy], slots[slot, 1, oy]
                    ev.append(jnp.where(even, z0, sroll(z1, 1)))
                    od.append(jnp.where(even, sroll(z0, -1), z1))
                half = 0.5 * od[1]
                a, b = od[0] + half, od[2] + half
                a_before, b_before = sroll(a, 2), sroll(b, 2)
                ydone[slot * 3, ox] = ev[0] + jnp.where(row < 2, 0.0, a_before)
                ydone[slot * 3 + 1, ox] = ev[0] + ev[2] + (ev[1] + ev[1]) + a + jnp.where(row < 2, 0.0, b_before)
                ydone[slot * 3 + 2, ox] = jnp.where(keep_y, ev[2] + b, 0.0)
                if slot % 2 == 0:
                    beyond[slot // 2] = jnp.where(row < 2, a_before, sroll(b, 4))
                else:
                    ends = jnp.where(row < 6, sroll(a, 6), b)
                    beyond[slot // 2] = jnp.where(row < 4, beyond[slot // 2], ends) * not_last_y
            ydone[12, ox], ydone[13, ox] = beyond
        kept, sent, rows = [None] * ITEMS, [None] * PLANE, {}
        for i in range(14):
            v = [jnp.take_along_axis(ydone[i, ox], apart, axis=1, mode="promise_in_bounds") for ox in range(3)]
            half = 0.5 * v[1]
            a, b = v[0] + half, v[2] + half
            lower = jnp.where(inner, v[0], 0.0) + jnp.where(after_x, lroll(a, 65), 0.0)
            middle = jnp.where(inner, v[0] + v[2] + (v[1] + v[1]) + lroll(a, 64), 0.0) + jnp.where(after_x, lroll(b, 65), 0.0)
            upper = jnp.where(upper_x, v[2] + lroll(b, 64), 0.0)
            for cx, v in enumerate((lower, middle, upper)):
                if i < 9:
                    kept[i * 3 + cx] = v
                elif i < 12:
                    sent[(i - 9) * 3 + cx] = v
                elif i == 12:
                    kept[27 + cx] = v
                else:
                    rows[cx] = v
        kept[30] = jnp.where(row < 4, rows[0], sroll(rows[1], 4))
        sent[9] = jnp.where(row < 4, sroll(rows[0], 4), rows[1])
        kept[31] = sent[10] = rows[2]
        for i, v in enumerate(kept):
            w[step, i] = v
        right[step], left[step] = pack_sides(kept)
        sent_right, plane_left[step] = pack_sides(sent)
        plane_right[step] = sent_right
        for i, v in enumerate(pack_plane(sent, sent_right)):
            plane[step * plane_size(PLANE) + i] = v

    def scales():
        low_x = jnp.where(jnp.logical_and(lane == 0, gx == 0), 0.0, 1.0)
        low_y = jnp.where(jnp.logical_and(row == 0, gy == 0), 0.0, 1.0)
        low_z = (gz > 0).astype(jnp.float32)
        for z in range(4):
            k = classes[z].astype(jnp.float32)
            s = 0.125 * (0.05 + 0.95 * (k * k * k) / 27.0)
            for cy in range(2):
                for cx in range(2):
                    v = s
                    if cy:
                        v = v * low_y
                    if cx:
                        v = v * low_x
                    scale[cy * 2 + cx, z] = v
                    scale[cy * 2 + cx, 5 + z] = (0.5 if z % 2 else 2.0) * v
                    if z == 0:
                        scale[cy * 2 + cx, 4] = v * low_z

    def loads():
        items = []
        for c in range(3):
            f = [residual[c, z] for z in range(4)]
            planes = [f[0] + 0.5 * f[1], 0.5 * f[1] + f[2] + 0.5 * f[3], 0.5 * f[3]]
            full, beyond = [], []
            for v in planes:
                h = 0.5 * v
                before = sroll(h, 1)
                full.append(v + sroll(h, -1) + jnp.where(row == 0, 0.0, before))
                beyond.append(h * not_last_y)
            main = jnp.where(even, full[0], sroll(full[1], 1))
            ghost = jnp.where(even, full[2], 0.0)
            for z in range(3):
                ghost = jnp.where(row == 1 + 2 * z, sroll(beyond[z], 2 + 2 * z), ghost)
            items.append((main, ghost))
        vs = []
        for v in [m for m, _ in items] + [g for _, g in items]:
            h = 0.5 * v
            v = v + lroll(h, -1) + jnp.where(lane == 0, 0.0, lroll(h, 1))
            v = jnp.where(lane == 127, h * not_last_x, v)
            vs.append(squeeze(v))
        for i, v in enumerate(vs):
            wl[i] = v

        right[9], left[9] = pack_sides(vs)
        sent_right, plane_left[9] = pack_sides(vs[3:])
        plane_right[9] = sent_right
        for i, v in enumerate(pack_plane(vs[3:], sent_right)):
            plane[9 * plane_size(PLANE) + i] = v

    classes_copy.wait()
    scales()
    residual_copy.wait()
    loads()

    def body(step, carry):
        fetch(step).wait()

        @pl.when(step + AHEAD < 9)
        def _():
            fetch(step + AHEAD).start()

        coarsen(step)
        return carry

    lax.fori_loop(0, 9, body, 0, unroll=9)


def planes_kernel(from_right, plane_right, plane_left, from_left, plane, w, wl, w_out, wl_out, up, down, total):
    row = rows_of()
    even = row % 2 == 0
    total[...] = jnp.zeros_like(total)

    def body(rc, carry):
        got = unpack_plane(lambda i: plane[rc * plane_size(PLANE) + i], PLANE, plane_left[rc], plane_right[rc])
        from_l, from_r = from_left[rc], from_right[rc]
        f = [None] * ITEMS
        for k in range(ITEMS):
            v = w[rc, k] + sides(from_l, from_r, k)
            if k < 9:
                v = v + jnp.where(even, got[k], 0.0)
            elif k < 18:
                v = v + jnp.where(even, sroll(got[k - 9], -1), 0.0)
            elif 27 <= k < 30:
                end = (sroll(got[9], 4), got[9], got[10])[k - 27]
                v = v + jnp.where(even, jnp.where(row < 4, sroll(end, 4), sroll(end, -1)), 0.0)
            f[k] = v
            w_out[rc, k] = v
        magnitude = jnp.abs(f[0])
        for k in range(1, 27):
            magnitude = magnitude + jnp.abs(f[k])
        total[rc // 3] += magnitude
        ups, downs = [], []
        for k in range(0, 27, 2):
            two = f[k + 1] if k + 1 < 27 else None
            ups.append(jnp.where(row < 4, sroll(f[k], 4), sroll(f[31], 4) if two is None else two))
            downs.append(jnp.where(row < 4, f[k], 0.0 if two is None else sroll(two, 4)))
        ups += f[27:31]
        for ref, vs in ((up, ups), (down, downs)):
            for i, v in enumerate(pack(vs)):
                ref[rc * packed_size(len(vs)) + i] = v
        return carry

    lax.fori_loop(0, 9, body, 0, unroll=9)
    got = unpack_plane(lambda i: plane[9 * plane_size(PLANE) + i], 3, plane_left[9], plane_right[9])
    ups, downs = [], []
    for c in range(3):
        load = wl[c] + sides(from_left[9], from_right[9], c) + jnp.where(even, got[c], 0.0)
        ghost = wl[3 + c] + jnp.where(row == 1, sroll(got[c], -4), 0.0)
        ghost = ghost + sides(from_left[9], from_right[9], 3 + c)
        wl_out[c] = load
        wl_out[3 + c] = ghost
        d = load * (1.0 / (total[c] + 1e-06)) / CENTRE
        v = jnp.where(row < 4, sroll(load, 4), 0.0)
        v = jnp.where(row == 4, sroll(ghost, 3), v)
        v = jnp.where(row == 5, sroll(ghost, 2), v)
        ups.append(jnp.where(row >= 6, sroll(d, 4), v))
        downs.append(jnp.where(row < 4, load, jnp.where(row >= 6, sroll(d, 2), 0.0)))
    for ref, vs, size in ((up, ups, packed_size(UPS)), (down, downs, packed_size(DOWNS))):
        for i, v in enumerate(pack(vs)):
            ref[9 * size + i] = v


def piece_rows(n):
    return n + 8 * ((n + 15) // 16)


def split_planes(one, two):
    n = one.shape[0]
    even = lax.broadcasted_iota(jnp.int32, one.shape, 0) % 2 == 0
    first = jnp.where(even, one, pltpu.roll(two, 1, 0))
    second = jnp.where(even, pltpu.roll(one, n - 1, 0), two)
    return first, second


def join_planes(below, above):
    n = below.shape[0]
    even = lax.broadcasted_iota(jnp.int32, below.shape, 0) % 2 == 0
    one = jnp.where(even, below, pltpu.roll(above, 1, 0))
    two = jnp.where(even, pltpu.roll(below, n - 1, 0), above)
    return one, two


def share(at, planes, to_other, to_pair):
    low_of_pair = lax.axis_index("gz") % 2 == 0
    first, second = planes
    n = first.shape[0]
    to_pair[at : at + n] = jnp.where(low_of_pair, second, first)
    to_other[at : at + n] = jnp.where(low_of_pair, first, second)


def shared(at, n, from_other, from_pair):
    low_of_pair = lax.axis_index("gz") % 2 == 0
    other, pair = from_other[at : at + n], from_pair[at : at + n]
    return jnp.where(low_of_pair, other, pair), jnp.where(low_of_pair, pair, other)


def share_vector(load, n, at, to_other, to_pair):
    share(at, split_planes(load(0), load(1)), to_other, to_pair)
    third = load(2)
    at += n
    for i in range(0, n, 16):
        one = third[i : i + 8]
        two = third[i + 8 : i + 16] if i + 8 < n else jnp.zeros_like(one)
        share(at, split_planes(one, two), to_other, to_pair)
        at += 8


def shared_vector(n, at, from_other, from_pair):
    one, two = join_planes(*shared(at, n, from_other, from_pair))
    at += n
    parts = []
    for i in range(0, n, 16):
        parts += join_planes(*shared(at, 8, from_other, from_pair))
        at += 8
    return one, two, jnp.concatenate(parts[: n // 8], axis=0)


def rows_kernel(from_high, from_low, w, wl, whole, q, d, inverse, to_other, to_pair, total, turned, near):
    row = rows_of()
    ghosts = jnp.logical_or(row == 4, row == 5)
    total[...] = jnp.zeros_like(total)

    def body(rc, carry):
        ups = unpack(lambda i: from_low[rc * packed_size(UPS) + i], UPS)
        downs = unpack(lambda i: from_high[rc * packed_size(DOWNS) + i], DOWNS)
        got_ends = [ups[17], sroll(ups[17], 4), sroll(ups[13], 4)]
        own_ends = [w[rc, 30], sroll(w[rc, 30], 4), w[rc, 31]]
        top_sum = jnp.zeros((8, 128), jnp.float32)
        bottom_sum = jnp.zeros((8, 128), jnp.float32)
        for cz in range(3):
            for cy in range(3):
                for cx in range(3):
                    k = cz * 9 + cy * 3 + cx
                    f = sroll(w[rc, k], 4)
                    above, below = ups[k // 2], downs[k // 2]
                    top = jnp.where(row < 4, sroll(above, 4) if k % 2 else above, f)
                    bottom = jnp.where(row < 4, f, below if k % 2 else sroll(below, 4))
                    if cy < 2:
                        at = (cz % 2) * 4 + cy * 2
                        got = ups[14 + cx] if cz < 2 else got_ends[cx]
                        own = w[rc, 27 + cx] if cz < 2 else own_ends[cx]
                        top = top + jnp.where(ghosts, sroll(got, 4 - at), 0.0)
                        bottom = bottom + jnp.where(ghosts, sroll(own, 4 - at), 0.0)
                    whole[rc, k, 0:8] = top
                    whole[rc, k, 8:16] = bottom
                    top_sum = top_sum + jnp.abs(top)
                    bottom_sum = bottom_sum + jnp.abs(bottom)
        total[rc // 3, 0:8] += top_sum
        total[rc // 3, 8:16] += bottom_sum
        return carry

    lax.fori_loop(0, 9, body, 0, unroll=9)
    ups = unpack(lambda i: from_low[9 * packed_size(UPS) + i], 3)
    downs = unpack(lambda i: from_high[9 * packed_size(DOWNS) + i], 3)
    for c in range(3):
        load, ghost = sroll(wl[c], 4), wl[3 + c]
        q[c, 0:8] = jnp.where(row < 4, ups[c], load + jnp.where(ghosts, ups[c], 0.0))
        below = sroll(downs[c], 4)
        below = below + jnp.where(row == 4, sroll(ghost, 3), jnp.where(row == 5, sroll(ghost, 2), 0.0))
        q[c, 8:16] = jnp.where(row < 4, load, below)
        part = 1.0 / (total[c] + 1e-06)
        inverse[c] = part
        d[c, 16:24] = jnp.zeros((8, 128), jnp.float32)
        d[c, 2:18] = part * q[c] / CENTRE
        turned[...] = ups[c]
        d[c, 0:2] = turned[6:8]
        turned[...] = downs[c]
        d[c, 18:20] = turned[6:8]
    for c in range(3):
        fill_near(near, c, d[c], None)
    for r, product in enumerate(apply_to(whole, near)):
        q[r] = q[r] - product
    items = [edge_of(whole, i // 9, i % 9) for i in range(81)] + [q[r] for r in range(3)] + [inverse[r] for r in range(3)]
    packed = pack([v[h : h + 8] for v in items for h in (0, 8)])
    for i in range(0, len(packed), 2):
        share(4 * i, split_planes(packed[i], packed[i + 1]), to_other, to_pair)
    share_vector(lambda c: d[c], 24, EDGES, to_other, to_pair)


def operator_kernel(whole, operator, written):
    written[...] = jnp.zeros_like(written)

    def body(rc, carry):
        for k in range(27):
            for z in range(2):
                v = whole[rc, k, pl.ds(4 + z, 4, stride=2), :]
                operator[k // 9, k // 3 % 3, k % 3, rc // 3, rc % 3, z] = v[:, 0:64]
        return carry

    lax.fori_loop(0, 9, body, 0, unroll=3)


def edge_of(whole, rc, at):
    even = lax.broadcasted_iota(jnp.int32, (16, 128), 0) % 2 == 0
    return jnp.where(even, whole[rc, at], whole[rc, 18 + at])


def fill_near(near, c, own, beyond):
    n = own.shape[0]
    even = lax.broadcasted_iota(jnp.int32, (n, 128), 0) % 2 == 0
    base = (24 - n) // 4
    if beyond is None:
        beyond = jnp.zeros_like(own)
    for cz, v in enumerate((
        jnp.where(even, beyond, pltpu.roll(own, 1, 0)),
        own,
        jnp.where(even, pltpu.roll(own, n - 1, 0), beyond),
    )):
        if base:
            near[cz, c, 0:8] = jnp.zeros((8, 128), jnp.float32)
            near[cz, c, 16:24] = jnp.zeros((8, 128), jnp.float32)
        near[cz, c, base : base + n] = v


def shifted(v):
    return pltpu.roll(v, 1, 1), v, pltpu.roll(v, 127, 1)


def apply_to(whole, near):
    sums = [jnp.zeros((16, 128), jnp.float32) for _ in range(3)]
    for cz in range(3):
        for cy in range(3):
            for c in range(3):
                for cx, moved in enumerate(shifted(near[cz, c, pl.ds(2 * cy, 16), :])):
                    for r in range(3):
                        sums[r] = sums[r] + whole[r * 3 + c, cz * 9 + cy * 3 + cx] * moved
    return sums


def two_steps_kernel(rhos, whole, q, d, inverse, from_other, from_pair, after, q_out, d_out, x_out, to_other, to_pair, near, packed, edges):
    even = rows_of() % 2 == 0
    for i in range(0, packed.shape[0], 2):
        packed[i], packed[i + 1] = join_planes(*shared(4 * i, 8, from_other, from_pair))
    for i, v in enumerate(unpack(lambda i: packed[i], 174)):
        edges[i // 2, 8 * (i % 2) : 8 * (i % 2) + 8] = v
    for c, v in enumerate(shared_vector(24, EDGES, from_other, from_pair)):
        near[0, c] = v
        near[1, c] = d[c]
    own = [jnp.zeros((16, 128), jnp.float32) for _ in range(3)]
    beyond = [jnp.zeros((16, 128), jnp.float32) for _ in range(3)]
    for cy in range(3):
        for c in range(3):
            outer = shifted(near[0, c, pl.ds(2 * cy, 16), :])
            inner = shifted(near[1, c, pl.ds(2 * cy, 16), :])
            for cx in range(3):
                for r in range(3):
                    rc, at = r * 3 + c, cy * 3 + cx
                    own[r] = own[r] + edge_of(whole, rc, at) * outer[cx]
                    beyond[r] = beyond[r] + edges[rc * 9 + at] * inner[cx]
    (same, slope), (same_next, slope_next) = rhos
    q_now, d_now, d_beyond = [], [], []
    for r in range(3):
        q_now.append(q[r] - own[r])
        d_now.append(same * d[r, 2:18] + slope * (inverse[r] * q_now[r]))
        d_beyond.append(same * near[0, r, 2:18] + slope * (edges[84 + r] * (edges[81 + r] - beyond[r])))
        x_out[r] = d[r, 2:18] + d_now[r]
    for r in range(3):
        fill_near(near, r, d_now[r], d_beyond[r])
    for r, product in enumerate(apply_to(whole, near)):
        q_next = q_now[r] - product
        q_out[r] = q_next
        d_out[r] = same_next * d_now[r] + slope_next * (inverse[r] * q_next)
    share_vector(lambda c: d_out[c], 16, 0, to_other, to_pair)


def last_step_kernel(rho, whole, q, d, inverse, x, from_other, from_pair, solution_out, near, turned):
    same, slope = rho
    for c, v in enumerate(shared_vector(16, 0, from_other, from_pair)):
        fill_near(near, c, d[c], v)
    for r, product in enumerate(apply_to(whole, near)):
        d_new = same * d[r] + slope * (inverse[r] * (q[r] - product))
        turned[...] = x[r] + d[r] + d_new
        for z in range(2):
            solution_out[r, z] = turned[pl.ds(4 + z, 4, stride=2), :][:, 0:64]


def shape(*dims):
    return jax.ShapeDtypeStruct(dims, jnp.float32)


def along(block, axes, distances):
    sizes = [lax.axis_size(a) for a in axes]
    route = []
    for source in itertools.product(*[range(n) for n in sizes]):
        target = [i + s for i, s in zip(source, distances)]
        if all(0 <= i < n for i, n in zip(target, sizes)):
            flat = [functools.reduce(lambda t, p: t * p[1] + p[0], zip(at, sizes), 0) for at in (source, target)]
            route.append(tuple(flat))
    return lax.ppermute(block, axes, route)


def exchanged(block, axis, first):
    n = lax.axis_size(axis)
    pairs = [(i, i + 1) for i in range(first, n - 1, 2)]
    return lax.ppermute(block, axis, pairs + [(j, i) for i, j in pairs])


def shards(blocks, classes, residual):
    w_shape, wl_shape = shape(9, ITEMS, 8, 128), shape(6, 8, 128)
    side = shape(10, 8, 128)
    w, wl, right, left, plane, plane_right, plane_left_sent = pl.pallas_call(
        coarsen_kernel,
        in_specs=[HBM] * 3,
        out_specs=[VMEM] * 7,
        out_shape=[w_shape, wl_shape, side, side, shape(9 * plane_size(PLANE) + plane_size(3), 8, 128), side, side],
        scratch_shapes=[
            pltpu.VMEM((9, 3, 3, 3, 4, 8, 128), jnp.float32),
            pltpu.VMEM((4, 8, 128), jnp.int32),
            pltpu.VMEM((3, 4, 8, 128), jnp.float32),
            pltpu.VMEM((4, 9, 8, 128), jnp.float32),
            pltpu.SemaphoreType.DMA((11,)),
        ],
        compiler_params=LIMIT,
    )(*(pltpu.with_memory_space_constraint(v, pltpu.HBM) for v in (blocks, classes, residual)))
    plane_left = along(plane_right, ("gx", "gz"), (1, 1))
    from_left = along(right, ("gx",), (1,))
    plane_right = along(plane_left_sent, ("gx", "gz"), (-1, 1))
    from_right = along(left, ("gx",), (-1,))
    plane = along(plane, ("gz",), (1,))
    w, wl, up, down = pl.pallas_call(
        planes_kernel,
        in_specs=[VMEM] * 7,
        out_specs=[VMEM] * 4,
        out_shape=[w_shape, wl_shape, shape(9 * packed_size(UPS) + packed_size(3), 8, 128), shape(9 * packed_size(UPS) + packed_size(3), 8, 128)],
        scratch_shapes=[pltpu.VMEM((3, 8, 128), jnp.float32)],
        compiler_params=LIMIT,
    )(from_right, plane_right, plane_left, from_left, plane, w, wl)
    from_high = along(down, ("gy",), (-1,))
    from_low = along(up, ("gy",), (1,))
    whole_shape, vector = shape(9, 27, 16, 128), shape(3, 16, 128)
    near = pltpu.VMEM((3, 3, 24, 128), jnp.float32)
    whole, q, d, inverse, to_other, to_pair = pl.pallas_call(
        rows_kernel,
        in_specs=[VMEM] * 4,
        out_specs=[VMEM] * 6,
        out_shape=[whole_shape, vector, shape(3, 24, 128), vector] + [shape(EDGES + piece_rows(24), 128)] * 2,
        scratch_shapes=[pltpu.VMEM((3, 16, 128), jnp.float32), pltpu.VMEM((8, 128), jnp.float32), near],
        compiler_params=LIMIT,
    )(from_high, from_low, w, wl)
    operator, written = pl.pallas_call(
        operator_kernel,
        in_specs=[VMEM],
        out_specs=[VMEM] * 2,
        out_shape=[shape(3, 3, 3, 3, 3, 2, 4, 64), shape(8, 128)],
        compiler_params=LIMIT,
        cost_estimate=pl.CostEstimate(flops=500000, bytes_accessed=3000000, transcendentals=0),
    )(whole)
    rhos, rho_now = [], 1.0 / SIGMA
    for _ in range(STEPS - 1):
        rho_next = 1.0 / (2.0 * SIGMA - rho_now)
        rhos.append((rho_next * rho_now, 2.0 * rho_next / HALF))
        rho_now = rho_next
    from_other, from_pair = exchanged(to_other, "gz", 1), exchanged(to_pair, "gz", 0)
    q, d, x, to_other, to_pair = pl.pallas_call(
        functools.partial(two_steps_kernel, rhos[:2]),
        in_specs=[VMEM] * 7,
        out_specs=[VMEM] * 5,
        out_shape=[vector] * 3 + [shape(piece_rows(16), 128)] * 2,
        scratch_shapes=[near, pltpu.VMEM((96, 8, 128), jnp.float32), pltpu.VMEM((87, 16, 128), jnp.float32)],
        compiler_params=LIMIT,
    )(whole, q, d, inverse, from_other, from_pair, written)
    from_other, from_pair = exchanged(to_other, "gz", 1), exchanged(to_pair, "gz", 0)
    coarse_solution = pl.pallas_call(
        functools.partial(last_step_kernel, rhos[2]),
        in_specs=[VMEM] * 7,
        out_specs=VMEM,
        out_shape=shape(3, 2, 4, 64),
        scratch_shapes=[near, pltpu.VMEM((16, 128), jnp.float32)],
        compiler_params=LIMIT,
    )(whole, q, d, inverse, x, from_other, from_pair)
    return operator, coarse_solution


def solution(mesh):
    placed = (
        P(None, None, None, None, None, "gz", "gy", "gx"),
        P("gz", "gy", "gx"),
        P(None, "gz", "gy", "gx"),
    )
    return jax.shard_map(
        shards,
        mesh=mesh,
        in_specs=placed,
        out_specs=(P(None, None, None, None, None, "gz", "gy", "gx"), P(None, "gz", "gy", "gx")),
        check_vma=False,
    )
```

```python
import functools
import itertools

import jax
import jax.numpy as jnp
from jax import lax
from jax.experimental import pallas as pl
from jax.experimental.pallas import tpu as pltpu
from jax.sharding import PartitionSpec as P

STEPS = 4
CHEB_LOW = 0.1
CHEB_HIGH = 1.0
CENTRE = (CHEB_HIGH + CHEB_LOW) / 2.0
HALF = (CHEB_HIGH - CHEB_LOW) / 2.0
SIGMA = CENTRE / HALF

ITEMS = 32
PLANE = 11
UPS, DOWNS = 18, 14
AHEAD = 3
EDGES = 8 * 48
VMEM = pl.BlockSpec(memory_space=pltpu.VMEM)
HBM = pl.BlockSpec(memory_space=pltpu.HBM)
LIMIT = pltpu.CompilerParams(vmem_limit_bytes=40 * 1024 * 1024)


def lanes_of():
    return lax.broadcasted_iota(jnp.int32, (8, 128), 1)


def rows_of():
    return lax.broadcasted_iota(jnp.int32, (8, 128), 0)


def lroll(v, s):
    s = s % 128
    return v if s == 0 else pltpu.roll(v, s, 1)


def sroll(v, s):
    s = s % 8
    return v if s == 0 else pltpu.roll(v, s, 0)


def halo_slots():
    lane = lanes_of()
    left = jnp.where(jnp.logical_and(lane >= 61, lane < 121), lax.div(lane - 61, 3), -1)
    return jnp.where(lane < 60, lax.div(lane, 3), left)


def packed_size(n):
    return (n + 1) // 2 + (n + 19) // 20


def pack(vs):
    lane = lanes_of()
    slots = halo_slots()
    out = []
    for i in range(0, len(vs), 2):
        other = lroll(vs[i + 1], 64) if i + 1 < len(vs) else jnp.zeros_like(vs[i])
        out.append(jnp.where(lane < 64, vs[i], other))
    for base in range(0, len(vs), 20):
        held = jnp.zeros((8, 128), jnp.float32)
        for j, v in enumerate(vs[base : base + 20]):
            held = jnp.where(slots == j, lroll(v, 3 * j - 64), held)
        out.append(held)
    return out


def unpack(load, n):
    lane = lanes_of()
    edge = jnp.logical_or(jnp.logical_and(lane >= 64, lane < 67), lane >= 125)
    mains = (n + 1) // 2
    out = []
    for i in range(n):
        main = load(i // 2)
        if i % 2:
            main = lroll(main, 64)
        held = lroll(load(mains + i // 20), 64 - 3 * (i % 20))
        out.append(jnp.where(lane < 64, main, jnp.where(edge, held, 0.0)))
    return out


def right_slots():
    return lax.div(lanes_of(), 4)


def left_slots():
    lane = lanes_of()
    return lax.div(jnp.where(lane < 67, lane + 61, lane - 67), 4)


def pack_sides(vs):
    rights, lefts = right_slots(), left_slots()
    right = jnp.zeros((8, 128), jnp.float32)
    left = jnp.zeros((8, 128), jnp.float32)
    for j, v in enumerate(vs):
        moved = lroll(v, 4 * j - 61)
        right = jnp.where(rights == j, moved, right)
        left = jnp.where(lefts == j, moved, left)
    return right, left


def sides(from_left, from_right, j):
    lane = lanes_of()
    both = lroll(jnp.where(right_slots() == j, from_left, from_right), -(4 * j + 3))
    ends = jnp.logical_or(jnp.logical_or(lane >= 125, lane == 0), jnp.logical_and(lane >= 64, lane < 67))
    return jnp.where(ends, both, 0.0)


def plane_size(n):
    return n // 2 + 1


def pack_plane(vs, right):
    lane = lanes_of()
    out = [jnp.where(lane < 64, vs[i], lroll(vs[i + 1], 64)) for i in range(0, len(vs) - 1, 2)]
    return out + [jnp.where(lane < 64, vs[-1], lroll(right, 64))]


def unpack_plane(load, n, from_left, from_right):
    lane = lanes_of()
    beyond = jnp.logical_and(jnp.logical_and(lane >= 67, lane < 64 + 4 * n), lax.rem(lane, 4) == 3)
    from_right = from_right + jnp.where(beyond, load(n // 2), 0.0)
    out = []
    for i in range(n):
        main = load(i // 2)
        if i % 2:
            main = lroll(main, 64)
        out.append(jnp.where(lane < 64, main, 0.0) + sides(from_left, from_right, i))
    return out


def coarsen_kernel(blocks_in, classes_in, residual_in, w, wl, right, left, plane, plane_right, plane_left, blocks, classes, residual, scale, sems):
    def fetch(i):
        source = blocks_in.at[:, :, :, i // 3, i % 3]
        return pltpu.make_async_copy(source, blocks.at[i], sems.at[i])

    classes_copy = pltpu.make_async_copy(classes_in, classes, sems.at[9])
    residual_copy = pltpu.make_async_copy(residual_in, residual, sems.at[10])
    classes_copy.start()
    fetch(0).start()
    residual_copy.start()
    for i in range(1, AHEAD):
        fetch(i).start()
    gx, gy, gz = (lax.axis_index(a) for a in ("gx", "gy", "gz"))
    lane, row = lanes_of(), rows_of()
    even = row % 2 == 0
    not_last_x = (gx < lax.axis_size("gx") - 1).astype(jnp.float32)
    last_x = gx == lax.axis_size("gx") - 1
    not_last_y = (gy < lax.axis_size("gy") - 1).astype(jnp.float32)
    keep_y = jnp.logical_or(row < 6, gy < lax.axis_size("gy") - 1)
    inner = lane < 64
    upper_x = jnp.logical_and(inner, jnp.logical_or(lane < 63, jnp.logical_not(last_x)))
    after_x = jnp.logical_and(lane > 0, jnp.logical_or(inner, jnp.logical_and(lane == 64, jnp.logical_not(last_x))))
    apart = jnp.where(inner, 2 * lane, 2 * lane - 127)
    not_last_z = (gz < lax.axis_size("gz") - 1).astype(jnp.float32)
    pick = jnp.where(lane < 64, 2 * lane, 127) % 128

    def squeeze(v):
        g = jnp.take_along_axis(v, pick, axis=1, mode="promise_in_bounds")
        return jnp.where(lane <= 64, g, 0.0)

    def coarsen(step):
        ydone = {}
        for ox in range(3):
            slots = {}
            for oy in range(3):
                kind = (2 if oy == 0 else 0) + (1 if ox == 0 else 0)
                s = [[None] * 4 for _ in range(3)]
                for oz in range(3):
                    for z in range(4):
                        factor = scale[kind, 5 + z if oz == 1 else 4 if (z == 0 and oz == 0) else z]
                        s[oz][z] = blocks[step, oz, oy, ox, z] * factor
                a1, b1 = s[0][1] + s[1][1], s[2][1] + s[1][1]
                a3, b3 = s[0][3] + s[1][3], s[2][3] + s[1][3]
                slots[0, 0, oy] = s[0][0]
                slots[1, 0, oy] = s[0][0] + s[2][0] + s[1][0] + a1
                slots[2, 0, oy] = s[2][0] + b1
                slots[0, 1, oy] = s[0][2] + a1
                slots[1, 1, oy] = s[0][2] + s[2][2] + s[1][2] + b1 + a3
                slots[2, 1, oy] = (s[2][2] + b3) * not_last_z
                slots[3, 0, oy] = a3
                slots[3, 1, oy] = b3
            beyond = [None, None]
            for slot in range(4):
                ev, od = [], []
                for oy in range(3):
                    z0, z1 = slots[slot, 0, oy], slots[slot, 1, oy]
                    ev.append(jnp.where(even, z0, sroll(z1, 1)))
                    od.append(jnp.where(even, sroll(z0, -1), z1))
                half = 0.5 * od[1]
                a, b = od[0] + half, od[2] + half
                a_before, b_before = sroll(a, 2), sroll(b, 2)
                ydone[slot * 3, ox] = ev[0] + jnp.where(row < 2, 0.0, a_before)
                ydone[slot * 3 + 1, ox] = ev[0] + ev[2] + (ev[1] + ev[1]) + a + jnp.where(row < 2, 0.0, b_before)
                ydone[slot * 3 + 2, ox] = jnp.where(keep_y, ev[2] + b, 0.0)
                if slot % 2 == 0:
                    beyond[slot // 2] = jnp.where(row < 2, a_before, sroll(b, 4))
                else:
                    ends = jnp.where(row < 6, sroll(a, 6), b)
                    beyond[slot // 2] = jnp.where(row < 4, beyond[slot // 2], ends) * not_last_y
            ydone[12, ox], ydone[13, ox] = beyond
        kept, sent, rows = [None] * ITEMS, [None] * PLANE, {}
        for i in range(14):
            v = [jnp.take_along_axis(ydone[i, ox], apart, axis=1, mode="promise_in_bounds") for ox in range(3)]
            half = 0.5 * v[1]
            a, b = v[0] + half, v[2] + half
            lower = jnp.where(inner, v[0], 0.0) + jnp.where(after_x, lroll(a, 65), 0.0)
            middle = jnp.where(inner, v[0] + v[2] + (v[1] + v[1]) + lroll(a, 64), 0.0) + jnp.where(after_x, lroll(b, 65), 0.0)
            upper = jnp.where(upper_x, v[2] + lroll(b, 64), 0.0)
            for cx, v in enumerate((lower, middle, upper)):
                if i < 9:
                    kept[i * 3 + cx] = v
                elif i < 12:
                    sent[(i - 9) * 3 + cx] = v
                elif i == 12:
                    kept[27 + cx] = v
                else:
                    rows[cx] = v
        kept[30] = jnp.where(row < 4, rows[0], sroll(rows[1], 4))
        sent[9] = jnp.where(row < 4, sroll(rows[0], 4), rows[1])
        kept[31] = sent[10] = rows[2]
        for i, v in enumerate(kept):
            w[step, i] = v
        right[step], left[step] = pack_sides(kept)
        sent_right, plane_left[step] = pack_sides(sent)
        plane_right[step] = sent_right
        for i, v in enumerate(pack_plane(sent, sent_right)):
            plane[step * plane_size(PLANE) + i] = v

    def scales():
        low_x = jnp.where(jnp.logical_and(lane == 0, gx == 0), 0.0, 1.0)
        low_y = jnp.where(jnp.logical_and(row == 0, gy == 0), 0.0, 1.0)
        low_z = (gz > 0).astype(jnp.float32)
        for z in range(4):
            k = classes[z].astype(jnp.float32)
            s = 0.125 * (0.05 + 0.95 * (k * k * k) / 27.0)
            for cy in range(2):
                for cx in range(2):
                    v = s
                    if cy:
                        v = v * low_y
                    if cx:
                        v = v * low_x
                    scale[cy * 2 + cx, z] = v
                    scale[cy * 2 + cx, 5 + z] = (0.5 if z % 2 else 2.0) * v
                    if z == 0:
                        scale[cy * 2 + cx, 4] = v * low_z

    def loads():
        items = []
        for c in range(3):
            f = [residual[c, z] for z in range(4)]
            planes = [f[0] + 0.5 * f[1], 0.5 * f[1] + f[2] + 0.5 * f[3], 0.5 * f[3]]
            full, beyond = [], []
            for v in planes:
                h = 0.5 * v
                before = sroll(h, 1)
                full.append(v + sroll(h, -1) + jnp.where(row == 0, 0.0, before))
                beyond.append(h * not_last_y)
            main = jnp.where(even, full[0], sroll(full[1], 1))
            ghost = jnp.where(even, full[2], 0.0)
            for z in range(3):
                ghost = jnp.where(row == 1 + 2 * z, sroll(beyond[z], 2 + 2 * z), ghost)
            items.append((main, ghost))
        vs = []
        for v in [m for m, _ in items] + [g for _, g in items]:
            h = 0.5 * v
            v = v + lroll(h, -1) + jnp.where(lane == 0, 0.0, lroll(h, 1))
            v = jnp.where(lane == 127, h * not_last_x, v)
            vs.append(squeeze(v))
        for i, v in enumerate(vs):
            wl[i] = v

        right[9], left[9] = pack_sides(vs)
        sent_right, plane_left[9] = pack_sides(vs[3:])
        plane_right[9] = sent_right
        for i, v in enumerate(pack_plane(vs[3:], sent_right)):
            plane[9 * plane_size(PLANE) + i] = v

    classes_copy.wait()
    scales()
    residual_copy.wait()
    loads()

    def body(step, carry):
        fetch(step).wait()

        @pl.when(step + AHEAD < 9)
        def _():
            fetch(step + AHEAD).start()

        coarsen(step)
        return carry

    lax.fori_loop(0, 9, body, 0, unroll=9)


def planes_kernel(plane_right, from_right, plane_left, from_left, plane, w, wl, w_out, wl_out, up, down, total):
    row = rows_of()
    even = row % 2 == 0
    total[...] = jnp.zeros_like(total)

    def body(rc, carry):
        got = unpack_plane(lambda i: plane[rc * plane_size(PLANE) + i], PLANE, plane_left[rc], plane_right[rc])
        from_l, from_r = from_left[rc], from_right[rc]
        f = [None] * ITEMS
        for k in range(ITEMS):
            v = w[rc, k] + sides(from_l, from_r, k)
            if k < 9:
                v = v + jnp.where(even, got[k], 0.0)
            elif k < 18:
                v = v + jnp.where(even, sroll(got[k - 9], -1), 0.0)
            elif 27 <= k < 30:
                end = (sroll(got[9], 4), got[9], got[10])[k - 27]
                v = v + jnp.where(even, jnp.where(row < 4, sroll(end, 4), sroll(end, -1)), 0.0)
            f[k] = v
            w_out[rc, k] = v
        magnitude = jnp.abs(f[0])
        for k in range(1, 27):
            magnitude = magnitude + jnp.abs(f[k])
        total[rc // 3] += magnitude
        ups, downs = [], []
        for k in range(0, 27, 2):
            two = f[k + 1] if k + 1 < 27 else None
            ups.append(jnp.where(row < 4, sroll(f[k], 4), sroll(f[31], 4) if two is None else two))
            downs.append(jnp.where(row < 4, f[k], 0.0 if two is None else sroll(two, 4)))
        ups += f[27:31]
        for ref, vs in ((up, ups), (down, downs)):
            for i, v in enumerate(pack(vs)):
                ref[rc * packed_size(len(vs)) + i] = v
        return carry

    lax.fori_loop(0, 9, body, 0, unroll=9)
    got = unpack_plane(lambda i: plane[9 * plane_size(PLANE) + i], 3, plane_left[9], plane_right[9])
    ups, downs = [], []
    for c in range(3):
        load = wl[c] + sides(from_left[9], from_right[9], c) + jnp.where(even, got[c], 0.0)
        ghost = wl[3 + c] + jnp.where(row == 1, sroll(got[c], -4), 0.0)
        ghost = ghost + sides(from_left[9], from_right[9], 3 + c)
        wl_out[c] = load
        wl_out[3 + c] = ghost
        d = load * (1.0 / (total[c] + 1e-06)) / CENTRE
        v = jnp.where(row < 4, sroll(load, 4), 0.0)
        v = jnp.where(row == 4, sroll(ghost, 3), v)
        v = jnp.where(row == 5, sroll(ghost, 2), v)
        ups.append(jnp.where(row >= 6, sroll(d, 4), v))
        downs.append(jnp.where(row < 4, load, jnp.where(row >= 6, sroll(d, 2), 0.0)))
    for ref, vs, size in ((up, ups, packed_size(UPS)), (down, downs, packed_size(DOWNS))):
        for i, v in enumerate(pack(vs)):
            ref[9 * size + i] = v


def piece_rows(n):
    return n + 8 * ((n + 15) // 16)


def split_planes(one, two):
    n = one.shape[0]
    even = lax.broadcasted_iota(jnp.int32, one.shape, 0) % 2 == 0
    first = jnp.where(even, one, pltpu.roll(two, 1, 0))
    second = jnp.where(even, pltpu.roll(one, n - 1, 0), two)
    return first, second


def join_planes(below, above):
    n = below.shape[0]
    even = lax.broadcasted_iota(jnp.int32, below.shape, 0) % 2 == 0
    one = jnp.where(even, below, pltpu.roll(above, 1, 0))
    two = jnp.where(even, pltpu.roll(below, n - 1, 0), above)
    return one, two


def share(at, planes, to_other, to_pair):
    low_of_pair = lax.axis_index("gz") % 2 == 0
    first, second = planes
    n = first.shape[0]
    to_pair[at : at + n] = jnp.where(low_of_pair, second, first)
    to_other[at : at + n] = jnp.where(low_of_pair, first, second)


def shared(at, n, from_other, from_pair):
    low_of_pair = lax.axis_index("gz") % 2 == 0
    other, pair = from_other[at : at + n], from_pair[at : at + n]
    return jnp.where(low_of_pair, other, pair), jnp.where(low_of_pair, pair, other)


def share_vector(load, n, at, to_other, to_pair):
    share(at, split_planes(load(0), load(1)), to_other, to_pair)
    third = load(2)
    at += n
    for i in range(0, n, 16):
        one = third[i : i + 8]
        two = third[i + 8 : i + 16] if i + 8 < n else jnp.zeros_like(one)
        share(at, split_planes(one, two), to_other, to_pair)
        at += 8


def shared_vector(n, at, from_other, from_pair):
    one, two = join_planes(*shared(at, n, from_other, from_pair))
    at += n
    parts = []
    for i in range(0, n, 16):
        parts += join_planes(*shared(at, 8, from_other, from_pair))
        at += 8
    return one, two, jnp.concatenate(parts[: n // 8], axis=0)


def rows_kernel(from_high, from_low, w, wl, whole, q, d, inverse, to_other, to_pair, total, turned, near):
    row = rows_of()
    ghosts = jnp.logical_or(row == 4, row == 5)
    total[...] = jnp.zeros_like(total)

    def body(rc, carry):
        ups = unpack(lambda i: from_low[rc * packed_size(UPS) + i], UPS)
        downs = unpack(lambda i: from_high[rc * packed_size(DOWNS) + i], DOWNS)
        got_ends = [ups[17], sroll(ups[17], 4), sroll(ups[13], 4)]
        own_ends = [w[rc, 30], sroll(w[rc, 30], 4), w[rc, 31]]
        top_sum = jnp.zeros((8, 128), jnp.float32)
        bottom_sum = jnp.zeros((8, 128), jnp.float32)
        for cz in range(3):
            for cy in range(3):
                for cx in range(3):
                    k = cz * 9 + cy * 3 + cx
                    f = sroll(w[rc, k], 4)
                    above, below = ups[k // 2], downs[k // 2]
                    top = jnp.where(row < 4, sroll(above, 4) if k % 2 else above, f)
                    bottom = jnp.where(row < 4, f, below if k % 2 else sroll(below, 4))
                    if cy < 2:
                        at = (cz % 2) * 4 + cy * 2
                        got = ups[14 + cx] if cz < 2 else got_ends[cx]
                        own = w[rc, 27 + cx] if cz < 2 else own_ends[cx]
                        top = top + jnp.where(ghosts, sroll(got, 4 - at), 0.0)
                        bottom = bottom + jnp.where(ghosts, sroll(own, 4 - at), 0.0)
                    whole[rc, k, 0:8] = top
                    whole[rc, k, 8:16] = bottom
                    top_sum = top_sum + jnp.abs(top)
                    bottom_sum = bottom_sum + jnp.abs(bottom)
        total[rc // 3, 0:8] += top_sum
        total[rc // 3, 8:16] += bottom_sum
        return carry

    lax.fori_loop(0, 9, body, 0, unroll=9)
    ups = unpack(lambda i: from_low[9 * packed_size(UPS) + i], 3)
    downs = unpack(lambda i: from_high[9 * packed_size(DOWNS) + i], 3)
    for c in range(3):
        load, ghost = sroll(wl[c], 4), wl[3 + c]
        q[c, 0:8] = jnp.where(row < 4, ups[c], load + jnp.where(ghosts, ups[c], 0.0))
        below = sroll(downs[c], 4)
        below = below + jnp.where(row == 4, sroll(ghost, 3), jnp.where(row == 5, sroll(ghost, 2), 0.0))
        q[c, 8:16] = jnp.where(row < 4, load, below)
        part = 1.0 / (total[c] + 1e-06)
        inverse[c] = part
        d[c, 16:24] = jnp.zeros((8, 128), jnp.float32)
        d[c, 2:18] = part * q[c] / CENTRE
        turned[...] = ups[c]
        d[c, 0:2] = turned[6:8]
        turned[...] = downs[c]
        d[c, 18:20] = turned[6:8]
    for c in range(3):
        fill_near(near, c, d[c], None)
    for r, product in enumerate(apply_to(whole, near)):
        q[r] = q[r] - product
    items = [edge_of(whole, i // 9, i % 9) for i in range(81)] + [q[r] for r in range(3)] + [inverse[r] for r in range(3)]
    packed = pack([v[h : h + 8] for v in items for h in (0, 8)])
    for i in range(0, len(packed), 2):
        share(4 * i, split_planes(packed[i], packed[i + 1]), to_other, to_pair)
    share_vector(lambda c: d[c], 24, EDGES, to_other, to_pair)


def operator_kernel(whole, operator, written):
    written[...] = jnp.zeros_like(written)

    def body(rc, carry):
        for k in range(27):
            for z in range(2):
                v = whole[rc, k, pl.ds(4 + z, 4, stride=2), :]
                operator[k // 9, k // 3 % 3, k % 3, rc // 3, rc % 3, z] = v[:, 0:64]
        return carry

    lax.fori_loop(0, 9, body, 0, unroll=3)


def edge_of(whole, rc, at):
    even = lax.broadcasted_iota(jnp.int32, (16, 128), 0) % 2 == 0
    return jnp.where(even, whole[rc, at], whole[rc, 18 + at])


def fill_near(near, c, own, beyond):
    n = own.shape[0]
    even = lax.broadcasted_iota(jnp.int32, (n, 128), 0) % 2 == 0
    base = (24 - n) // 4
    if beyond is None:
        beyond = jnp.zeros_like(own)
    for cz, v in enumerate((
        jnp.where(even, beyond, pltpu.roll(own, 1, 0)),
        own,
        jnp.where(even, pltpu.roll(own, n - 1, 0), beyond),
    )):
        if base:
            near[cz, c, 0:8] = jnp.zeros((8, 128), jnp.float32)
            near[cz, c, 16:24] = jnp.zeros((8, 128), jnp.float32)
        near[cz, c, base : base + n] = v


def shifted(v):
    return pltpu.roll(v, 1, 1), v, pltpu.roll(v, 127, 1)


def apply_to(whole, near):
    sums = [jnp.zeros((16, 128), jnp.float32) for _ in range(3)]
    for cz in range(3):
        for cy in range(3):
            for c in range(3):
                for cx, moved in enumerate(shifted(near[cz, c, pl.ds(2 * cy, 16), :])):
                    for r in range(3):
                        sums[r] = sums[r] + whole[r * 3 + c, cz * 9 + cy * 3 + cx] * moved
    return sums


def two_steps_kernel(rhos, whole, q, d, inverse, from_other, from_pair, after, q_out, d_out, x_out, to_other, to_pair, near, packed, edges):
    even = rows_of() % 2 == 0
    for i in range(0, packed.shape[0], 2):
        packed[i], packed[i + 1] = join_planes(*shared(4 * i, 8, from_other, from_pair))
    for i, v in enumerate(unpack(lambda i: packed[i], 174)):
        edges[i // 2, 8 * (i % 2) : 8 * (i % 2) + 8] = v
    for c, v in enumerate(shared_vector(24, EDGES, from_other, from_pair)):
        near[0, c] = v
        near[1, c] = d[c]
    own = [jnp.zeros((16, 128), jnp.float32) for _ in range(3)]
    beyond = [jnp.zeros((16, 128), jnp.float32) for _ in range(3)]
    for cy in range(3):
        for c in range(3):
            outer = shifted(near[0, c, pl.ds(2 * cy, 16), :])
            inner = shifted(near[1, c, pl.ds(2 * cy, 16), :])
            for cx in range(3):
                for r in range(3):
                    rc, at = r * 3 + c, cy * 3 + cx
                    own[r] = own[r] + edge_of(whole, rc, at) * outer[cx]
                    beyond[r] = beyond[r] + edges[rc * 9 + at] * inner[cx]
    (same, slope), (same_next, slope_next) = rhos
    q_now, d_now, d_beyond = [], [], []
    for r in range(3):
        q_now.append(q[r] - own[r])
        d_now.append(same * d[r, 2:18] + slope * (inverse[r] * q_now[r]))
        d_beyond.append(same * near[0, r, 2:18] + slope * (edges[84 + r] * (edges[81 + r] - beyond[r])))
        x_out[r] = d[r, 2:18] + d_now[r]
    for r in range(3):
        fill_near(near, r, d_now[r], d_beyond[r])
    for r, product in enumerate(apply_to(whole, near)):
        q_next = q_now[r] - product
        q_out[r] = q_next
        d_out[r] = same_next * d_now[r] + slope_next * (inverse[r] * q_next)
    share_vector(lambda c: d_out[c], 16, 0, to_other, to_pair)


def last_step_kernel(rho, whole, q, d, inverse, x, from_other, from_pair, solution_out, near, turned):
    same, slope = rho
    for c, v in enumerate(shared_vector(16, 0, from_other, from_pair)):
        fill_near(near, c, d[c], v)
    for r, product in enumerate(apply_to(whole, near)):
        d_new = same * d[r] + slope * (inverse[r] * (q[r] - product))
        turned[...] = x[r] + d[r] + d_new
        for z in range(2):
            solution_out[r, z] = turned[pl.ds(4 + z, 4, stride=2), :][:, 0:64]


def shape(*dims):
    return jax.ShapeDtypeStruct(dims, jnp.float32)


def along(block, axes, distances):
    sizes = [lax.axis_size(a) for a in axes]
    route = []
    for source in itertools.product(*[range(n) for n in sizes]):
        target = [i + s for i, s in zip(source, distances)]
        if all(0 <= i < n for i, n in zip(target, sizes)):
            flat = [functools.reduce(lambda t, p: t * p[1] + p[0], zip(at, sizes), 0) for at in (source, target)]
            route.append(tuple(flat))
    return lax.ppermute(block, axes, route)


def exchanged(block, axis, first):
    n = lax.axis_size(axis)
    pairs = [(i, i + 1) for i in range(first, n - 1, 2)]
    return lax.ppermute(block, axis, pairs + [(j, i) for i, j in pairs])


def shards(blocks, classes, residual):
    w_shape, wl_shape = shape(9, ITEMS, 8, 128), shape(6, 8, 128)
    side = shape(10, 8, 128)
    w, wl, right, left, plane, plane_right, plane_left_sent = pl.pallas_call(
        coarsen_kernel,
        in_specs=[HBM] * 3,
        out_specs=[VMEM] * 7,
        out_shape=[w_shape, wl_shape, side, side, shape(9 * plane_size(PLANE) + plane_size(3), 8, 128), side, side],
        scratch_shapes=[
            pltpu.VMEM((9, 3, 3, 3, 4, 8, 128), jnp.float32),
            pltpu.VMEM((4, 8, 128), jnp.int32),
            pltpu.VMEM((3, 4, 8, 128), jnp.float32),
            pltpu.VMEM((4, 9, 8, 128), jnp.float32),
            pltpu.SemaphoreType.DMA((11,)),
        ],
        compiler_params=LIMIT,
    )(*(pltpu.with_memory_space_constraint(v, pltpu.HBM) for v in (blocks, classes, residual)))
    plane_left = along(plane_right, ("gx", "gz"), (1, 1))
    from_left = along(right, ("gx",), (1,))
    plane_right = along(plane_left_sent, ("gx", "gz"), (-1, 1))
    from_right = along(left, ("gx",), (-1,))
    plane = along(plane, ("gz",), (1,))
    w, wl, up, down = pl.pallas_call(
        planes_kernel,
        in_specs=[VMEM] * 7,
        out_specs=[VMEM] * 4,
        out_shape=[w_shape, wl_shape, shape(9 * packed_size(UPS) + packed_size(3), 8, 128), shape(9 * packed_size(UPS) + packed_size(3), 8, 128)],
        scratch_shapes=[pltpu.VMEM((3, 8, 128), jnp.float32)],
        compiler_params=LIMIT,
    )(plane_right, from_right, plane_left, from_left, plane, w, wl)
    from_high = along(down, ("gy",), (-1,))
    from_low = along(up, ("gy",), (1,))
    whole_shape, vector = shape(9, 27, 16, 128), shape(3, 16, 128)
    near = pltpu.VMEM((3, 3, 24, 128), jnp.float32)
    whole, q, d, inverse, to_other, to_pair = pl.pallas_call(
        rows_kernel,
        in_specs=[VMEM] * 4,
        out_specs=[VMEM] * 6,
        out_shape=[whole_shape, vector, shape(3, 24, 128), vector] + [shape(EDGES + piece_rows(24), 128)] * 2,
        scratch_shapes=[pltpu.VMEM((3, 16, 128), jnp.float32), pltpu.VMEM((8, 128), jnp.float32), near],
        compiler_params=LIMIT,
    )(from_high, from_low, w, wl)
    operator, written = pl.pallas_call(
        operator_kernel,
        in_specs=[VMEM],
        out_specs=[VMEM] * 2,
        out_shape=[shape(3, 3, 3, 3, 3, 2, 4, 64), shape(8, 128)],
        compiler_params=LIMIT,
        cost_estimate=pl.CostEstimate(flops=500000, bytes_accessed=3000000, transcendentals=0),
    )(whole)
    rhos, rho_now = [], 1.0 / SIGMA
    for _ in range(STEPS - 1):
        rho_next = 1.0 / (2.0 * SIGMA - rho_now)
        rhos.append((rho_next * rho_now, 2.0 * rho_next / HALF))
        rho_now = rho_next
    from_other, from_pair = exchanged(to_other, "gz", 1), exchanged(to_pair, "gz", 0)
    q, d, x, to_other, to_pair = pl.pallas_call(
        functools.partial(two_steps_kernel, rhos[:2]),
        in_specs=[VMEM] * 7,
        out_specs=[VMEM] * 5,
        out_shape=[vector] * 3 + [shape(piece_rows(16), 128)] * 2,
        scratch_shapes=[near, pltpu.VMEM((96, 8, 128), jnp.float32), pltpu.VMEM((87, 16, 128), jnp.float32)],
        compiler_params=LIMIT,
    )(whole, q, d, inverse, from_other, from_pair, written)
    from_other, from_pair = exchanged(to_other, "gz", 1), exchanged(to_pair, "gz", 0)
    coarse_solution = pl.pallas_call(
        functools.partial(last_step_kernel, rhos[2]),
        in_specs=[VMEM] * 7,
        out_specs=VMEM,
        out_shape=shape(3, 2, 4, 64),
        scratch_shapes=[near, pltpu.VMEM((16, 128), jnp.float32)],
        compiler_params=LIMIT,
    )(whole, q, d, inverse, x, from_other, from_pair)
    return operator, coarse_solution


def solution(mesh):
    placed = (
        P(None, None, None, None, None, "gz", "gy", "gx"),
        P("gz", "gy", "gx"),
        P(None, "gz", "gy", "gx"),
    )
    return jax.shard_map(
        shards,
        mesh=mesh,
        in_specs=placed,
        out_specs=(P(None, None, None, None, None, "gz", "gy", "gx"), P(None, "gz", "gy", "gx")),
        check_vma=False,
    )
```
